32 devices in a mesh: groups: 2 (over y), tp: 4 (over z), seq: 4 (over x, core).
Axes of the slice: x: 2, y: 2, z: 4, core: 2. Of those that a mesh axis runs over, the one named last changes fastest.
Arguments:
- tokens_values: bfloat16 [1024, 8192], P(('groups', 'seq'), 'tp'), parts along dimension 0, may hold values from -1 to 1
- tokens_scales: float32 [1024, 64], P(('groups', 'seq'), 'tp'), parts along dimension 0, may hold values from 0.25 to 4
- gate_weight: bfloat16 [8192, 16384], P('seq', 'tp'), may hold values from -0.0625 to 0.0625
- up_weight: bfloat16 [8192, 16384], P('seq', 'tp'), may hold values from -0.0625 to 0.0625
- down_weight: bfloat16 [16384, 8192], P('tp', 'seq'), may hold values from -0.0625 to 0.0625
Outputs:
- mixed_values: bfloat16 [1024, 8192], P(('groups', 'seq'), 'tp'), parts along dimension 0
- mixed_scales: float32 [1024, 64], P(('groups', 'seq'), 'tp'), parts along dimension 0
The draws below stay inside these ranges and needn't reach their ends.
There are 2 independent parts, one for each index of `groups`. The reference program is written for one: setup_inputs(seed, part) draws one part's arguments, and reference() takes and returns one part's arrays. A program takes and returns all parts, laid end to end along the dimension named above; an argument that names none is the same for every part. Nothing has to cross between parts.
All inputs are finite; a program needn't handle non-finite values.
Results may differ from the reference program's by a relative error of at most 0.02.
Values may be sent and summed in bfloat16 or wider, within the bound.
No kernel may reach another device: no remote copies, remote signals or barrier semaphores. Data moves between devices by JAX's collectives and lax.ppermute only.
A program may use at most 512 MiB of HBM per device.

```python
import math
import jax
import jax.numpy as jnp
from jax import lax

D = 8192
FF = 16384
TOKENS = 512
N_TP = 4


def spiked(drawn, own_key, source, target, shards_of, factor):
    def block_of(axis_at):
        return (jnp.arange(drawn.shape[axis_at]) // (drawn.shape[axis_at] // shards_of)).reshape((-1,) + (1,) * (drawn.ndim - 1 - axis_at))

    near = jax.random.permutation(own_key, shards_of)[block_of(target)]
    other_side = (block_of(target) + shards_of // 2) % shards_of
    return jnp.where((block_of(source) == near) | (block_of(source) == other_side), factor * drawn, drawn)


def steps_of(own_key, extent, cuts, low, top_value):
    level = 1.0
    for dim, parts in cuts:
        heights = jax.random.uniform(jax.random.fold_in(jax.random.fold_in(own_key, 6), dim), (parts,), jnp.float32, low / len(cuts), top_value / len(cuts))
        level = level * jnp.repeat(jnp.exp(heights), extent[dim] // parts).reshape((-1,) + (1,) * (len(extent) - 1 - dim))
    return level


def gaussian(stream_key, shape, scale, reach, cuts=(), kind=jnp.bfloat16):
    values = scale * jax.random.normal(stream_key, shape, jnp.float32)
    if cuts:
        values = values * steps_of(stream_key, shape, cuts, -0.22, 0.18)
    return jnp.clip(values, -reach, reach).astype(kind)


def bell_draw_with(rng, extent, width, reach, cuts, heavy, held_as=jnp.bfloat16):
    drawn = width * jax.random.normal(rng, extent, jnp.float32)
    if cuts:
        drawn = drawn * steps_of(rng, extent, cuts, -0.22, 0.18)
    return jnp.clip(spiked(drawn, jax.random.fold_in(rng, 3), *heavy), -reach, reach).astype(held_as)


def setup_inputs(seed: int = 0, part: int = 0) -> dict:
    streams_of = jax.random.split(jax.random.key(seed), 6)
    part_splits = jax.random.split(jax.random.fold_in(streams_of[5], part), 6)
    tokens_values = jnp.clip(jax.random.uniform(part_splits[0], (TOKENS, D), jnp.float32, -1.0, 1.0) * steps_of(part_splits[0], (TOKENS, D), ((0, 4), (1, 4)), -0.4, 0.0), -1.0, 1.0).astype(jnp.bfloat16)
    tokens_scales = jnp.clip(jnp.exp(math.log(4.0) - 2.7725887 * jax.random.uniform(part_splits[1], (TOKENS, D // 128), jnp.float32) ** steps_of(part_splits[1], (TOKENS, D // 128), ((0, 4), (1, 4)), -0.2, 0.2)), 0.25, 4.0)
    gate_weight = gaussian(streams_of[2], (D, FF), D ** -0.5, 0.0625, ((0, 4), (1, 4)))
    up_weight = gaussian(streams_of[3], (D, FF), D ** -0.5, 0.0625, ((0, 4), (1, 4)))
    down_weight = bell_draw_with(streams_of[4], (FF, D), FF ** -0.5, 0.0625, ((0, 4), (1, 4)), (0, 1, 4, 2.0))
    return dict(tokens_values=tokens_values, tokens_scales=tokens_scales, gate_weight=gate_weight, up_weight=up_weight, down_weight=down_weight)


def blocks(array):
    return array.reshape(array.shape[0], array.shape[1] // 128, 128)


def block_scale(array):
    return jnp.max(jnp.abs(blocks(array)), axis=2) + 1e-6


def reference(tokens_values, tokens_scales, gate_weight, up_weight, down_weight):
    inputs = (blocks(tokens_values.astype(jnp.float32)) * tokens_scales[:, :, None]).reshape(TOKENS, D).astype(jnp.bfloat16)
    group_width = FF // N_TP
    gate_parts = gate_weight.reshape(D, N_TP, group_width).transpose(1, 0, 2)
    up_parts = up_weight.reshape(D, N_TP, group_width).transpose(1, 0, 2)
    down_parts = down_weight.reshape(N_TP, group_width, D)

    def accumulate(total, pieces):
        gate_piece, up_piece, down_piece = pieces
        gate = jnp.dot(inputs, gate_piece, preferred_element_type=jnp.float32)
        up = jnp.dot(inputs, up_piece, preferred_element_type=jnp.float32)
        hidden = (jax.nn.silu(gate) * up).astype(jnp.bfloat16)
        partial_sum = jnp.dot(hidden, down_piece, preferred_element_type=jnp.float32)
        scale = block_scale(partial_sum)
        quant = (blocks(partial_sum) / scale[:, :, None]).astype(jnp.bfloat16)
        term = (quant.astype(jnp.float32) * scale[:, :, None]).reshape(TOKENS, D)
        return total + term, None

    total, unused = lax.scan(accumulate, jnp.zeros((TOKENS, D), jnp.float32), (gate_parts, up_parts, down_parts))
    mixed_scales = block_scale(total)
    mixed_values = (blocks(total) / mixed_scales[:, :, None]).reshape(TOKENS, D).astype(jnp.bfloat16)
    return mixed_values, mixed_scales
```

```python
import jax
import jax.numpy as jnp
from jax import lax
from jax.sharding import PartitionSpec as P


def blocks(array):
    return array.reshape(array.shape[0], array.shape[1] // 128, 128)


def block_scale(array):
    return jnp.max(jnp.abs(blocks(array)), axis=2) + 1e-06


def expand(values, scales):
    return (blocks(values.astype(jnp.float32)) * scales[:, :, None]).reshape(values.shape)


def shards(tokens_values, tokens_scales, gate_weight, up_weight, down_weight):
    mine = expand(tokens_values, tokens_scales).astype(jnp.bfloat16)
    mine = lax.all_gather(mine, "tp", axis=1, tiled=True)
    inputs = lax.all_to_all(mine, "seq", split_axis=1, concat_axis=0, tiled=True)
    gate = jnp.dot(inputs, gate_weight, preferred_element_type=jnp.float32).astype(jnp.bfloat16)
    up = jnp.dot(inputs, up_weight, preferred_element_type=jnp.float32).astype(jnp.bfloat16)
    gate = lax.psum_scatter(gate, "seq", scatter_dimension=0, tiled=True).astype(jnp.float32)
    up = lax.psum_scatter(up, "seq", scatter_dimension=0, tiled=True).astype(jnp.float32)
    hidden = (jax.nn.silu(gate) * up).astype(jnp.bfloat16)
    hidden = lax.all_gather(hidden, "seq", axis=0, tiled=True)
    partial_sum = jnp.dot(hidden, down_weight, preferred_element_type=jnp.float32).astype(jnp.bfloat16)
    partial_sum = lax.all_to_all(partial_sum, "seq", split_axis=0, concat_axis=1, tiled=True)
    total = lax.psum_scatter(partial_sum, "tp", scatter_dimension=1, tiled=True).astype(jnp.float32)
    mixed_scales = block_scale(total)
    mixed_values = (
        (blocks(total) / mixed_scales[:, :, None]).reshape(total.shape).astype(jnp.bfloat16)
    )
    return (mixed_values, mixed_scales)


def solution(mesh):
    placed = (
        P(("groups", "seq"), "tp"),
        P(("groups", "seq"), "tp"),
        P("seq", "tp"),
        P("seq", "tp"),
        P("tp", "seq"),
    )
    return jax.shard_map(
        shards,
        mesh=mesh,
        in_specs=placed,
        out_specs=(P(("groups", "seq"), "tp"), P(("groups", "seq"), "tp")),
        check_vma=False,
    )
```

```python
import jax
import jax.numpy as jnp
from jax import lax
from jax.sharding import PartitionSpec as P

CHUNKS = 2


def blocks(array):
    return array.reshape(array.shape[0], array.shape[1] // 128, 128)


def block_scale(array):
    return jnp.max(jnp.abs(blocks(array)), axis=2) + 1e-06


def expand(values, scales):
    return (blocks(values.astype(jnp.float32)) * scales[:, :, None]).reshape(values.shape)


def scaled(total):
    scales = block_scale(total)
    values = (blocks(total) / scales[:, :, None]).reshape(total.shape).astype(jnp.bfloat16)
    return values, scales


def wide(array):
    return array.astype(jnp.float32)


def narrow(array):
    return array.astype(jnp.bfloat16)


def dot(a, b):
    return jnp.dot(a, b, preferred_element_type=jnp.float32)


def any_shards(tokens_values, tokens_scales, gate_weight, up_weight, down_weight):
    mine = narrow(expand(tokens_values, tokens_scales))
    mine = lax.all_gather(mine, "tp", axis=1, tiled=True)
    inputs = lax.all_to_all(mine, "seq", split_axis=1, concat_axis=0, tiled=True)
    gate = narrow(dot(inputs, gate_weight))
    up = narrow(dot(inputs, up_weight))
    gate = wide(lax.psum_scatter(gate, "seq", scatter_dimension=0, tiled=True))
    up = wide(lax.psum_scatter(up, "seq", scatter_dimension=0, tiled=True))
    hidden = narrow(jax.nn.silu(gate) * up)
    hidden = lax.all_gather(hidden, "seq", axis=0, tiled=True)
    partial_sum = narrow(dot(hidden, down_weight))
    partial_sum = lax.all_to_all(partial_sum, "seq", split_axis=0, concat_axis=1, tiled=True)
    return scaled(wide(lax.psum_scatter(partial_sum, "tp", scatter_dimension=1, tiled=True)))


def over_seq(array, bit):
    return lax.ppermute(array, "seq", [(i, i ^ bit) for i in range(4)])


def over_tp(array, bit):
    return lax.ppermute(array, "tp", [(i, i ^ bit) for i in range(4)])


def device(tp, seq):
    return tp * 4 + seq


FIRST_IN, SECOND, FIRST_OUT = [], [], []
for tp in range(4):
    for seq in range(4):
        if (tp ^ seq) & 1:
            FIRST_IN.append((device(tp, seq), device(tp, seq ^ 1)))
            SECOND.append((device(tp, seq), device(tp ^ 1, seq ^ 1)))
            FIRST_OUT.append((device(tp, seq), device(tp ^ 1, seq)))
        else:
            FIRST_IN.append((device(tp, seq), device(tp ^ 1, seq)))
            FIRST_OUT.append((device(tp, seq), device(tp, seq ^ 1)))


def over_both(array, pairs):
    return lax.ppermute(array, ("tp", "seq"), pairs)


def arrange(low_first, one, other):
    return jnp.concatenate([jnp.where(low_first, one, other), jnp.where(low_first, other, one)], axis=0)


def gather_inputs(mine, place):
    tp, seq = place
    x, c, even = seq >> 1, seq & 1, (tp ^ seq) & 1 == 0
    high = tp >> 1
    far = over_tp(mine, 2)
    sent = jnp.where(high == x, far, mine)
    kept = jnp.where(high == x, mine, far)
    got = over_seq(sent, 2)
    pair = arrange(x == 0, kept, got)
    first = over_both(pair, FIRST_IN)
    second = over_both(pair, SECOND)
    own = jnp.where(even, pair, first)
    others = jnp.where(even, first, second)
    return arrange(c == 0, own, others)


def scatter_outputs(partial_sum, place):
    tp, seq = place
    x, c, even = seq >> 1, seq & 1, (tp ^ seq) & 1 == 0
    high = tp >> 1
    half = partial_sum.shape[0] // 2
    rows = half // 2
    low, top = partial_sum[:half], partial_sum[half:]
    own = jnp.where(c == 0, low, top)
    others = jnp.where(c == 0, top, low)
    first = over_both(narrow(jnp.where(even, others, own)), FIRST_OUT)
    second = over_both(narrow(others), SECOND)
    pair = wide(first) + jnp.where(even, own, wide(second))
    low, top = pair[:rows], pair[rows:]
    kept = jnp.where(x == 0, low, top)
    got = over_seq(narrow(jnp.where(x == 0, top, low)), 2)
    sent = jnp.where(high == x, got, narrow(kept))
    held = jnp.where(high == x, kept, wide(got))
    return held + wide(over_tp(sent, 2))


def four_shards(tokens_values, tokens_scales, gate_weight, up_weight, down_weight):
    tp, seq = lax.axis_index("tp"), lax.axis_index("seq")
    place = tp, seq
    width = gate_weight.shape[1] // 4
    rows = tokens_values.shape[0] // CHUNKS

    def columns(weight, bits):
        return lax.dynamic_slice_in_dim(weight, (seq ^ bits) * width, width, axis=1)

    def depth(weight, bits):
        return lax.dynamic_slice_in_dim(weight, (seq ^ bits) * width, width, axis=0)

    mine = narrow(expand(tokens_values, tokens_scales))
    inputs = [gather_inputs(mine[i * rows : (i + 1) * rows], place) for i in range(CHUNKS)]

    def reduced(some, weight):
        a = over_seq(narrow(dot(some, columns(weight, 3))), 1)
        b = over_seq(narrow(dot(some, columns(weight, 2)) + wide(a)), 2)
        c = over_seq(narrow(dot(some, columns(weight, 1))), 1)
        return dot(some, columns(weight, 0)) + wide(c) + wide(b)

    outs = []
    for some in inputs:
        gate = reduced(some, gate_weight)
        up = reduced(some, up_weight)
        hidden = narrow(jax.nn.silu(gate) * up)
        far = over_seq(hidden, 2)
        near = over_seq(hidden, 1)
        last = over_seq(far, 1)
        partial_sum = dot(hidden, depth(down_weight, 0)) + dot(near, depth(down_weight, 1))
        partial_sum += dot(far, depth(down_weight, 2))
        partial_sum += dot(last, depth(down_weight, 3))
        outs.append(scaled(scatter_outputs(partial_sum, place)))
    return tuple(jnp.concatenate(parts, axis=0) for parts in zip(*outs))


def solution(mesh):
    placed = (
        P(("groups", "seq"), "tp"),
        P(("groups", "seq"), "tp"),
        P("seq", "tp"),
        P("seq", "tp"),
        P("tp", "seq"),
    )
    fours = mesh.shape["tp"] == 4 and mesh.shape["seq"] == 4
    return jax.shard_map(
        four_shards if fours else any_shards,
        mesh=mesh,
        in_specs=placed,
        out_specs=(P(("groups", "seq"), "tp"), P(("groups", "seq"), "tp")),
        check_vma=False,
    )
```

```python
import functools

import jax
import jax.numpy as jnp
from jax import lax
from jax.experimental import pallas as pl
from jax.experimental.pallas import tpu as pltpu
from jax.sharding import PartitionSpec as P

ROWS = (32, 64, 32)
ORDER = (
    "far0", "sel0", "far1", "arr0", "sel1", "far2", "take0", "a0", "c0", "arr1", "b0", "sel2", "d0", "take1",
    "a1", "c1", "arr2", "hide0", "b1", "d1", "take2", "a2", "own0", "c2", "forward0", "b2", "rest0", "out0",
    "d2", "mix0", "hide1", "far_out0", "own1", "hide2", "end0", "forward1", "own2", "rest1", "out1",
    "forward2", "rest2", "out2", "mix1", "mix2", "far_out1", "far_out2", "end1", "end2",
)
TILE = 256
COST = 1 << 33


def blocks(array):
    return array.reshape(array.shape[0], array.shape[1] // 128, 128)


def block_scale(array):
    return jnp.max(jnp.abs(blocks(array)), axis=2) + 1e-06


def expand(values, scales):
    return (blocks(values.astype(jnp.float32)) * scales[:, :, None]).reshape(values.shape)


def scaled(total):
    scales = block_scale(total)
    values = (blocks(total) / scales[:, :, None]).reshape(total.shape).astype(jnp.bfloat16)
    return values, scales


def wide(array):
    return array.astype(jnp.float32)


def narrow(array):
    return array.astype(jnp.bfloat16)


def dot(a, b):
    return jnp.dot(a, b, preferred_element_type=jnp.float32)


def any_shards(tokens_values, tokens_scales, gate_weight, up_weight, down_weight):
    mine = narrow(expand(tokens_values, tokens_scales))
    mine = lax.all_gather(mine, "tp", axis=1, tiled=True)
    inputs = lax.all_to_all(mine, "seq", split_axis=1, concat_axis=0, tiled=True)
    gate = narrow(dot(inputs, gate_weight))
    up = narrow(dot(inputs, up_weight))
    gate = wide(lax.psum_scatter(gate, "seq", scatter_dimension=0, tiled=True))
    up = wide(lax.psum_scatter(up, "seq", scatter_dimension=0, tiled=True))
    hidden = narrow(jax.nn.silu(gate) * up)
    hidden = lax.all_gather(hidden, "seq", axis=0, tiled=True)
    partial_sum = narrow(dot(hidden, down_weight))
    partial_sum = lax.all_to_all(partial_sum, "seq", split_axis=0, concat_axis=1, tiled=True)
    return scaled(wide(lax.psum_scatter(partial_sum, "tp", scatter_dimension=1, tiled=True)))


def over_seq(array, bit):
    return lax.ppermute(array, "seq", [(i, i ^ bit) for i in range(4)])


def over_tp(array, bit):
    return lax.ppermute(array, "tp", [(i, i ^ bit) for i in range(4)])


def device(tp, seq):
    return tp * 4 + seq


FIRST_IN, SECOND, FIRST_OUT = [], [], []
for tp in range(4):
    for seq in range(4):
        if (tp ^ seq) & 1:
            FIRST_IN.append((device(tp, seq), device(tp, seq ^ 1)))
            SECOND.append((device(tp, seq), device(tp ^ 1, seq ^ 1)))
            FIRST_OUT.append((device(tp, seq), device(tp ^ 1, seq)))
        else:
            FIRST_IN.append((device(tp, seq), device(tp ^ 1, seq)))
            FIRST_OUT.append((device(tp, seq), device(tp, seq ^ 1)))


def over_both(array, pairs):
    return lax.ppermute(array, ("tp", "seq"), pairs)


def arrange(low_first, one, other):
    return jnp.concatenate([jnp.where(low_first, one, other), jnp.where(low_first, other, one)], axis=0)


def sums_kernel(has_got, quarters, some, gate_weight, up_weight, *rest):
    out = rest[-1]
    for k, weight in enumerate((gate_weight, up_weight)):
        value = dot(some[...], weight[...])
        if has_got:
            value += wide(rest[0][0, k])
        out[0, k] = value.astype(out.dtype)


def sums(some, gate_weight, up_weight, quarters, got=None, kind=jnp.bfloat16):
    rows, deep = some.shape
    width = gate_weight.shape[1] // 4
    count, tiles = len(quarters), width // TILE
    pair = pl.BlockSpec((1, 2, rows, TILE), lambda i, j, q: (i, 0, 0, j))
    weight = pl.BlockSpec((deep, TILE), lambda i, j, q: (0, q[i] * tiles + j))
    return pl.pallas_call(
        functools.partial(sums_kernel, got is not None),
        out_shape=jax.ShapeDtypeStruct((count, 2, rows, width), kind),
        grid_spec=pltpu.PrefetchScalarGridSpec(
            num_scalar_prefetch=1,
            grid=(count, tiles),
            in_specs=[pl.BlockSpec((rows, deep), lambda i, j, q: (0, 0)), weight, weight]
            + [pair] * (got is not None),
            out_specs=pair,
        ),
        compiler_params=pltpu.CompilerParams(vmem_limit_bytes=24 << 20),
        cost_estimate=pl.CostEstimate(flops=COST, bytes_accessed=1, transcendentals=0),
    )(jnp.stack(quarters).astype(jnp.int32), some, gate_weight, up_weight, *([] if got is None else [got]))


def products_kernel(quarters, one, two, first_weight, second_weight, *rest):
    value = dot(one[...], first_weight[...]) + dot(two[...], second_weight[...])
    if len(rest) > 1:
        value += rest[0][...]
    rest[-1][...] = value


def products(pieces, weight, quarters, total=None):
    rows, deep = pieces[0].shape
    wide_tile = 2 * TILE
    piece = pl.BlockSpec((rows, deep), lambda j, q: (0, 0))
    out = pl.BlockSpec((rows, wide_tile), lambda j, q: (0, j))
    return pl.pallas_call(
        products_kernel,
        out_shape=jax.ShapeDtypeStruct((rows, weight.shape[1]), jnp.float32),
        grid_spec=pltpu.PrefetchScalarGridSpec(
            num_scalar_prefetch=1,
            grid=(weight.shape[1] // wide_tile,),
            in_specs=[
                piece,
                piece,
                pl.BlockSpec((deep, wide_tile), lambda j, q: (q[0], j)),
                pl.BlockSpec((deep, wide_tile), lambda j, q: (q[1], j)),
            ]
            + [out] * (total is not None),
            out_specs=out,
        ),
        compiler_params=pltpu.CompilerParams(vmem_limit_bytes=24 << 20),
        cost_estimate=pl.CostEstimate(flops=COST, bytes_accessed=1, transcendentals=0),
    )(jnp.stack(quarters).astype(jnp.int32), *pieces, weight, weight, *([] if total is None else [total]))


class Steps:

    def __init__(self, tokens_values, tokens_scales, gate_weight, up_weight, down_weight):
        tp, seq = lax.axis_index("tp"), lax.axis_index("seq")
        self.seq, self.x, self.core = seq, seq >> 1, seq & 1
        self.high, self.even = tp >> 1, (tp ^ seq) & 1 == 0
        self.gate_weight = pltpu.with_memory_space_constraint(gate_weight, pltpu.HBM)
        self.up_weight = pltpu.with_memory_space_constraint(up_weight, pltpu.HBM)
        self.down_weight = pltpu.with_memory_space_constraint(down_weight, pltpu.HBM)
        self.mine = narrow(expand(tokens_values, tokens_scales))
        unit = tokens_values.shape[0] // sum(ROWS)
        self.starts = [sum(ROWS[:i]) * unit for i in range(len(ROWS) + 1)]
        self.last = self.mine
        self.held = {}

    def run(self, order):
        for step in order:
            with jax.named_scope(step):
                getattr(self, step[:-1])(int(step[-1]))
        return tuple(
            jnp.concatenate([self.held["end", i][k] for i in range(len(ROWS))], axis=0) for k in range(2)
        )

    def now(self, array):
        return lax.optimization_barrier((array, self.last))[0]

    def far(self, i):
        part = self.now(self.mine[self.starts[i] : self.starts[i + 1]])
        self.held["far", i] = part, over_tp(part, 2)

    def sel(self, i):
        part, other = self.held["far", i]
        other = self.now(other)
        sent = jnp.where(self.high == self.x, other, part)
        kept = jnp.where(self.high == self.x, part, other)
        self.held["sel", i] = kept, over_seq(sent, 2)
        self.last = sent

    def arr(self, i):
        kept, got = self.held["sel", i]
        pair = arrange(self.x == 0, kept, self.now(got))
        self.held["arr", i] = pair, over_both(pair, FIRST_IN), over_both(pair, SECOND)
        self.last = pair

    def take(self, i):
        pair, first, second = self.held["arr", i]
        first = self.now(first)
        own = jnp.where(self.even, pair, first)
        others = jnp.where(self.even, first, second)
        self.held["take", i] = self.last = arrange(self.core == 0, own, others)

    def part(self, i, bits, got=None, kind=jnp.bfloat16):
        some = self.now(self.held["take", i])
        quarters = [self.seq ^ bit for bit in bits]
        self.last = sums(some, self.gate_weight, self.up_weight, quarters, got, kind)
        return self.last

    def a(self, i):
        self.held["a", i] = over_seq(self.part(i, (3,)), 1)

    def c(self, i):
        self.held["c", i] = over_seq(self.part(i, (1,)), 1)

    def b(self, i):
        self.held["b", i] = over_seq(self.part(i, (2,), self.held["a", i]), 2)

    def d(self, i):
        self.held["d", i] = self.part(i, (0,), self.held["c", i], jnp.float32)

    def hide(self, i):
        gate, up = (self.held["d", i] + wide(self.now(self.held["b", i])))[0]
        hidden = narrow(jax.nn.silu(gate) * up)
        far = over_seq(hidden, 2)
        self.held["hide", i] = hidden, far, over_seq(hidden, 1)
        self.last = hidden

    def down(self, pieces, bits, total=None):
        return products(pieces, self.down_weight, [self.seq ^ bit for bit in bits], total)

    def own(self, i):
        hidden, far, near = self.held["hide", i]
        self.held["own", i] = self.last = self.down((self.now(hidden), near), (0, 1))

    def forward(self, i):
        far = self.now(self.held["hide", i][1])
        self.held["pass", i] = far, over_seq(far, 1)

    def rest(self, i):
        far, last = self.held["pass", i]
        self.held["rest", i] = self.last = self.down((self.now(far), last), (2, 3), self.held["own", i])

    def out(self, i):
        partial_sum = self.now(self.held["rest", i])
        half = partial_sum.shape[0] // 2
        low, top = partial_sum[:half], partial_sum[half:]
        own = jnp.where(self.core == 0, low, top)
        others = jnp.where(self.core == 0, top, low)
        one, two = narrow(jnp.where(self.even, others, own)), narrow(others)
        self.held["out", i] = own, over_both(one, FIRST_OUT), over_both(two, SECOND)
        self.last = one

    def mix(self, i):
        own, first, second = self.held["out", i]
        pair = wide(self.now(first)) + jnp.where(self.even, own, wide(second))
        rows = pair.shape[0] // 2
        low, top = pair[:rows], pair[rows:]
        kept = jnp.where(self.x == 0, low, top)
        sent = narrow(jnp.where(self.x == 0, top, low))
        self.held["mix", i] = kept, over_seq(sent, 2)
        self.last = sent

    def far_out(self, i):
        kept, got = self.held["mix", i]
        got = self.now(got)
        sent = jnp.where(self.high == self.x, got, narrow(kept))
        kept = jnp.where(self.high == self.x, kept, wide(got))
        self.held["far_out", i] = kept, over_tp(sent, 2)
        self.last = sent

    def end(self, i):
        kept, got = self.held["far_out", i]
        self.held["end", i] = scaled(kept + wide(self.now(got)))
        self.last = self.held["end", i][0]


def four_shards(*arrays):
    return Steps(*arrays).run(ORDER)


def solution(mesh):
    placed = (
        P(("groups", "seq"), "tp"),
        P(("groups", "seq"), "tp"),
        P("seq", "tp"),
        P("seq", "tp"),
        P("tp", "seq"),
    )
    fours = mesh.shape["tp"] == 4 and mesh.shape["seq"] == 4
    return jax.shard_map(
        four_shards if fours else any_shards,
        mesh=mesh,
        in_specs=placed,
        out_specs=(P(("groups", "seq"), "tp"), P(("groups", "seq"), "tp")),
        check_vma=False,
    )
```

```python
import functools

import jax
import jax.numpy as jnp
from jax import lax
from jax.experimental import pallas as pl
from jax.experimental.pallas import tpu as pltpu
from jax.sharding import PartitionSpec as P

ROWS = (32, 64, 32)
ORDER = (
    "far0", "sel0", "far1", "arr0", "sel1", "far2", "take0", "a0", "c0", "arr1", "b0", "sel2", "d0", "take1",
    "a1", "c1", "arr2", "hide0", "b1", "d1", "own0", "take2", "a2", "c2", "forward0", "b2", "d2", "hide1",
    "rest0", "out0", "own1", "mix0", "hide2", "own2", "far_out0", "end0", "forward1", "rest1", "out1",
    "forward2", "rest2", "out2", "mix1", "mix2", "far_out1", "far_out2", "end1", "end2",
)
TILE = 256
COST = 1 << 33
VMEM = 32 << 20


def blocks(array):
    return array.reshape(array.shape[0], array.shape[1] // 128, 128)


def block_scale(array):
    return jnp.max(jnp.abs(blocks(array)), axis=2) + 1e-06


def expand(values, scales):
    return (blocks(values.astype(jnp.float32)) * scales[:, :, None]).reshape(values.shape)


def scaled(total):
    scales = block_scale(total)
    values = (blocks(total) / scales[:, :, None]).reshape(total.shape).astype(jnp.bfloat16)
    return values, scales


def wide(array):
    return array.astype(jnp.float32)


def narrow(array):
    return array.astype(jnp.bfloat16)


def dot(a, b):
    return jnp.dot(a, b, preferred_element_type=jnp.float32)


def any_shards(tokens_values, tokens_scales, gate_weight, up_weight, down_weight):
    mine = narrow(expand(tokens_values, tokens_scales))
    mine = lax.all_gather(mine, "tp", axis=1, tiled=True)
    inputs = lax.all_to_all(mine, "seq", split_axis=1, concat_axis=0, tiled=True)
    gate = narrow(dot(inputs, gate_weight))
    up = narrow(dot(inputs, up_weight))
    gate = wide(lax.psum_scatter(gate, "seq", scatter_dimension=0, tiled=True))
    up = wide(lax.psum_scatter(up, "seq", scatter_dimension=0, tiled=True))
    hidden = narrow(jax.nn.silu(gate) * up)
    hidden = lax.all_gather(hidden, "seq", axis=0, tiled=True)
    partial_sum = narrow(dot(hidden, down_weight))
    partial_sum = lax.all_to_all(partial_sum, "seq", split_axis=0, concat_axis=1, tiled=True)
    return scaled(wide(lax.psum_scatter(partial_sum, "tp", scatter_dimension=1, tiled=True)))


def over_seq(array, bit):
    return lax.ppermute(array, "seq", [(i, i ^ bit) for i in range(4)])


def over_tp(array, bit):
    return lax.ppermute(array, "tp", [(i, i ^ bit) for i in range(4)])


def device(tp, seq):
    return tp * 4 + seq


FIRST_IN, SECOND, FIRST_OUT = [], [], []
for tp in range(4):
    for seq in range(4):
        if (tp ^ seq) & 1:
            FIRST_IN.append((device(tp, seq), device(tp, seq ^ 1)))
            SECOND.append((device(tp, seq), device(tp ^ 1, seq ^ 1)))
            FIRST_OUT.append((device(tp, seq), device(tp ^ 1, seq)))
        else:
            FIRST_IN.append((device(tp, seq), device(tp ^ 1, seq)))
            FIRST_OUT.append((device(tp, seq), device(tp, seq ^ 1)))


def over_both(array, pairs):
    return lax.ppermute(array, ("tp", "seq"), pairs)


def arrange(low_first, one, other):
    return jnp.concatenate([jnp.where(low_first, one, other), jnp.where(low_first, other, one)], axis=0)


def sums_kernel(has_got, quarter, some, gate_weight, up_weight, *rest):
    out, near, done = rest[-3:]
    tiles, tile = near.shape[1], near.shape[3]
    base = quarter[0] * (tiles * tile)
    copies = [
        [
            pltpu.make_async_copy(
                weight.at[:, pl.ds(pl.multiple_of(base + j * tile, tile), tile)], near.at[k, j], done.at[k, j]
            )
            for k, weight in enumerate((gate_weight, up_weight))
        ]
        for j in range(tiles)
    ]
    for pair in copies:
        for copy in pair:
            copy.start()
    for j, pair in enumerate(copies):
        here = pl.ds(j * tile, tile)
        for k, copy in enumerate(pair):
            copy.wait()
            value = dot(some[...], near[k, j])
            if has_got:
                value += wide(rest[0][k, :, here])
            out[k, :, here] = value.astype(out.dtype)


def sums(some, gate_weight, up_weight, quarter, got=None, kind=jnp.bfloat16):
    rows, deep = some.shape
    width = gate_weight.shape[1] // 4
    near = pl.BlockSpec(memory_space=pltpu.VMEM)
    far = pl.BlockSpec(memory_space=pl.ANY)
    return pl.pallas_call(
        functools.partial(sums_kernel, got is not None),
        out_shape=jax.ShapeDtypeStruct((2, rows, width), kind),
        in_specs=[pl.BlockSpec(memory_space=pltpu.SMEM), near, far, far] + [near] * (got is not None),
        out_specs=near,
        scratch_shapes=[
            pltpu.VMEM((2, width // TILE, deep, TILE), gate_weight.dtype),
            pltpu.SemaphoreType.DMA((2, width // TILE)),
        ],
        compiler_params=pltpu.CompilerParams(vmem_limit_bytes=VMEM),
        cost_estimate=pl.CostEstimate(flops=COST, bytes_accessed=1, transcendentals=0),
    )(quarter.reshape(1).astype(jnp.int32), some, gate_weight, up_weight, *([] if got is None else [got]))


def products_kernel(has_total, quarters, one, two, weight, *rest):
    out, near, done = rest[-3:]
    deep, tile = near.shape[2], near.shape[3]
    pieces = one, two
    copies = [
        [
            pltpu.make_async_copy(
                weight.at[pl.ds(pl.multiple_of(quarters[k] * deep, deep), deep), pl.ds(j * tile, tile)],
                near.at[k, j],
                done.at[k, j],
            )
            for k in range(2)
        ]
        for j in range(near.shape[1])
    ]
    for pair in copies:
        for copy in pair:
            copy.start()
    for j, pair in enumerate(copies):
        here = pl.ds(j * tile, tile)
        for copy in pair:
            copy.wait()
        value = sum(dot(pieces[k][...], near[k, j]) for k in range(2))
        if has_total:
            value += rest[0][:, here]
        out[:, here] = value


def products(pieces, weight, quarters, total=None):
    rows, deep = pieces[0].shape
    tiles = weight.shape[1] // (2 * TILE)
    near = pl.BlockSpec(memory_space=pltpu.VMEM)
    return pl.pallas_call(
        functools.partial(products_kernel, total is not None),
        out_shape=jax.ShapeDtypeStruct((rows, weight.shape[1]), jnp.float32),
        in_specs=[pl.BlockSpec(memory_space=pltpu.SMEM), near, near, pl.BlockSpec(memory_space=pl.ANY)]
        + [near] * (total is not None),
        out_specs=near,
        scratch_shapes=[
            pltpu.VMEM((2, tiles, deep, 2 * TILE), weight.dtype),
            pltpu.SemaphoreType.DMA((2, tiles)),
        ],
        compiler_params=pltpu.CompilerParams(vmem_limit_bytes=VMEM),
        cost_estimate=pl.CostEstimate(flops=COST, bytes_accessed=1, transcendentals=0),
    )(jnp.stack(quarters).astype(jnp.int32), *pieces, weight, *([] if total is None else [total]))


class Steps:

    def __init__(self, tokens_values, tokens_scales, gate_weight, up_weight, down_weight):
        tp, seq = lax.axis_index("tp"), lax.axis_index("seq")
        self.seq, self.x, self.core = seq, seq >> 1, seq & 1
        self.high, self.even = tp >> 1, (tp ^ seq) & 1 == 0
        self.gate_weight = pltpu.with_memory_space_constraint(gate_weight, pltpu.HBM)
        self.up_weight = pltpu.with_memory_space_constraint(up_weight, pltpu.HBM)
        self.down_weight = pltpu.with_memory_space_constraint(down_weight, pltpu.HBM)
        self.mine = narrow(expand(tokens_values, tokens_scales))
        unit = tokens_values.shape[0] // sum(ROWS)
        self.starts = [sum(ROWS[:i]) * unit for i in range(len(ROWS) + 1)]
        self.last = self.mine
        self.held = {}

    def run(self, order):
        for step in order:
            with jax.named_scope(step):
                getattr(self, step[:-1])(int(step[-1]))
        return tuple(
            jnp.concatenate([self.held["end", i][k] for i in range(len(ROWS))], axis=0) for k in range(2)
        )

    def now(self, array):
        return lax.optimization_barrier((array, self.last))[0]

    def far(self, i):
        part = self.now(self.mine[self.starts[i] : self.starts[i + 1]])
        self.held["far", i] = part, over_tp(part, 2)

    def sel(self, i):
        part, other = self.held["far", i]
        other = self.now(other)
        sent = jnp.where(self.high == self.x, other, part)
        kept = jnp.where(self.high == self.x, part, other)
        self.held["sel", i] = kept, over_seq(sent, 2)
        self.last = sent

    def arr(self, i):
        kept, got = self.held["sel", i]
        pair = arrange(self.x == 0, kept, self.now(got))
        self.held["arr", i] = pair, over_both(pair, FIRST_IN), over_both(pair, SECOND)
        self.last = pair

    def take(self, i):
        pair, first, second = self.held["arr", i]
        first = self.now(first)
        own = jnp.where(self.even, pair, first)
        others = jnp.where(self.even, first, second)
        self.held["take", i] = self.last = arrange(self.core == 0, own, others)

    def part(self, i, bit, got=None, kind=jnp.bfloat16):
        some = self.now(self.held["take", i])
        self.last = sums(some, self.gate_weight, self.up_weight, self.seq ^ bit, got, kind)
        return self.last

    def a(self, i):
        self.held["a", i] = over_seq(self.part(i, 3), 1)

    def c(self, i):
        self.held["c", i] = over_seq(self.part(i, 1), 1)

    def b(self, i):
        self.held["b", i] = over_seq(self.part(i, 2, self.held["a", i]), 2)

    def d(self, i):
        self.held["d", i] = self.part(i, 0, self.held["c", i], jnp.float32)

    def hide(self, i):
        gate, up = self.held["d", i] + wide(self.now(self.held["b", i]))
        hidden = narrow(jax.nn.silu(gate) * up)
        far = over_seq(hidden, 2)
        self.held["hide", i] = hidden, far, over_seq(hidden, 1)
        self.last = hidden

    def down(self, pieces, bits, total=None):
        return products(pieces, self.down_weight, [self.seq ^ bit for bit in bits], total)

    def own(self, i):
        hidden, far, near = self.held["hide", i]
        self.held["own", i] = self.last = self.down((self.now(hidden), near), (0, 1))

    def forward(self, i):
        far = self.now(self.held["hide", i][1])
        self.held["pass", i] = far, over_seq(far, 1)

    def rest(self, i):
        far, last = self.held["pass", i]
        self.held["rest", i] = self.last = self.down((self.now(far), last), (2, 3), self.held["own", i])

    def out(self, i):
        partial_sum = self.now(self.held["rest", i])
        half = partial_sum.shape[0] // 2
        low, top = partial_sum[:half], partial_sum[half:]
        own = jnp.where(self.core == 0, low, top)
        others = jnp.where(self.core == 0, top, low)
        one, two = narrow(jnp.where(self.even, others, own)), narrow(others)
        self.held["out", i] = own, over_both(one, FIRST_OUT), over_both(two, SECOND)
        self.last = one

    def mix(self, i):
        own, first, second = self.held["out", i]
        pair = wide(self.now(first)) + jnp.where(self.even, own, wide(second))
        rows = pair.shape[0] // 2
        low, top = pair[:rows], pair[rows:]
        kept = jnp.where(self.x == 0, low, top)
        sent = narrow(jnp.where(self.x == 0, top, low))
        self.held["mix", i] = kept, over_seq(sent, 2)
        self.last = sent

    def far_out(self, i):
        kept, got = self.held["mix", i]
        got = self.now(got)
        sent = jnp.where(self.high == self.x, got, narrow(kept))
        kept = jnp.where(self.high == self.x, kept, wide(got))
        self.held["far_out", i] = kept, over_tp(sent, 2)
        self.last = sent

    def end(self, i):
        kept, got = self.held["far_out", i]
        self.held["end", i] = scaled(kept + wide(self.now(got)))
        self.last = self.held["end", i][0]


def four_shards(*arrays):
    return Steps(*arrays).run(ORDER)


def solution(mesh):
    placed = (
        P(("groups", "seq"), "tp"),
        P(("groups", "seq"), "tp"),
        P("seq", "tp"),
        P("seq", "tp"),
        P("tp", "seq"),
    )
    fours = mesh.shape["tp"] == 4 and mesh.shape["seq"] == 4
    return jax.shard_map(
        four_shards if fours else any_shards,
        mesh=mesh,
        in_specs=placed,
        out_specs=(P(("groups", "seq"), "tp"), P(("groups", "seq"), "tp")),
        check_vma=False,
    )
```

```python
import functools

import jax
import jax.numpy as jnp
from jax import lax
from jax.experimental import pallas as pl
from jax.experimental.pallas import tpu as pltpu
from jax.sharding import PartitionSpec as P

ROWS = (48, 48, 32)
ORDER = (
    "far0", "load3", "load1", "sel0", "far1", "load2", "arr0", "sel1", "far2", "load0", "take0", "a0", "c0",
    "arr1", "b0", "sel2", "d0", "take1", "a1", "c1", "arr2", "hide0", "b1", "d1", "own0", "take2", "a2", "c2",
    "forward0", "b2", "d2", "hide1", "rest0", "out0", "hide2", "own1", "mix0", "forward1", "own2", "far_out0",
    "rest1", "forward2", "out1", "end0", "rest2", "out2", "mix1", "mix2", "far_out1", "far_out2", "end1",
    "end2",
)
TILE = 256
COST = 1 << 33
VMEM = 10 << 20


def blocks(array):
    return array.reshape(array.shape[0], array.shape[1] // 128, 128)


def block_scale(array):
    return jnp.max(jnp.abs(blocks(array)), axis=2) + 1e-06


def expand(values, scales):
    return (blocks(values.astype(jnp.float32)) * scales[:, :, None]).reshape(values.shape)


def scaled(total):
    scales = block_scale(total)
    values = (blocks(total) / scales[:, :, None]).reshape(total.shape).astype(jnp.bfloat16)
    return values, scales


def wide(array):
    return array.astype(jnp.float32)


def narrow(array):
    return array.astype(jnp.bfloat16)


def dot(a, b):
    return jnp.dot(a, b, preferred_element_type=jnp.float32)


def any_shards(tokens_values, tokens_scales, gate_weight, up_weight, down_weight):
    mine = narrow(expand(tokens_values, tokens_scales))
    mine = lax.all_gather(mine, "tp", axis=1, tiled=True)
    inputs = lax.all_to_all(mine, "seq", split_axis=1, concat_axis=0, tiled=True)
    gate = narrow(dot(inputs, gate_weight))
    up = narrow(dot(inputs, up_weight))
    gate = wide(lax.psum_scatter(gate, "seq", scatter_dimension=0, tiled=True))
    up = wide(lax.psum_scatter(up, "seq", scatter_dimension=0, tiled=True))
    hidden = narrow(jax.nn.silu(gate) * up)
    hidden = lax.all_gather(hidden, "seq", axis=0, tiled=True)
    partial_sum = narrow(dot(hidden, down_weight))
    partial_sum = lax.all_to_all(partial_sum, "seq", split_axis=0, concat_axis=1, tiled=True)
    return scaled(wide(lax.psum_scatter(partial_sum, "tp", scatter_dimension=1, tiled=True)))


def over_seq(array, bit):
    return lax.ppermute(array, "seq", [(i, i ^ bit) for i in range(4)])


def over_tp(array, bit):
    return lax.ppermute(array, "tp", [(i, i ^ bit) for i in range(4)])


def device(tp, seq):
    return tp * 4 + seq


FIRST_IN, SECOND, FIRST_OUT = [], [], []
for tp in range(4):
    for seq in range(4):
        if (tp ^ seq) & 1:
            FIRST_IN.append((device(tp, seq), device(tp, seq ^ 1)))
            SECOND.append((device(tp, seq), device(tp ^ 1, seq ^ 1)))
            FIRST_OUT.append((device(tp, seq), device(tp ^ 1, seq)))
        else:
            FIRST_IN.append((device(tp, seq), device(tp ^ 1, seq)))
            FIRST_OUT.append((device(tp, seq), device(tp, seq ^ 1)))


def over_both(array, pairs):
    return lax.ppermute(array, ("tp", "seq"), pairs)


def arrange(low_first, one, other):
    return jnp.concatenate([jnp.where(low_first, one, other), jnp.where(low_first, other, one)], axis=0)


def load_kernel(quarter, gate_weight, up_weight, out, done):
    width = out.shape[2]
    here = pl.ds(pl.multiple_of(quarter[0] * width, width), width)
    pieces = done.shape[1]
    rows = out.shape[1] // pieces
    copies = [
        pltpu.make_async_copy(weight.at[pl.ds(i * rows, rows), here], out.at[k, pl.ds(i * rows, rows)], done.at[k, i])
        for k, weight in enumerate((gate_weight, up_weight))
        for i in range(pieces)
    ]
    for copy in copies:
        copy.start()
    for copy in copies:
        copy.wait()


def load(gate_weight, up_weight, quarter):
    deep, width = gate_weight.shape
    far = pl.BlockSpec(memory_space=pl.ANY)
    return pl.pallas_call(
        load_kernel,
        out_shape=jax.ShapeDtypeStruct((2, deep, width // 4), gate_weight.dtype),
        in_specs=[pl.BlockSpec(memory_space=pltpu.SMEM), far, far],
        out_specs=far,
        scratch_shapes=[pltpu.SemaphoreType.DMA((2, 4))],
        cost_estimate=pl.CostEstimate(flops=COST, bytes_accessed=1, transcendentals=0),
    )(quarter.reshape(1).astype(jnp.int32), gate_weight, up_weight)


def sums_kernel(has_got, some, weights, *rest):
    out = rest[-1]

    @pl.loop(0, 2)
    def side(k):
        value = dot(some[...], weights[k])
        if has_got:
            value += wide(rest[0][k])
        out[k] = value.astype(out.dtype)


def sums(some, weights, got=None, kind=jnp.bfloat16):
    near = pl.BlockSpec(memory_space=pltpu.VMEM)
    return pl.pallas_call(
        functools.partial(sums_kernel, got is not None),
        out_shape=jax.ShapeDtypeStruct((2, some.shape[0], weights.shape[2]), kind),
        in_specs=[near] * (2 + (got is not None)),
        out_specs=near,
        compiler_params=pltpu.CompilerParams(vmem_limit_bytes=VMEM),
        cost_estimate=pl.CostEstimate(flops=COST, bytes_accessed=1, transcendentals=0),
    )(some, weights, *([] if got is None else [got]))


def products_kernel(has_total, quarters, one, two, weight, *rest):
    out, near, done = rest[-3:]
    deep, tile = near.shape[2], near.shape[3]
    pieces = one, two
    copies = [
        [
            pltpu.make_async_copy(
                weight.at[pl.ds(pl.multiple_of(quarters[k] * deep, deep), deep), pl.ds(j * tile, tile)],
                near.at[k, j],
                done.at[k, j],
            )
            for k in range(2)
        ]
        for j in range(near.shape[1])
    ]
    for pair in copies:
        for copy in pair:
            copy.start()
    for j, pair in enumerate(copies):
        here = pl.ds(j * tile, tile)
        for copy in pair:
            copy.wait()
        value = sum(dot(pieces[k][...], near[k, j]) for k in range(2))
        if has_total:
            value += rest[0][:, here]
        out[:, here] = value


def products(pieces, weight, quarters, total=None):
    rows, deep = pieces[0].shape
    tiles = weight.shape[1] // (2 * TILE)
    near = pl.BlockSpec(memory_space=pltpu.VMEM)
    return pl.pallas_call(
        functools.partial(products_kernel, total is not None),
        out_shape=jax.ShapeDtypeStruct((rows, weight.shape[1]), jnp.float32),
        in_specs=[pl.BlockSpec(memory_space=pltpu.SMEM), near, near, pl.BlockSpec(memory_space=pl.ANY)]
        + [near] * (total is not None),
        out_specs=near,
        scratch_shapes=[
            pltpu.VMEM((2, tiles, deep, 2 * TILE), weight.dtype),
            pltpu.SemaphoreType.DMA((2, tiles)),
        ],
        compiler_params=pltpu.CompilerParams(vmem_limit_bytes=VMEM),
        cost_estimate=pl.CostEstimate(flops=COST, bytes_accessed=1, transcendentals=0),
    )(jnp.stack(quarters).astype(jnp.int32), *pieces, weight, *([] if total is None else [total]))


def hide_kernel(held, got, out):
    rows = 32

    @pl.loop(0, out.shape[0] // rows)
    def strip(i):
        here = pl.ds(pl.multiple_of(i * rows, rows), rows)
        gate = held[0, here] + wide(got[0, here])
        up = held[1, here] + wide(got[1, here])
        out[here] = narrow(jax.nn.silu(gate) * up)


def hide(held, got):
    near = pl.BlockSpec(memory_space=pltpu.VMEM)
    return pl.pallas_call(
        hide_kernel,
        out_shape=jax.ShapeDtypeStruct(held.shape[1:], got.dtype),
        in_specs=[near] * 2,
        out_specs=near,
        compiler_params=pltpu.CompilerParams(vmem_limit_bytes=VMEM),
        cost_estimate=pl.CostEstimate(flops=COST, bytes_accessed=1, transcendentals=0),
    )(held, got)


def end_kernel(kept, got, values, scales):
    for j in range(scales.shape[1]):
        here = pl.ds(j * 128, 128)
        total = kept[:, here] + wide(got[:, here])
        scale = jnp.max(jnp.abs(total), axis=1, keepdims=True) + 1e-06
        values[:, here] = narrow(total / scale)
        scales[:, pl.ds(j, 1)] = scale


def end(kept, got):
    rows, width = kept.shape
    near = pl.BlockSpec(memory_space=pltpu.VMEM)
    return pl.pallas_call(
        end_kernel,
        out_shape=(
            jax.ShapeDtypeStruct((rows, width), got.dtype),
            jax.ShapeDtypeStruct((rows, width // 128), kept.dtype),
        ),
        in_specs=[near] * 2,
        out_specs=(near, near),
        compiler_params=pltpu.CompilerParams(vmem_limit_bytes=VMEM),
        cost_estimate=pl.CostEstimate(flops=COST, bytes_accessed=1, transcendentals=0),
    )(kept, got)


class Steps:

    def __init__(self, tokens_values, tokens_scales, gate_weight, up_weight, down_weight):
        tp, seq = lax.axis_index("tp"), lax.axis_index("seq")
        self.seq, self.x, self.core = seq, seq >> 1, seq & 1
        self.high, self.even = tp >> 1, (tp ^ seq) & 1 == 0
        self.gate_weight = pltpu.with_memory_space_constraint(gate_weight, pltpu.HBM)
        self.up_weight = pltpu.with_memory_space_constraint(up_weight, pltpu.HBM)
        self.down_weight = pltpu.with_memory_space_constraint(down_weight, pltpu.HBM)
        self.mine = narrow(expand(tokens_values, tokens_scales))
        unit = tokens_values.shape[0] // sum(ROWS)
        self.starts = [sum(ROWS[:i]) * unit for i in range(len(ROWS) + 1)]
        self.last = self.mine
        self.held = {}

    def run(self, order):
        for step in order:
            with jax.named_scope(step):
                getattr(self, step[:-1])(int(step[-1]))
        return tuple(
            jnp.concatenate([self.held["end", i][k] for i in range(len(ROWS))], axis=0) for k in range(2)
        )

    def now(self, array):
        return lax.optimization_barrier((array, self.last))[0]

    def far(self, i):
        part = self.now(self.mine[self.starts[i] : self.starts[i + 1]])
        self.held["far", i] = part, over_tp(part, 2)

    def sel(self, i):
        part, other = self.held["far", i]
        other = self.now(other)
        sent = jnp.where(self.high == self.x, other, part)
        kept = jnp.where(self.high == self.x, part, other)
        self.held["sel", i] = kept, over_seq(sent, 2)
        self.last = sent

    def arr(self, i):
        kept, got = self.held["sel", i]
        pair = arrange(self.x == 0, kept, self.now(got))
        self.held["arr", i] = pair, over_both(pair, FIRST_IN), over_both(pair, SECOND)
        self.last = pair

    def take(self, i):
        pair, first, second = self.held["arr", i]
        first = self.now(first)
        own = jnp.where(self.even, pair, first)
        others = jnp.where(self.even, first, second)
        self.held["take", i] = self.last = arrange(self.core == 0, own, others)

    def load(self, bits):
        gate_weight = self.now(self.gate_weight)
        self.held["load", bits] = self.last = load(gate_weight, self.up_weight, self.seq ^ bits)

    def part(self, i, bits, got=None, kind=jnp.bfloat16):
        some = self.now(self.held["take", i])
        self.last = sums(some, self.held["load", bits], got, kind)
        return self.last

    def a(self, i):
        self.held["a", i] = over_seq(self.part(i, 3), 1)

    def c(self, i):
        self.held["c", i] = over_seq(self.part(i, 1), 1)

    def b(self, i):
        self.held["b", i] = over_seq(self.part(i, 2, self.held["a", i]), 2)

    def d(self, i):
        self.held["d", i] = self.part(i, 0, self.held["c", i], jnp.float32)

    def hide(self, i):
        hidden = hide(self.held["d", i], self.now(self.held["b", i]))
        far = over_seq(hidden, 2)
        self.held["hide", i] = hidden, far, over_seq(hidden, 1)
        self.last = hidden

    def down(self, pieces, bits, total=None):
        return products(pieces, self.down_weight, [self.seq ^ bit for bit in bits], total)

    def own(self, i):
        hidden, far, near = self.held["hide", i]
        self.held["own", i] = self.last = self.down((self.now(hidden), near), (0, 1))

    def forward(self, i):
        far = self.now(self.held["hide", i][1])
        self.held["pass", i] = far, over_seq(far, 1)

    def rest(self, i):
        far, last = self.held["pass", i]
        self.held["rest", i] = self.last = self.down((self.now(far), last), (2, 3), self.held["own", i])

    def out(self, i):
        partial_sum = self.now(self.held["rest", i])
        half = partial_sum.shape[0] // 2
        low, top = partial_sum[:half], partial_sum[half:]
        own = jnp.where(self.core == 0, low, top)
        others = jnp.where(self.core == 0, top, low)
        one, two = narrow(jnp.where(self.even, others, own)), narrow(others)
        self.held["out", i] = own, over_both(one, FIRST_OUT), over_both(two, SECOND)
        self.last = one

    def mix(self, i):
        own, first, second = self.held["out", i]
        pair = wide(self.now(first)) + jnp.where(self.even, own, wide(second))
        rows = pair.shape[0] // 2
        low, top = pair[:rows], pair[rows:]
        kept = jnp.where(self.x == 0, low, top)
        sent = narrow(jnp.where(self.x == 0, top, low))
        self.held["mix", i] = kept, over_seq(sent, 2)
        self.last = sent

    def far_out(self, i):
        kept, got = self.held["mix", i]
        got = self.now(got)
        sent = jnp.where(self.high == self.x, got, narrow(kept))
        kept = jnp.where(self.high == self.x, kept, wide(got))
        self.held["far_out", i] = kept, over_tp(sent, 2)
        self.last = sent

    def end(self, i):
        kept, got = self.held["far_out", i]
        self.held["end", i] = end(kept, self.now(got))
        self.last = self.held["end", i][0]


def four_shards(*arrays):
    return Steps(*arrays).run(ORDER)


def solution(mesh):
    placed = (
        P(("groups", "seq"), "tp"),
        P(("groups", "seq"), "tp"),
        P("seq", "tp"),
        P("seq", "tp"),
        P("tp", "seq"),
    )
    fours = mesh.shape["tp"] == 4 and mesh.shape["seq"] == 4
    return jax.shard_map(
        four_shards if fours else any_shards,
        mesh=mesh,
        in_specs=placed,
        out_specs=(P(("groups", "seq"), "tp"), P(("groups", "seq"), "tp")),
        check_vma=False,
    )
```

```python
import functools

import jax
import jax.numpy as jnp
from jax import lax
from jax.experimental import pallas as pl
from jax.experimental.pallas import tpu as pltpu
from jax.sharding import PartitionSpec as P

ROWS = (48, 32, 48)
ORDER = (
    "far0", "load3", "load1", "sel0", "far1", "load2", "arr0", "sel1", "far2", "load0", "take0", "a0", "c0",
    "arr1", "b0", "d0", "sel2", "take1", "a1", "c1", "b1", "arr2", "hide0", "d1", "take2", "a2", "c2", "b2",
    "own0", "d2", "hide1", "forward0", "hide2", "rest0", "out0", "own1", "mix0", "forward1", "own2",
    "far_out0", "rest1", "forward2", "out1", "end0", "rest2", "out2", "mix1", "mix2", "far_out1", "far_out2",
    "end1", "end2",
)
TILE = 256
COST = 1 << 33
VMEM = 10 << 20


def blocks(array):
    return array.reshape(array.shape[0], array.shape[1] // 128, 128)


def block_scale(array):
    return jnp.max(jnp.abs(blocks(array)), axis=2) + 1e-06


def expand(values, scales):
    return (blocks(values.astype(jnp.float32)) * scales[:, :, None]).reshape(values.shape)


def scaled(total):
    scales = block_scale(total)
    values = (blocks(total) / scales[:, :, None]).reshape(total.shape).astype(jnp.bfloat16)
    return values, scales


def wide(array):
    return array.astype(jnp.float32)


def narrow(array):
    return array.astype(jnp.bfloat16)


def dot(a, b):
    return jnp.dot(a, b, preferred_element_type=jnp.float32)


def any_shards(tokens_values, tokens_scales, gate_weight, up_weight, down_weight):
    mine = narrow(expand(tokens_values, tokens_scales))
    mine = lax.all_gather(mine, "tp", axis=1, tiled=True)
    inputs = lax.all_to_all(mine, "seq", split_axis=1, concat_axis=0, tiled=True)
    gate = narrow(dot(inputs, gate_weight))
    up = narrow(dot(inputs, up_weight))
    gate = wide(lax.psum_scatter(gate, "seq", scatter_dimension=0, tiled=True))
    up = wide(lax.psum_scatter(up, "seq", scatter_dimension=0, tiled=True))
    hidden = narrow(jax.nn.silu(gate) * up)
    hidden = lax.all_gather(hidden, "seq", axis=0, tiled=True)
    partial_sum = narrow(dot(hidden, down_weight))
    partial_sum = lax.all_to_all(partial_sum, "seq", split_axis=0, concat_axis=1, tiled=True)
    return scaled(wide(lax.psum_scatter(partial_sum, "tp", scatter_dimension=1, tiled=True)))


def over_seq(array, bit):
    return lax.ppermute(array, "seq", [(i, i ^ bit) for i in range(4)])


def over_tp(array, bit):
    return lax.ppermute(array, "tp", [(i, i ^ bit) for i in range(4)])


def device(tp, seq):
    return tp * 4 + seq


FIRST_IN, SECOND, FIRST_OUT = [], [], []
for tp in range(4):
    for seq in range(4):
        if (tp ^ seq) & 1:
            FIRST_IN.append((device(tp, seq), device(tp, seq ^ 1)))
            SECOND.append((device(tp, seq), device(tp ^ 1, seq ^ 1)))
            FIRST_OUT.append((device(tp, seq), device(tp ^ 1, seq)))
        else:
            FIRST_IN.append((device(tp, seq), device(tp ^ 1, seq)))
            FIRST_OUT.append((device(tp, seq), device(tp, seq ^ 1)))


def over_both(array, pairs):
    return lax.ppermute(array, ("tp", "seq"), pairs)


def arrange(low_first, one, other):
    return jnp.concatenate([jnp.where(low_first, one, other), jnp.where(low_first, other, one)], axis=0)


def load_kernel(quarter, gate_weight, up_weight, out, done):
    width = out.shape[2]
    here = pl.ds(pl.multiple_of(quarter[0] * width, width), width)
    pieces = done.shape[1]
    rows = out.shape[1] // pieces
    copies = [
        pltpu.make_async_copy(weight.at[pl.ds(i * rows, rows), here], out.at[k, pl.ds(i * rows, rows)], done.at[k, i])
        for k, weight in enumerate((gate_weight, up_weight))
        for i in range(pieces)
    ]
    for copy in copies:
        copy.start()
    for copy in copies:
        copy.wait()


def load(gate_weight, up_weight, quarter):
    deep, width = gate_weight.shape
    far = pl.BlockSpec(memory_space=pl.ANY)
    return pl.pallas_call(
        load_kernel,
        out_shape=jax.ShapeDtypeStruct((2, deep, width // 4), gate_weight.dtype),
        in_specs=[pl.BlockSpec(memory_space=pltpu.SMEM), far, far],
        out_specs=pl.BlockSpec(memory_space=pltpu.VMEM),
        scratch_shapes=[pltpu.SemaphoreType.DMA((2, 4))],
        compiler_params=pltpu.CompilerParams(vmem_limit_bytes=VMEM),
        cost_estimate=pl.CostEstimate(flops=COST, bytes_accessed=1, transcendentals=0),
    )(quarter.reshape(1).astype(jnp.int32), gate_weight, up_weight)


def sums_kernel(has_got, split, some, weights, *rest):
    def value(k):
        product = dot(some[...], weights[k])
        return product + wide(rest[0][k]) if has_got else product

    if split:
        for k, out in enumerate(rest[-2:]):
            out[...] = value(k).astype(out.dtype)
    else:

        @pl.loop(0, 2)
        def side(k):
            rest[-1][k] = value(k).astype(rest[-1].dtype)


def sums(some, weights, got=None, kind=jnp.bfloat16, split=False):
    near = pl.BlockSpec(memory_space=pltpu.VMEM)
    shape = some.shape[0], weights.shape[2]
    return pl.pallas_call(
        functools.partial(sums_kernel, got is not None, split),
        out_shape=(jax.ShapeDtypeStruct(shape, kind),) * 2 if split else jax.ShapeDtypeStruct((2,) + shape, kind),
        in_specs=[near] * (2 + (got is not None)),
        out_specs=(near, near) if split else near,
        compiler_params=pltpu.CompilerParams(vmem_limit_bytes=VMEM),
        cost_estimate=pl.CostEstimate(flops=COST, bytes_accessed=1, transcendentals=0),
    )(some, weights, *([] if got is None else [got]))


def products_kernel(has_total, quarters, one, two, weight, *rest):
    out, near, done = rest[-3:]
    deep, tile = near.shape[2], near.shape[3]
    pieces = one, two
    copies = [
        [
            pltpu.make_async_copy(
                weight.at[pl.ds(pl.multiple_of(quarters[k] * deep, deep), deep), pl.ds(j * tile, tile)],
                near.at[k, j],
                done.at[k, j],
            )
            for k in range(2)
        ]
        for j in range(near.shape[1])
    ]
    for pair in copies:
        for copy in pair:
            copy.start()
    for j, pair in enumerate(copies):
        here = pl.ds(j * tile, tile)
        for copy in pair:
            copy.wait()
        value = sum(dot(pieces[k][...], near[k, j]) for k in range(2))
        if has_total:
            value += rest[0][:, here]
        out[:, here] = value


def products(pieces, weight, quarters, total=None):
    rows, deep = pieces[0].shape
    tiles = weight.shape[1] // (2 * TILE)
    near = pl.BlockSpec(memory_space=pltpu.VMEM)
    return pl.pallas_call(
        functools.partial(products_kernel, total is not None),
        out_shape=jax.ShapeDtypeStruct((rows, weight.shape[1]), jnp.float32),
        in_specs=[pl.BlockSpec(memory_space=pltpu.SMEM), near, near, pl.BlockSpec(memory_space=pl.ANY)]
        + [near] * (total is not None),
        out_specs=near,
        scratch_shapes=[
            pltpu.VMEM((2, tiles, deep, 2 * TILE), weight.dtype),
            pltpu.SemaphoreType.DMA((2, tiles)),
        ],
        compiler_params=pltpu.CompilerParams(vmem_limit_bytes=VMEM),
        cost_estimate=pl.CostEstimate(flops=COST, bytes_accessed=1, transcendentals=0),
    )(jnp.stack(quarters).astype(jnp.int32), *pieces, weight, *([] if total is None else [total]))


def hide_kernel(held, got_gate, got_up, out):
    rows = 32

    @pl.loop(0, out.shape[0] // rows)
    def strip(i):
        here = pl.ds(pl.multiple_of(i * rows, rows), rows)
        gate = held[0, here] + wide(got_gate[here])
        up = held[1, here] + wide(got_up[here])
        out[here] = narrow(jax.nn.silu(gate) * up)


def hide(held, got_gate, got_up):
    near = pl.BlockSpec(memory_space=pltpu.VMEM)
    return pl.pallas_call(
        hide_kernel,
        out_shape=jax.ShapeDtypeStruct(held.shape[1:], got_up.dtype),
        in_specs=[near] * 3,
        out_specs=near,
        compiler_params=pltpu.CompilerParams(vmem_limit_bytes=VMEM),
        cost_estimate=pl.CostEstimate(flops=COST, bytes_accessed=1, transcendentals=0),
    )(held, got_gate, got_up)


def end_kernel(kept, got, values, scales):
    for j in range(scales.shape[1]):
        here = pl.ds(j * 128, 128)
        total = kept[:, here] + wide(got[:, here])
        scale = jnp.max(jnp.abs(total), axis=1, keepdims=True) + 1e-06
        values[:, here] = narrow(total / scale)
        scales[:, pl.ds(j, 1)] = scale


def end(kept, got):
    rows, width = kept.shape
    near = pl.BlockSpec(memory_space=pltpu.VMEM)
    return pl.pallas_call(
        end_kernel,
        out_shape=(
            jax.ShapeDtypeStruct((rows, width), got.dtype),
            jax.ShapeDtypeStruct((rows, width // 128), kept.dtype),
        ),
        in_specs=[near] * 2,
        out_specs=(near, near),
        compiler_params=pltpu.CompilerParams(vmem_limit_bytes=VMEM),
        cost_estimate=pl.CostEstimate(flops=COST, bytes_accessed=1, transcendentals=0),
    )(kept, got)


class Steps:

    def __init__(self, tokens_values, tokens_scales, gate_weight, up_weight, down_weight):
        tp, seq = lax.axis_index("tp"), lax.axis_index("seq")
        self.seq, self.x, self.core = seq, seq >> 1, seq & 1
        self.high, self.even = tp >> 1, (tp ^ seq) & 1 == 0
        self.gate_weight = pltpu.with_memory_space_constraint(gate_weight, pltpu.HBM)
        self.up_weight = pltpu.with_memory_space_constraint(up_weight, pltpu.HBM)
        self.down_weight = pltpu.with_memory_space_constraint(down_weight, pltpu.HBM)
        self.mine = narrow(expand(tokens_values, tokens_scales))
        unit = tokens_values.shape[0] // sum(ROWS)
        self.starts = [sum(ROWS[:i]) * unit for i in range(len(ROWS) + 1)]
        self.last = self.mine
        self.held = {}

    def run(self, order):
        for step in order:
            with jax.named_scope(step):
                getattr(self, step[:-1])(int(step[-1]))
        return tuple(
            jnp.concatenate([self.held["end", i][k] for i in range(len(ROWS))], axis=0) for k in range(2)
        )

    def now(self, array):
        return lax.optimization_barrier((array, self.last))[0]

    def far(self, i):
        part = self.now(self.mine[self.starts[i] : self.starts[i + 1]])
        self.held["far", i] = part, over_tp(part, 2)

    def sel(self, i):
        part, other = self.held["far", i]
        other = self.now(other)
        sent = jnp.where(self.high == self.x, other, part)
        kept = jnp.where(self.high == self.x, part, other)
        self.held["sel", i] = kept, over_seq(sent, 2)
        self.last = sent

    def arr(self, i):
        kept, got = self.held["sel", i]
        pair = arrange(self.x == 0, kept, self.now(got))
        self.held["arr", i] = pair, over_both(pair, FIRST_IN), over_both(pair, SECOND)
        self.last = pair

    def take(self, i):
        pair, first, second = self.held["arr", i]
        first = self.now(first)
        own = jnp.where(self.even, pair, first)
        others = jnp.where(self.even, first, second)
        self.held["take", i] = self.last = arrange(self.core == 0, own, others)

    def load(self, bits):
        gate_weight = self.now(self.gate_weight)
        self.held["load", bits] = self.last = load(gate_weight, self.up_weight, self.seq ^ bits)

    def part(self, i, bits, got=None, kind=jnp.bfloat16, split=False):
        some = self.now(self.held["take", i])
        result = sums(some, self.held["load", bits], got, kind, split)
        self.last = result[0] if split else result
        return result

    def a(self, i):
        self.held["a", i] = over_seq(self.part(i, 3), 1)

    def c(self, i):
        self.held["c", i] = over_seq(self.part(i, 1), 1)

    def b(self, i):
        both = self.part(i, 2, self.held["a", i], split=True)
        self.held["b", i] = over_seq(both[0], 2), over_seq(both[1], 2)

    def d(self, i):
        self.held["d", i] = self.part(i, 0, self.held["c", i], jnp.float32)

    def hide(self, i):
        hidden = hide(self.held["d", i], *(self.now(got) for got in self.held["b", i]))
        far = over_seq(hidden, 2)
        self.held["hide", i] = hidden, far, over_seq(hidden, 1)
        self.last = hidden

    def down(self, pieces, bits, total=None):
        return products(pieces, self.down_weight, [self.seq ^ bit for bit in bits], total)

    def own(self, i):
        hidden, far, near = self.held["hide", i]
        self.held["own", i] = self.last = self.down((self.now(hidden), near), (0, 1))

    def forward(self, i):
        far = self.now(self.held["hide", i][1])
        self.held["pass", i] = far, over_seq(far, 1)

    def rest(self, i):
        far, last = self.held["pass", i]
        self.held["rest", i] = self.last = self.down((self.now(far), last), (2, 3), self.held["own", i])

    def out(self, i):
        partial_sum = self.now(self.held["rest", i])
        half = partial_sum.shape[0] // 2
        low, top = partial_sum[:half], partial_sum[half:]
        own = jnp.where(self.core == 0, low, top)
        others = jnp.where(self.core == 0, top, low)
        one, two = narrow(jnp.where(self.even, others, own)), narrow(others)
        self.held["out", i] = own, over_both(one, FIRST_OUT), over_both(two, SECOND)
        self.last = one

    def mix(self, i):
        own, first, second = self.held["out", i]
        pair = wide(self.now(first)) + jnp.where(self.even, own, wide(second))
        rows = pair.shape[0] // 2
        low, top = pair[:rows], pair[rows:]
        kept = jnp.where(self.x == 0, low, top)
        sent = narrow(jnp.where(self.x == 0, top, low))
        self.held["mix", i] = kept, over_seq(sent, 2)
        self.last = sent

    def far_out(self, i):
        kept, got = self.held["mix", i]
        got = self.now(got)
        sent = jnp.where(self.high == self.x, got, narrow(kept))
        kept = jnp.where(self.high == self.x, kept, wide(got))
        self.held["far_out", i] = kept, over_tp(sent, 2)
        self.last = sent

    def end(self, i):
        kept, got = self.held["far_out", i]
        self.held["end", i] = end(kept, self.now(got))
        self.last = self.held["end", i][0]


def four_shards(*arrays):
    return Steps(*arrays).run(ORDER)


def solution(mesh):
    placed = (
        P(("groups", "seq"), "tp"),
        P(("groups", "seq"), "tp"),
        P("seq", "tp"),
        P("seq", "tp"),
        P("tp", "seq"),
    )
    fours = mesh.shape["tp"] == 4 and mesh.shape["seq"] == 4
    return jax.shard_map(
        four_shards if fours else any_shards,
        mesh=mesh,
        in_specs=placed,
        out_specs=(P(("groups", "seq"), "tp"), P(("groups", "seq"), "tp")),
        check_vma=False,
    )
```

```python
import functools

import jax
import jax.numpy as jnp
from jax import lax
from jax.experimental import pallas as pl
from jax.experimental.pallas import tpu as pltpu
from jax.sharding import PartitionSpec as P

ROWS = (32, 64, 32)
ORDER = (
    "far0", "load3", "load1", "sel0", "far1", "load2", "arr0", "load0", "sel1", "far2", "take0", "a0", "c0",
    "arr1", "b0", "d0", "sel2", "take1", "a1", "c1", "b1", "arr2", "hide0", "d1", "take2", "a2", "c2", "b2",
    "d2", "down0", "own0", "down2", "hide1", "forward0", "hide2", "rest0", "out0", "own1", "mix0", "forward1",
    "own2", "far_out0", "rest1", "forward2", "out1", "end0", "rest2", "out2", "mix1", "mix2", "far_out1",
    "far_out2", "end1", "end2",
)
TILE = 256
COST = 1 << 34
VMEM = 10 << 20


def blocks(array):
    return array.reshape(array.shape[0], array.shape[1] // 128, 128)


def block_scale(array):
    return jnp.max(jnp.abs(blocks(array)), axis=2) + 1e-06


def expand(values, scales):
    return (blocks(values.astype(jnp.float32)) * scales[:, :, None]).reshape(values.shape)


def scaled(total):
    scales = block_scale(total)
    values = (blocks(total) / scales[:, :, None]).reshape(total.shape).astype(jnp.bfloat16)
    return values, scales


def wide(array):
    return array.astype(jnp.float32)


def narrow(array):
    return array.astype(jnp.bfloat16)


def dot(a, b):
    return jnp.dot(a, b, preferred_element_type=jnp.float32)


def any_shards(tokens_values, tokens_scales, gate_weight, up_weight, down_weight):
    mine = narrow(expand(tokens_values, tokens_scales))
    mine = lax.all_gather(mine, "tp", axis=1, tiled=True)
    inputs = lax.all_to_all(mine, "seq", split_axis=1, concat_axis=0, tiled=True)
    gate = narrow(dot(inputs, gate_weight))
    up = narrow(dot(inputs, up_weight))
    gate = wide(lax.psum_scatter(gate, "seq", scatter_dimension=0, tiled=True))
    up = wide(lax.psum_scatter(up, "seq", scatter_dimension=0, tiled=True))
    hidden = narrow(jax.nn.silu(gate) * up)
    hidden = lax.all_gather(hidden, "seq", axis=0, tiled=True)
    partial_sum = narrow(dot(hidden, down_weight))
    partial_sum = lax.all_to_all(partial_sum, "seq", split_axis=0, concat_axis=1, tiled=True)
    return scaled(wide(lax.psum_scatter(partial_sum, "tp", scatter_dimension=1, tiled=True)))


def over_seq(array, bit):
    return lax.ppermute(array, "seq", [(i, i ^ bit) for i in range(4)])


def over_tp(array, bit):
    return lax.ppermute(array, "tp", [(i, i ^ bit) for i in range(4)])


def device(tp, seq):
    return tp * 4 + seq


FIRST_IN, SECOND, FIRST_OUT = [], [], []
for tp in range(4):
    for seq in range(4):
        if (tp ^ seq) & 1:
            FIRST_IN.append((device(tp, seq), device(tp, seq ^ 1)))
            SECOND.append((device(tp, seq), device(tp ^ 1, seq ^ 1)))
            FIRST_OUT.append((device(tp, seq), device(tp ^ 1, seq)))
        else:
            FIRST_IN.append((device(tp, seq), device(tp ^ 1, seq)))
            FIRST_OUT.append((device(tp, seq), device(tp, seq ^ 1)))


def over_both(array, pairs):
    return lax.ppermute(array, ("tp", "seq"), pairs)


def arrange(low_first, one, other):
    return jnp.concatenate([jnp.where(low_first, one, other), jnp.where(low_first, other, one)], axis=0)


def load_kernel(quarter, gate_weight, up_weight, out, done):
    width = out.shape[2]
    here = pl.ds(pl.multiple_of(quarter[0] * width, width), width)
    pieces = done.shape[1]
    rows = out.shape[1] // pieces
    copies = [
        pltpu.make_async_copy(weight.at[pl.ds(i * rows, rows), here], out.at[k, pl.ds(i * rows, rows)], done.at[k, i])
        for k, weight in enumerate((gate_weight, up_weight))
        for i in range(pieces)
    ]
    for copy in copies:
        copy.start()
    for copy in copies:
        copy.wait()


def load(gate_weight, up_weight, quarter):
    deep, width = gate_weight.shape
    far = pl.BlockSpec(memory_space=pl.ANY)
    return pl.pallas_call(
        load_kernel,
        out_shape=jax.ShapeDtypeStruct((2, deep, width // 4), gate_weight.dtype),
        in_specs=[pl.BlockSpec(memory_space=pltpu.SMEM), far, far],
        out_specs=pl.BlockSpec(memory_space=pltpu.VMEM),
        scratch_shapes=[pltpu.SemaphoreType.DMA((2, 4))],
        compiler_params=pltpu.CompilerParams(vmem_limit_bytes=VMEM),
        cost_estimate=pl.CostEstimate(flops=COST, bytes_accessed=1, transcendentals=0),
    )(quarter.reshape(1).astype(jnp.int32), gate_weight, up_weight)


def sums_kernel(has_got, split, some, weights, *rest):
    def value(k):
        product = dot(some[...], weights[k])
        return product + wide(rest[0][k]) if has_got else product

    if split:
        for k, out in enumerate(rest[-2:]):
            out[...] = value(k).astype(out.dtype)
    else:

        @pl.loop(0, 2)
        def side(k):
            rest[-1][k] = value(k).astype(rest[-1].dtype)


def sums(some, weights, got=None, kind=jnp.bfloat16, split=False):
    near = pl.BlockSpec(memory_space=pltpu.VMEM)
    shape = some.shape[0], weights.shape[2]
    return pl.pallas_call(
        functools.partial(sums_kernel, got is not None, split),
        out_shape=(jax.ShapeDtypeStruct(shape, kind),) * 2 if split else jax.ShapeDtypeStruct((2,) + shape, kind),
        in_specs=[near] * (2 + (got is not None)),
        out_specs=(near, near) if split else near,
        compiler_params=pltpu.CompilerParams(vmem_limit_bytes=VMEM),
        cost_estimate=pl.CostEstimate(flops=COST, bytes_accessed=1, transcendentals=0),
    )(some, weights, *([] if got is None else [got]))


def load_rows_kernel(quarters, weight, out, done):
    rows = out.shape[1]
    pieces = done.shape[1]
    part = rows // pieces
    copies = [
        pltpu.make_async_copy(
            weight.at[pl.ds(pl.multiple_of(quarters[k] * rows + i * part, part), part)],
            out.at[k, pl.ds(i * part, part)],
            done.at[k, i],
        )
        for k in range(2)
        for i in range(pieces)
    ]
    for copy in copies:
        copy.start()
    for copy in copies:
        copy.wait()


def load_rows(weight, quarters):
    deep, width = weight.shape
    return pl.pallas_call(
        load_rows_kernel,
        out_shape=jax.ShapeDtypeStruct((2, deep // 4, width), weight.dtype),
        in_specs=[pl.BlockSpec(memory_space=pltpu.SMEM), pl.BlockSpec(memory_space=pl.ANY)],
        out_specs=pl.BlockSpec(memory_space=pltpu.VMEM),
        scratch_shapes=[pltpu.SemaphoreType.DMA((2, 4))],
        compiler_params=pltpu.CompilerParams(vmem_limit_bytes=VMEM),
        cost_estimate=pl.CostEstimate(flops=COST, bytes_accessed=1, transcendentals=0),
    )(jnp.stack(quarters).astype(jnp.int32), weight)


def products_kernel(has_total, one, two, weights, *rest):
    tile = 4 * TILE

    @pl.loop(0, weights.shape[2] // tile)
    def strip(j):
        here = pl.ds(pl.multiple_of(j * tile, tile), tile)
        value = dot(one[...], weights[0, :, here]) + dot(two[...], weights[1, :, here])
        rest[-1][:, here] = value + rest[0][:, here] if has_total else value


def products(pieces, weights, total=None):
    near = pl.BlockSpec(memory_space=pltpu.VMEM)
    return pl.pallas_call(
        functools.partial(products_kernel, total is not None),
        out_shape=jax.ShapeDtypeStruct((pieces[0].shape[0], weights.shape[2]), jnp.float32),
        in_specs=[near] * (3 + (total is not None)),
        out_specs=near,
        compiler_params=pltpu.CompilerParams(vmem_limit_bytes=VMEM),
        cost_estimate=pl.CostEstimate(flops=COST, bytes_accessed=1, transcendentals=0),
    )(*pieces, weights, *([] if total is None else [total]))


def begin_kernel(starts, values, turned_scales, *outs):
    scales = turned_scales[...].T
    for j in range(scales.shape[1]):
        here = pl.ds(j * 128, 128)
        scaled_values = narrow(wide(values[:, here]) * scales[:, j : j + 1])
        for i, out in enumerate(outs):
            out[:, here] = scaled_values[starts[i] : starts[i + 1]]


def begin(values, scales, starts):
    near = pl.BlockSpec(memory_space=pltpu.VMEM)
    count = len(starts) - 1
    return pl.pallas_call(
        functools.partial(begin_kernel, starts),
        out_shape=[jax.ShapeDtypeStruct((starts[i + 1] - starts[i], values.shape[1]), values.dtype) for i in range(count)],
        in_specs=[near] * 2,
        out_specs=[near] * count,
        compiler_params=pltpu.CompilerParams(vmem_limit_bytes=VMEM),
        cost_estimate=pl.CostEstimate(flops=COST, bytes_accessed=1, transcendentals=0),
    )(values, scales.T)


def hide_kernel(held, got_gate, got_up, out):
    rows = 32

    @pl.loop(0, out.shape[0] // rows)
    def strip(i):
        here = pl.ds(pl.multiple_of(i * rows, rows), rows)
        gate = held[0, here] + wide(got_gate[here])
        up = held[1, here] + wide(got_up[here])
        out[here] = narrow(jax.nn.silu(gate) * up)


def hide(held, got_gate, got_up):
    near = pl.BlockSpec(memory_space=pltpu.VMEM)
    return pl.pallas_call(
        hide_kernel,
        out_shape=jax.ShapeDtypeStruct(held.shape[1:], got_up.dtype),
        in_specs=[near] * 3,
        out_specs=near,
        compiler_params=pltpu.CompilerParams(vmem_limit_bytes=VMEM),
        cost_estimate=pl.CostEstimate(flops=COST, bytes_accessed=1, transcendentals=0),
    )(held, got_gate, got_up)


def end_kernel(count, kept, got, *rest):
    before, (values, scales) = rest[: 2 * count], rest[2 * count :]
    first = sum(part.shape[0] for part in before[::2])
    rows = pl.ds(first, kept.shape[0])
    columns = []
    for j in range(kept.shape[1] // 128):
        here = pl.ds(j * 128, 128)
        total = kept[:, here] + wide(got[:, here])
        scale = jnp.max(jnp.abs(total), axis=1, keepdims=True) + 1e-06
        values[rows, here] = narrow(total / scale)
        columns.append(scale)
    ended = jnp.concatenate(columns, axis=1)
    if not count:
        scales[...] = ended
        return
    row = 0
    for part in before[::2]:
        values[pl.ds(row, part.shape[0])] = part[...]
        row += part.shape[0]
    scales[...] = jnp.concatenate([part[...] for part in before[1::2]] + [ended], axis=0).T


def end(kept, got, before=()):
    rows, width = kept.shape
    count = len(before)
    rows += sum(values.shape[0] for values, scales in before)
    near = pl.BlockSpec(memory_space=pltpu.VMEM)
    shape = (width // 128, rows) if count else (rows, width // 128)
    return pl.pallas_call(
        functools.partial(end_kernel, count),
        out_shape=(jax.ShapeDtypeStruct((rows, width), got.dtype), jax.ShapeDtypeStruct(shape, kept.dtype)),
        in_specs=[near] * (2 + 2 * count),
        out_specs=(near, near),
        compiler_params=pltpu.CompilerParams(vmem_limit_bytes=VMEM),
        cost_estimate=pl.CostEstimate(flops=COST, bytes_accessed=1, transcendentals=0),
    )(kept, got, *(array for pair in before for array in pair))


class Steps:

    def __init__(self, tokens_values, tokens_scales, gate_weight, up_weight, down_weight):
        tp, seq = lax.axis_index("tp"), lax.axis_index("seq")
        self.seq, self.x, self.core = seq, seq >> 1, seq & 1
        self.high, self.even = tp >> 1, (tp ^ seq) & 1 == 0
        self.gate_weight = pltpu.with_memory_space_constraint(gate_weight, pltpu.HBM)
        self.up_weight = pltpu.with_memory_space_constraint(up_weight, pltpu.HBM)
        self.down_weight = pltpu.with_memory_space_constraint(down_weight, pltpu.HBM)
        unit = tokens_values.shape[0] // sum(ROWS)
        self.mine = begin(tokens_values, tokens_scales, [sum(ROWS[:i]) * unit for i in range(len(ROWS) + 1)])
        self.last = self.mine[0]
        self.held = {}

    def run(self, order):
        for step in order:
            with jax.named_scope(step):
                getattr(self, step[:-1])(int(step[-1]))
        values, scales = self.held["end", len(ROWS) - 1]
        return values, scales.T

    def now(self, array):
        return lax.optimization_barrier((array, self.last))[0]

    def far(self, i):
        part = self.now(self.mine[i])
        self.held["far", i] = part, over_tp(part, 2)

    def sel(self, i):
        part, other = self.held["far", i]
        other = self.now(other)
        sent = jnp.where(self.high == self.x, other, part)
        kept = jnp.where(self.high == self.x, part, other)
        self.held["sel", i] = kept, over_seq(sent, 2)
        self.last = sent

    def arr(self, i):
        kept, got = self.held["sel", i]
        pair = arrange(self.x == 0, kept, self.now(got))
        self.held["arr", i] = pair, over_both(pair, FIRST_IN), over_both(pair, SECOND)
        self.last = pair

    def take(self, i):
        pair, first, second = self.held["arr", i]
        first = self.now(first)
        own = jnp.where(self.even, pair, first)
        others = jnp.where(self.even, first, second)
        self.held["take", i] = self.last = arrange(self.core == 0, own, others)

    def load(self, bits):
        gate_weight = self.now(self.gate_weight)
        self.held["load", bits] = self.last = load(gate_weight, self.up_weight, self.seq ^ bits)

    def part(self, i, bits, got=None, kind=jnp.bfloat16, split=False):
        some = self.now(self.held["take", i])
        result = sums(some, self.held["load", bits], got, kind, split)
        self.last = result[0] if split else result
        return result

    def a(self, i):
        self.held["a", i] = over_seq(self.part(i, 3), 1)

    def c(self, i):
        self.held["c", i] = over_seq(self.part(i, 1), 1)

    def b(self, i):
        both = self.part(i, 2, self.held["a", i], split=True)
        self.held["b", i] = over_seq(both[0], 2), over_seq(both[1], 2)

    def d(self, i):
        self.held["d", i] = self.part(i, 0, self.held["c", i], jnp.float32)

    def hide(self, i):
        hidden = hide(self.held["d", i], *(self.now(got) for got in self.held["b", i]))
        far = over_seq(hidden, 2)
        self.held["hide", i] = hidden, far, over_seq(hidden, 1)
        self.last = hidden

    def down(self, bits):
        quarters = [self.seq ^ bits, self.seq ^ bits ^ 1]
        self.held["down", bits] = self.last = load_rows(self.now(self.down_weight), quarters)

    def own(self, i):
        hidden, far, near = self.held["hide", i]
        self.held["own", i] = self.last = products((self.now(hidden), near), self.held["down", 0])

    def forward(self, i):
        far = self.now(self.held["hide", i][1])
        self.held["pass", i] = far, over_seq(far, 1)

    def rest(self, i):
        far, last = self.held["pass", i]
        self.held["rest", i] = self.last = products((self.now(far), last), self.held["down", 2], self.held["own", i])

    def out(self, i):
        partial_sum = self.now(self.held["rest", i])
        half = partial_sum.shape[0] // 2
        low, top = partial_sum[:half], partial_sum[half:]
        own = jnp.where(self.core == 0, low, top)
        others = jnp.where(self.core == 0, top, low)
        one, two = narrow(jnp.where(self.even, others, own)), narrow(others)
        self.held["out", i] = own, over_both(one, FIRST_OUT), over_both(two, SECOND)
        self.last = one

    def mix(self, i):
        own, first, second = self.held["out", i]
        pair = wide(self.now(first)) + jnp.where(self.even, own, wide(second))
        rows = pair.shape[0] // 2
        low, top = pair[:rows], pair[rows:]
        kept = jnp.where(self.x == 0, low, top)
        sent = narrow(jnp.where(self.x == 0, top, low))
        self.held["mix", i] = kept, over_seq(sent, 2)
        self.last = sent

    def far_out(self, i):
        kept, got = self.held["mix", i]
        got = self.now(got)
        sent = jnp.where(self.high == self.x, got, narrow(kept))
        kept = jnp.where(self.high == self.x, kept, wide(got))
        self.held["far_out", i] = kept, over_tp(sent, 2)
        self.last = sent

    def end(self, i):
        kept, got = self.held["far_out", i]
        before = [self.held["end", k] for k in range(i)] if i == len(ROWS) - 1 else ()
        self.held["end", i] = end(kept, self.now(got), before)
        self.last = self.held["end", i][0]


def four_shards(*arrays):
    return Steps(*arrays).run(ORDER)


def solution(mesh):
    placed = (
        P(("groups", "seq"), "tp"),
        P(("groups", "seq"), "tp"),
        P("seq", "tp"),
        P("seq", "tp"),
        P("tp", "seq"),
    )
    fours = mesh.shape["tp"] == 4 and mesh.shape["seq"] == 4
    return jax.shard_map(
        four_shards if fours else any_shards,
        mesh=mesh,
        in_specs=placed,
        out_specs=(P(("groups", "seq"), "tp"), P(("groups", "seq"), "tp")),
        check_vma=False,
    )
```

```python
import functools

import jax
import jax.numpy as jnp
from jax import lax
from jax.experimental import pallas as pl
from jax.experimental.pallas import tpu as pltpu
from jax.sharding import PartitionSpec as P

ROWS = (32, 48, 48)
ORDER = (
    "far0", "load3", "load1", "sel0", "far1", "load2", "arr0", "load0", "sel1", "far2", "take0", "a0", "c0",
    "arr1", "b0", "d0", "sel2", "take1", "a1", "c1", "b1", "arr2", "d1", "hide0", "take2", "a2", "c2", "b2",
    "d2", "down0", "own0", "forward0", "down2", "rest0", "out0", "hide1", "mix0", "hide2", "far_out0", "own1",
    "forward1", "own2", "rest1", "out1", "forward2", "end0", "rest2", "out2", "mix1", "mix2", "far_out1",
    "far_out2", "end1", "end2",
)
TILE = 256
COST = 1 << 34
LOAD_COST = 1 << 30
VMEM = 10 << 20


def blocks(array):
    return array.reshape(array.shape[0], array.shape[1] // 128, 128)


def block_scale(array):
    return jnp.max(jnp.abs(blocks(array)), axis=2) + 1e-06


def expand(values, scales):
    return (blocks(values.astype(jnp.float32)) * scales[:, :, None]).reshape(values.shape)


def scaled(total):
    scales = block_scale(total)
    values = (blocks(total) / scales[:, :, None]).reshape(total.shape).astype(jnp.bfloat16)
    return values, scales


def wide(array):
    return array.astype(jnp.float32)


def narrow(array):
    return array.astype(jnp.bfloat16)


def dot(a, b):
    return jnp.dot(a, b, preferred_element_type=jnp.float32)


def any_shards(tokens_values, tokens_scales, gate_weight, up_weight, down_weight):
    mine = narrow(expand(tokens_values, tokens_scales))
    mine = lax.all_gather(mine, "tp", axis=1, tiled=True)
    inputs = lax.all_to_all(mine, "seq", split_axis=1, concat_axis=0, tiled=True)
    gate = narrow(dot(inputs, gate_weight))
    up = narrow(dot(inputs, up_weight))
    gate = wide(lax.psum_scatter(gate, "seq", scatter_dimension=0, tiled=True))
    up = wide(lax.psum_scatter(up, "seq", scatter_dimension=0, tiled=True))
    hidden = narrow(jax.nn.silu(gate) * up)
    hidden = lax.all_gather(hidden, "seq", axis=0, tiled=True)
    partial_sum = narrow(dot(hidden, down_weight))
    partial_sum = lax.all_to_all(partial_sum, "seq", split_axis=0, concat_axis=1, tiled=True)
    return scaled(wide(lax.psum_scatter(partial_sum, "tp", scatter_dimension=1, tiled=True)))


def over_seq(array, bit):
    return lax.ppermute(array, "seq", [(i, i ^ bit) for i in range(4)])


def over_tp(array, bit):
    return lax.ppermute(array, "tp", [(i, i ^ bit) for i in range(4)])


def device(tp, seq):
    return tp * 4 + seq


FIRST_IN, SECOND, FIRST_OUT = [], [], []
for tp in range(4):
    for seq in range(4):
        if (tp ^ seq) & 1:
            FIRST_IN.append((device(tp, seq), device(tp, seq ^ 1)))
            SECOND.append((device(tp, seq), device(tp ^ 1, seq ^ 1)))
            FIRST_OUT.append((device(tp, seq), device(tp ^ 1, seq)))
        else:
            FIRST_IN.append((device(tp, seq), device(tp ^ 1, seq)))
            FIRST_OUT.append((device(tp, seq), device(tp, seq ^ 1)))


def over_both(array, pairs):
    return lax.ppermute(array, ("tp", "seq"), pairs)


def arrange(low_first, one, other):
    return jnp.concatenate([jnp.where(low_first, one, other), jnp.where(low_first, other, one)], axis=0)


def load_kernel(quarter, gate_weight, up_weight, out, done):
    width = out.shape[2]
    here = pl.ds(pl.multiple_of(quarter[0] * width, width), width)
    pieces = done.shape[1]
    rows = out.shape[1] // pieces
    copies = [
        pltpu.make_async_copy(weight.at[pl.ds(i * rows, rows), here], out.at[k, pl.ds(i * rows, rows)], done.at[k, i])
        for k, weight in enumerate((gate_weight, up_weight))
        for i in range(pieces)
    ]
    for copy in copies:
        copy.start()
    for copy in copies:
        copy.wait()


def load(gate_weight, up_weight, quarter):
    deep, width = gate_weight.shape
    far = pl.BlockSpec(memory_space=pl.ANY)
    return pl.pallas_call(
        load_kernel,
        out_shape=jax.ShapeDtypeStruct((2, deep, width // 4), gate_weight.dtype),
        in_specs=[pl.BlockSpec(memory_space=pltpu.SMEM), far, far],
        out_specs=pl.BlockSpec(memory_space=pltpu.VMEM),
        scratch_shapes=[pltpu.SemaphoreType.DMA((2, 4))],
        compiler_params=pltpu.CompilerParams(vmem_limit_bytes=VMEM),
        cost_estimate=pl.CostEstimate(flops=LOAD_COST, bytes_accessed=1, transcendentals=0),
    )(quarter.reshape(1).astype(jnp.int32), gate_weight, up_weight)


def sums_kernel(has_got, split, some, weights, *rest):
    def value(k):
        product = dot(some[...], weights[k])
        return product + wide(rest[0][k]) if has_got else product

    if split:
        for k, out in enumerate(rest[-2:]):
            out[...] = value(k).astype(out.dtype)
    else:

        @pl.loop(0, 2)
        def side(k):
            rest[-1][k] = value(k).astype(rest[-1].dtype)


def sums(some, weights, got=None, kind=jnp.bfloat16, split=False):
    near = pl.BlockSpec(memory_space=pltpu.VMEM)
    shape = some.shape[0], weights.shape[2]
    return pl.pallas_call(
        functools.partial(sums_kernel, got is not None, split),
        out_shape=(jax.ShapeDtypeStruct(shape, kind),) * 2 if split else jax.ShapeDtypeStruct((2,) + shape, kind),
        in_specs=[near] * (2 + (got is not None)),
        out_specs=(near, near) if split else near,
        compiler_params=pltpu.CompilerParams(vmem_limit_bytes=VMEM),
        cost_estimate=pl.CostEstimate(flops=COST, bytes_accessed=1, transcendentals=0),
    )(some, weights, *([] if got is None else [got]))


def load_rows_kernel(quarters, weight, out, done):
    rows = out.shape[1]
    pieces = done.shape[1]
    part = rows // pieces
    copies = [
        pltpu.make_async_copy(
            weight.at[pl.ds(pl.multiple_of(quarters[k] * rows + i * part, part), part)],
            out.at[k, pl.ds(i * part, part)],
            done.at[k, i],
        )
        for k in range(2)
        for i in range(pieces)
    ]
    for copy in copies:
        copy.start()
    for copy in copies:
        copy.wait()


def load_rows(weight, quarters):
    deep, width = weight.shape
    return pl.pallas_call(
        load_rows_kernel,
        out_shape=jax.ShapeDtypeStruct((2, deep // 4, width), weight.dtype),
        in_specs=[pl.BlockSpec(memory_space=pltpu.SMEM), pl.BlockSpec(memory_space=pl.ANY)],
        out_specs=pl.BlockSpec(memory_space=pltpu.VMEM),
        scratch_shapes=[pltpu.SemaphoreType.DMA((2, 4))],
        compiler_params=pltpu.CompilerParams(vmem_limit_bytes=VMEM),
        cost_estimate=pl.CostEstimate(flops=COST, bytes_accessed=1, transcendentals=0),
    )(jnp.stack(quarters).astype(jnp.int32), weight)


def products_kernel(has_total, one, two, weights, *rest):
    tile = 4 * TILE

    @pl.loop(0, weights.shape[2] // tile)
    def strip(j):
        here = pl.ds(pl.multiple_of(j * tile, tile), tile)
        value = dot(one[...], weights[0, :, here]) + dot(two[...], weights[1, :, here])
        rest[-1][:, here] = value + rest[0][:, here] if has_total else value


def products(pieces, weights, total=None):
    near = pl.BlockSpec(memory_space=pltpu.VMEM)
    return pl.pallas_call(
        functools.partial(products_kernel, total is not None),
        out_shape=jax.ShapeDtypeStruct((pieces[0].shape[0], weights.shape[2]), jnp.float32),
        in_specs=[near] * (3 + (total is not None)),
        out_specs=near,
        compiler_params=pltpu.CompilerParams(vmem_limit_bytes=VMEM),
        cost_estimate=pl.CostEstimate(flops=COST, bytes_accessed=1, transcendentals=0),
    )(*pieces, weights, *([] if total is None else [total]))


def begin_kernel(starts, values, turned_scales, *outs):
    scales = turned_scales[...].T
    for j in range(scales.shape[1]):
        here = pl.ds(j * 128, 128)
        scaled_values = narrow(wide(values[:, here]) * scales[:, j : j + 1])
        for i, out in enumerate(outs):
            out[:, here] = scaled_values[starts[i] : starts[i + 1]]


def begin(values, scales, starts):
    near = pl.BlockSpec(memory_space=pltpu.VMEM)
    count = len(starts) - 1
    return pl.pallas_call(
        functools.partial(begin_kernel, starts),
        out_shape=[jax.ShapeDtypeStruct((starts[i + 1] - starts[i], values.shape[1]), values.dtype) for i in range(count)],
        in_specs=[near] * 2,
        out_specs=[near] * count,
        compiler_params=pltpu.CompilerParams(vmem_limit_bytes=VMEM),
        cost_estimate=pl.CostEstimate(flops=LOAD_COST, bytes_accessed=1, transcendentals=0),
    )(values, scales.T)


def hide_kernel(held, got_gate, got_up, out):
    rows = 32

    @pl.loop(0, out.shape[0] // rows)
    def strip(i):
        here = pl.ds(pl.multiple_of(i * rows, rows), rows)
        gate = held[0, here] + wide(got_gate[here])
        up = held[1, here] + wide(got_up[here])
        out[here] = narrow(jax.nn.silu(gate) * up)


def hide(held, got_gate, got_up):
    near = pl.BlockSpec(memory_space=pltpu.VMEM)
    return pl.pallas_call(
        hide_kernel,
        out_shape=jax.ShapeDtypeStruct(held.shape[1:], got_up.dtype),
        in_specs=[near] * 3,
        out_specs=near,
        compiler_params=pltpu.CompilerParams(vmem_limit_bytes=VMEM),
        cost_estimate=pl.CostEstimate(flops=COST, bytes_accessed=1, transcendentals=0),
    )(held, got_gate, got_up)


def end_kernel(count, kept, got, *rest):
    before, (values, scales) = rest[: 2 * count], rest[2 * count :]
    first = sum(part.shape[0] for part in before[::2])
    rows = pl.ds(first, kept.shape[0])
    columns = []
    for j in range(kept.shape[1] // 128):
        here = pl.ds(j * 128, 128)
        total = kept[:, here] + wide(got[:, here])
        scale = jnp.max(jnp.abs(total), axis=1, keepdims=True) + 1e-06
        values[rows, here] = narrow(total / scale)
        columns.append(scale)
    ended = jnp.concatenate(columns, axis=1)
    if not count:
        scales[...] = ended
        return
    row = 0
    for part in before[::2]:
        values[pl.ds(row, part.shape[0])] = part[...]
        row += part.shape[0]
    scales[...] = jnp.concatenate([part[...] for part in before[1::2]] + [ended], axis=0).T


def end(kept, got, before=()):
    rows, width = kept.shape
    count = len(before)
    rows += sum(values.shape[0] for values, scales in before)
    near = pl.BlockSpec(memory_space=pltpu.VMEM)
    shape = (width // 128, rows) if count else (rows, width // 128)
    return pl.pallas_call(
        functools.partial(end_kernel, count),
        out_shape=(jax.ShapeDtypeStruct((rows, width), got.dtype), jax.ShapeDtypeStruct(shape, kept.dtype)),
        in_specs=[near] * (2 + 2 * count),
        out_specs=(near, near),
        compiler_params=pltpu.CompilerParams(vmem_limit_bytes=VMEM),
        cost_estimate=pl.CostEstimate(flops=COST, bytes_accessed=1, transcendentals=0),
    )(kept, got, *(array for pair in before for array in pair))


class Steps:

    def __init__(self, tokens_values, tokens_scales, gate_weight, up_weight, down_weight):
        tp, seq = lax.axis_index("tp"), lax.axis_index("seq")
        self.seq, self.x, self.core = seq, seq >> 1, seq & 1
        self.high, self.even = tp >> 1, (tp ^ seq) & 1 == 0
        self.gate_weight = pltpu.with_memory_space_constraint(gate_weight, pltpu.HBM)
        self.up_weight = pltpu.with_memory_space_constraint(up_weight, pltpu.HBM)
        self.down_weight = pltpu.with_memory_space_constraint(down_weight, pltpu.HBM)
        unit = tokens_values.shape[0] // sum(ROWS)
        self.mine = begin(tokens_values, tokens_scales, [sum(ROWS[:i]) * unit for i in range(len(ROWS) + 1)])
        self.last = self.mine[0]
        self.held = {}

    def run(self, order):
        for step in order:
            with jax.named_scope(step):
                getattr(self, step[:-1])(int(step[-1]))
        values, scales = self.held["end", len(ROWS) - 1]
        return values, scales.T

    def now(self, array):
        return lax.optimization_barrier((array, self.last))[0]

    def far(self, i):
        part = self.now(self.mine[i])
        self.held["far", i] = part, over_tp(part, 2)

    def sel(self, i):
        part, other = self.held["far", i]
        other = self.now(other)
        sent = jnp.where(self.high == self.x, other, part)
        kept = jnp.where(self.high == self.x, part, other)
        self.held["sel", i] = kept, over_seq(sent, 2)
        self.last = sent

    def arr(self, i):
        kept, got = self.held["sel", i]
        pair = arrange(self.x == 0, kept, self.now(got))
        self.held["arr", i] = pair, over_both(pair, FIRST_IN), over_both(pair, SECOND)
        self.last = pair

    def take(self, i):
        pair, first, second = self.held["arr", i]
        first = self.now(first)
        own = jnp.where(self.even, pair, first)
        others = jnp.where(self.even, first, second)
        self.held["take", i] = self.last = arrange(self.core == 0, own, others)

    def load(self, bits):
        gate_weight = self.now(self.gate_weight)
        self.held["load", bits] = self.last = load(gate_weight, self.up_weight, self.seq ^ bits)

    def part(self, i, bits, got=None, kind=jnp.bfloat16, split=False):
        some = self.now(self.held["take", i])
        result = sums(some, self.held["load", bits], got, kind, split)
        self.last = result[0] if split else result
        return result

    def a(self, i):
        self.held["a", i] = over_seq(self.part(i, 3), 1)

    def c(self, i):
        self.held["c", i] = over_seq(self.part(i, 1), 1)

    def b(self, i):
        both = self.part(i, 2, self.held["a", i], split=True)
        self.held["b", i] = over_seq(both[0], 2), over_seq(both[1], 2)

    def d(self, i):
        self.held["d", i] = self.part(i, 0, self.held["c", i], jnp.float32)

    def hide(self, i):
        hidden = hide(self.held["d", i], *(self.now(got) for got in self.held["b", i]))
        far = over_seq(hidden, 2)
        self.held["hide", i] = hidden, far, over_seq(hidden, 1)
        self.last = hidden

    def down(self, bits):
        quarters = [self.seq ^ bits, self.seq ^ bits ^ 1]
        self.held["down", bits] = self.last = load_rows(self.now(self.down_weight), quarters)

    def own(self, i):
        hidden, far, near = self.held["hide", i]
        self.held["own", i] = self.last = products((self.now(hidden), near), self.held["down", 0])

    def forward(self, i):
        far = self.now(self.held["hide", i][1])
        self.held["pass", i] = far, over_seq(far, 1)

    def rest(self, i):
        far, last = self.held["pass", i]
        self.held["rest", i] = self.last = products((self.now(far), last), self.held["down", 2], self.held["own", i])

    def out(self, i):
        partial_sum = self.now(self.held["rest", i])
        half = partial_sum.shape[0] // 2
        low, top = partial_sum[:half], partial_sum[half:]
        own = jnp.where(self.core == 0, low, top)
        others = jnp.where(self.core == 0, top, low)
        one, two = narrow(jnp.where(self.even, others, own)), narrow(others)
        self.held["out", i] = own, over_both(one, FIRST_OUT), over_both(two, SECOND)
        self.last = one

    def mix(self, i):
        own, first, second = self.held["out", i]
        pair = wide(self.now(first)) + jnp.where(self.even, own, wide(second))
        rows = pair.shape[0] // 2
        low, top = pair[:rows], pair[rows:]
        kept = jnp.where(self.x == 0, low, top)
        sent = narrow(jnp.where(self.x == 0, top, low))
        self.held["mix", i] = kept, over_seq(sent, 2)
        self.last = sent

    def far_out(self, i):
        kept, got = self.held["mix", i]
        got = self.now(got)
        sent = jnp.where(self.high == self.x, got, narrow(kept))
        kept = jnp.where(self.high == self.x, kept, wide(got))
        self.held["far_out", i] = kept, over_tp(sent, 2)
        self.last = sent

    def end(self, i):
        kept, got = self.held["far_out", i]
        before = [self.held["end", k] for k in range(i)] if i == len(ROWS) - 1 else ()
        self.held["end", i] = end(kept, self.now(got), before)
        self.last = self.held["end", i][0]


def four_shards(*arrays):
    return Steps(*arrays).run(ORDER)


def solution(mesh):
    placed = (
        P(("groups", "seq"), "tp"),
        P(("groups", "seq"), "tp"),
        P("seq", "tp"),
        P("seq", "tp"),
        P("tp", "seq"),
    )
    fours = mesh.shape["tp"] == 4 and mesh.shape["seq"] == 4
    return jax.shard_map(
        four_shards if fours else any_shards,
        mesh=mesh,
        in_specs=placed,
        out_specs=(P(("groups", "seq"), "tp"), P(("groups", "seq"), "tp")),
        check_vma=False,
    )
```

```python
import functools

import jax
import jax.numpy as jnp
from jax import lax
from jax.experimental import pallas as pl
from jax.experimental.pallas import tpu as pltpu
from jax.sharding import PartitionSpec as P

ROWS = (32, 48, 48)
ORDER = (
    "far0", "load3", "sel0", "far1", "load1", "arr0", "load2", "load0", "sel1", "far2", "take0", "a0", "c0",
    "arr1", "b0", "d0", "sel2", "take1", "a1", "c1", "b1", "arr2", "d1", "hide0", "take2", "a2", "c2", "b2",
    "d2", "down0", "own0", "forward0", "down2", "rest0", "out0", "hide1", "mix0", "hide2", "far_out0", "own1",
    "forward1", "own2", "rest1", "out1", "forward2", "end0", "rest2", "out2", "mix1", "mix2", "far_out1",
    "far_out2", "end1", "end2",
)
TILE = 256
COST = 1 << 34
LOAD_COST = 1 << 30
VMEM = 6 << 20


def blocks(array):
    return array.reshape(array.shape[0], array.shape[1] // 128, 128)


def block_scale(array):
    return jnp.max(jnp.abs(blocks(array)), axis=2) + 1e-06


def expand(values, scales):
    return (blocks(values.astype(jnp.float32)) * scales[:, :, None]).reshape(values.shape)


def scaled(total):
    scales = block_scale(total)
    values = (blocks(total) / scales[:, :, None]).reshape(total.shape).astype(jnp.bfloat16)
    return values, scales


def wide(array):
    return array.astype(jnp.float32)


def narrow(array):
    return array.astype(jnp.bfloat16)


def dot(a, b):
    return jnp.dot(a, b, preferred_element_type=jnp.float32)


def any_shards(tokens_values, tokens_scales, gate_weight, up_weight, down_weight):
    mine = narrow(expand(tokens_values, tokens_scales))
    mine = lax.all_gather(mine, "tp", axis=1, tiled=True)
    inputs = lax.all_to_all(mine, "seq", split_axis=1, concat_axis=0, tiled=True)
    gate = narrow(dot(inputs, gate_weight))
    up = narrow(dot(inputs, up_weight))
    gate = wide(lax.psum_scatter(gate, "seq", scatter_dimension=0, tiled=True))
    up = wide(lax.psum_scatter(up, "seq", scatter_dimension=0, tiled=True))
    hidden = narrow(jax.nn.silu(gate) * up)
    hidden = lax.all_gather(hidden, "seq", axis=0, tiled=True)
    partial_sum = narrow(dot(hidden, down_weight))
    partial_sum = lax.all_to_all(partial_sum, "seq", split_axis=0, concat_axis=1, tiled=True)
    return scaled(wide(lax.psum_scatter(partial_sum, "tp", scatter_dimension=1, tiled=True)))


def over_seq(array, bit):
    return lax.ppermute(array, "seq", [(i, i ^ bit) for i in range(4)])


def over_tp(array, bit):
    return lax.ppermute(array, "tp", [(i, i ^ bit) for i in range(4)])


def device(tp, seq):
    return tp * 4 + seq


FIRST_IN, SECOND, FIRST_OUT = [], [], []
for tp in range(4):
    for seq in range(4):
        if (tp ^ seq) & 1:
            FIRST_IN.append((device(tp, seq), device(tp, seq ^ 1)))
            SECOND.append((device(tp, seq), device(tp ^ 1, seq ^ 1)))
            FIRST_OUT.append((device(tp, seq), device(tp ^ 1, seq)))
        else:
            FIRST_IN.append((device(tp, seq), device(tp ^ 1, seq)))
            FIRST_OUT.append((device(tp, seq), device(tp, seq ^ 1)))


def over_both(array, pairs):
    return lax.ppermute(array, ("tp", "seq"), pairs)


def arrange(low_first, one, other):
    return jnp.concatenate([jnp.where(low_first, one, other), jnp.where(low_first, other, one)], axis=0)


def load_kernel(quarter, gate_weight, up_weight, out, done):
    width = out.shape[2]
    here = pl.ds(pl.multiple_of(quarter[0] * width, width), width)
    pieces = done.shape[1]
    rows = out.shape[1] // pieces
    copies = [
        pltpu.make_async_copy(weight.at[pl.ds(i * rows, rows), here], out.at[k, pl.ds(i * rows, rows)], done.at[k, i])
        for k, weight in enumerate((gate_weight, up_weight))
        for i in range(pieces)
    ]
    for copy in copies:
        copy.start()
    for copy in copies:
        copy.wait()


def load(gate_weight, up_weight, quarter):
    deep, width = gate_weight.shape
    far = pl.BlockSpec(memory_space=pl.ANY)
    return pl.pallas_call(
        load_kernel,
        out_shape=jax.ShapeDtypeStruct((2, deep, width // 4), gate_weight.dtype),
        in_specs=[pl.BlockSpec(memory_space=pltpu.SMEM), far, far],
        out_specs=pl.BlockSpec(memory_space=pltpu.VMEM),
        scratch_shapes=[pltpu.SemaphoreType.DMA((2, 4))],
        compiler_params=pltpu.CompilerParams(vmem_limit_bytes=VMEM),
        cost_estimate=pl.CostEstimate(flops=LOAD_COST, bytes_accessed=1, transcendentals=0),
    )(quarter, gate_weight, up_weight)


def sums_kernel(has_got, split, some, weights, *rest):
    def value(k):
        product = dot(some[...], weights[k])
        return product + wide(rest[0][k]) if has_got else product

    if split:
        for k, out in enumerate(rest[-2:]):
            out[...] = value(k).astype(out.dtype)
    else:

        @pl.loop(0, 2)
        def side(k):
            rest[-1][k] = value(k).astype(rest[-1].dtype)


def sums(some, weights, got=None, kind=jnp.bfloat16, split=False):
    near = pl.BlockSpec(memory_space=pltpu.VMEM)
    shape = some.shape[0], weights.shape[2]
    return pl.pallas_call(
        functools.partial(sums_kernel, got is not None, split),
        out_shape=(jax.ShapeDtypeStruct(shape, kind),) * 2 if split else jax.ShapeDtypeStruct((2,) + shape, kind),
        in_specs=[near] * (2 + (got is not None)),
        out_specs=(near, near) if split else near,
        compiler_params=pltpu.CompilerParams(vmem_limit_bytes=VMEM),
        cost_estimate=pl.CostEstimate(flops=COST, bytes_accessed=1, transcendentals=0),
    )(some, weights, *([] if got is None else [got]))


def load_rows_kernel(quarters, weight, out, done):
    rows = out.shape[1]
    pieces = done.shape[1]
    part = rows // pieces
    copies = [
        pltpu.make_async_copy(
            weight.at[pl.ds(pl.multiple_of(quarters[k] * rows + i * part, part), part)],
            out.at[k, pl.ds(i * part, part)],
            done.at[k, i],
        )
        for k in range(2)
        for i in range(pieces)
    ]
    for copy in copies:
        copy.start()
    for copy in copies:
        copy.wait()


def load_rows(weight, quarters):
    deep, width = weight.shape
    return pl.pallas_call(
        load_rows_kernel,
        out_shape=jax.ShapeDtypeStruct((2, deep // 4, width), weight.dtype),
        in_specs=[pl.BlockSpec(memory_space=pltpu.SMEM), pl.BlockSpec(memory_space=pl.ANY)],
        out_specs=pl.BlockSpec(memory_space=pltpu.VMEM),
        scratch_shapes=[pltpu.SemaphoreType.DMA((2, 4))],
        compiler_params=pltpu.CompilerParams(vmem_limit_bytes=VMEM),
        cost_estimate=pl.CostEstimate(flops=COST, bytes_accessed=1, transcendentals=0),
    )(quarters, weight)


def products_kernel(has_total, one, two, weights, *rest):
    tile = 4 * TILE

    @pl.loop(0, weights.shape[2] // tile)
    def strip(j):
        here = pl.ds(pl.multiple_of(j * tile, tile), tile)
        value = dot(one[...], weights[0, :, here]) + dot(two[...], weights[1, :, here])
        rest[-1][:, here] = value + rest[0][:, here] if has_total else value


def products(pieces, weights, total=None):
    near = pl.BlockSpec(memory_space=pltpu.VMEM)
    return pl.pallas_call(
        functools.partial(products_kernel, total is not None),
        out_shape=jax.ShapeDtypeStruct((pieces[0].shape[0], weights.shape[2]), jnp.float32),
        in_specs=[near] * (3 + (total is not None)),
        out_specs=near,
        compiler_params=pltpu.CompilerParams(vmem_limit_bytes=VMEM),
        cost_estimate=pl.CostEstimate(flops=COST, bytes_accessed=1, transcendentals=0),
    )(*pieces, weights, *([] if total is None else [total]))


def begin_kernel(starts, values, turned_scales, *outs):
    scales = turned_scales[...].T
    for j in range(scales.shape[1]):
        here = pl.ds(j * 128, 128)
        scaled_values = narrow(wide(values[:, here]) * scales[:, j : j + 1])
        for i, out in enumerate(outs):
            out[:, here] = scaled_values[starts[i] : starts[i + 1]]


def begin(values, scales, starts):
    near = pl.BlockSpec(memory_space=pltpu.VMEM)
    count = len(starts) - 1
    return pl.pallas_call(
        functools.partial(begin_kernel, starts),
        out_shape=[jax.ShapeDtypeStruct((starts[i + 1] - starts[i], values.shape[1]), values.dtype) for i in range(count)],
        in_specs=[near] * 2,
        out_specs=[near] * count,
        compiler_params=pltpu.CompilerParams(vmem_limit_bytes=VMEM),
        cost_estimate=pl.CostEstimate(flops=LOAD_COST, bytes_accessed=1, transcendentals=0),
    )(values, scales.T)


def hide_kernel(held, got_gate, got_up, out):
    rows = 32

    @pl.loop(0, out.shape[0] // rows)
    def strip(i):
        here = pl.ds(pl.multiple_of(i * rows, rows), rows)
        gate = held[0, here] + wide(got_gate[here])
        up = held[1, here] + wide(got_up[here])
        out[here] = narrow(jax.nn.silu(gate) * up)


def hide(held, got_gate, got_up):
    near = pl.BlockSpec(memory_space=pltpu.VMEM)
    return pl.pallas_call(
        hide_kernel,
        out_shape=jax.ShapeDtypeStruct(held.shape[1:], got_up.dtype),
        in_specs=[near] * 3,
        out_specs=near,
        compiler_params=pltpu.CompilerParams(vmem_limit_bytes=VMEM),
        cost_estimate=pl.CostEstimate(flops=COST, bytes_accessed=1, transcendentals=0),
    )(held, got_gate, got_up)


def end_kernel(count, kept, got, *rest):
    before, (values, scales) = rest[: 2 * count], rest[2 * count :]
    first = sum(part.shape[0] for part in before[::2])
    rows = pl.ds(first, kept.shape[0])
    columns = []
    for j in range(kept.shape[1] // 128):
        here = pl.ds(j * 128, 128)
        total = kept[:, here] + wide(got[:, here])
        scale = jnp.max(jnp.abs(total), axis=1, keepdims=True) + 1e-06
        values[rows, here] = narrow(total / scale)
        columns.append(scale)
    ended = jnp.concatenate(columns, axis=1)
    if not count:
        scales[...] = ended
        return
    row = 0
    for part in before[::2]:
        values[pl.ds(row, part.shape[0])] = part[...]
        row += part.shape[0]
    scales[...] = jnp.concatenate([part[...] for part in before[1::2]] + [ended], axis=0).T


def end(kept, got, before=()):
    rows, width = kept.shape
    count = len(before)
    rows += sum(values.shape[0] for values, scales in before)
    near = pl.BlockSpec(memory_space=pltpu.VMEM)
    shape = (width // 128, rows) if count else (rows, width // 128)
    return pl.pallas_call(
        functools.partial(end_kernel, count),
        out_shape=(jax.ShapeDtypeStruct((rows, width), got.dtype), jax.ShapeDtypeStruct(shape, kept.dtype)),
        in_specs=[near] * (2 + 2 * count),
        out_specs=(near, near),
        compiler_params=pltpu.CompilerParams(vmem_limit_bytes=VMEM),
        cost_estimate=pl.CostEstimate(flops=COST, bytes_accessed=1, transcendentals=0),
    )(kept, got, *(array for pair in before for array in pair))


class Steps:

    def __init__(self, tokens_values, tokens_scales, gate_weight, up_weight, down_weight):
        tp, seq = lax.axis_index("tp"), lax.axis_index("seq")
        x, core, high = seq >> 1, seq & 1, tp >> 1
        facts = x == 0, core == 0, (tp ^ seq) & 1 == 0, high == x
        quarters = [(seq ^ bits).reshape(1) for bits in range(4)]
        pairs = [jnp.stack([seq ^ bits, seq ^ bits ^ 1]) for bits in (0, 2)]
        facts, self.quarters, self.pairs, gate_weight = lax.optimization_barrier((facts, quarters, pairs, gate_weight))
        self.first_x, self.first_core, self.even, self.same_half = facts
        self.gate_weight = pltpu.with_memory_space_constraint(gate_weight, pltpu.HBM)
        self.up_weight = pltpu.with_memory_space_constraint(up_weight, pltpu.HBM)
        self.down_weight = pltpu.with_memory_space_constraint(down_weight, pltpu.HBM)
        unit = tokens_values.shape[0] // sum(ROWS)
        self.mine = begin(tokens_values, tokens_scales, [sum(ROWS[:i]) * unit for i in range(len(ROWS) + 1)])
        self.last = self.mine[0]
        self.held = {}

    def run(self, order):
        for step in order:
            with jax.named_scope(step):
                getattr(self, step[:-1])(int(step[-1]))
        values, scales = self.held["end", len(ROWS) - 1]
        return values, scales.T

    def now(self, array):
        return lax.optimization_barrier((array, self.last))[0]

    def far(self, i):
        part = self.now(self.mine[i])
        self.held["far", i] = part, over_tp(part, 2)

    def sel(self, i):
        part, other = self.held["far", i]
        other = self.now(other)
        sent = jnp.where(self.same_half, other, part)
        kept = jnp.where(self.same_half, part, other)
        self.held["sel", i] = kept, over_seq(sent, 2)
        self.last = sent

    def arr(self, i):
        kept, got = self.held["sel", i]
        pair = arrange(self.first_x, kept, self.now(got))
        self.held["arr", i] = pair, over_both(pair, FIRST_IN), over_both(pair, SECOND)
        self.last = pair

    def take(self, i):
        pair, first, second = self.held["arr", i]
        first = self.now(first)
        own = jnp.where(self.even, pair, first)
        others = jnp.where(self.even, first, second)
        self.held["take", i] = self.last = arrange(self.first_core, own, others)

    def load(self, bits):
        gate_weight = self.now(self.gate_weight)
        self.held["load", bits] = self.last = load(gate_weight, self.up_weight, self.quarters[bits])

    def part(self, i, bits, got=None, kind=jnp.bfloat16, split=False):
        some = self.now(self.held["take", i])
        result = sums(some, self.held["load", bits], got, kind, split)
        self.last = result[0] if split else result
        return result

    def a(self, i):
        self.held["a", i] = over_seq(self.part(i, 3), 1)

    def c(self, i):
        self.held["c", i] = over_seq(self.part(i, 1), 1)

    def b(self, i):
        both = self.part(i, 2, self.held["a", i], split=True)
        self.held["b", i] = over_seq(both[0], 2), over_seq(both[1], 2)

    def d(self, i):
        self.held["d", i] = self.part(i, 0, self.held["c", i], jnp.float32)

    def hide(self, i):
        hidden = hide(self.held["d", i], *(self.now(got) for got in self.held["b", i]))
        far = over_seq(hidden, 2)
        self.held["hide", i] = hidden, far, over_seq(hidden, 1)
        self.last = hidden

    def down(self, bits):
        self.held["down", bits] = self.last = load_rows(self.now(self.down_weight), self.pairs[bits // 2])

    def own(self, i):
        hidden, far, near = self.held["hide", i]
        self.held["own", i] = self.last = products((self.now(hidden), near), self.held["down", 0])

    def forward(self, i):
        far = self.now(self.held["hide", i][1])
        self.held["pass", i] = far, over_seq(far, 1)

    def rest(self, i):
        far, last = self.held["pass", i]
        self.held["rest", i] = self.last = products((self.now(far), last), self.held["down", 2], self.held["own", i])

    def out(self, i):
        partial_sum = self.now(self.held["rest", i])
        half = partial_sum.shape[0] // 2
        low, top = partial_sum[:half], partial_sum[half:]
        own = jnp.where(self.first_core, low, top)
        others = jnp.where(self.first_core, top, low)
        one, two = narrow(jnp.where(self.even, others, own)), narrow(others)
        self.held["out", i] = own, over_both(one, FIRST_OUT), over_both(two, SECOND)
        self.last = one

    def mix(self, i):
        own, first, second = self.held["out", i]
        pair = wide(self.now(first)) + jnp.where(self.even, own, wide(second))
        rows = pair.shape[0] // 2
        low, top = pair[:rows], pair[rows:]
        kept = jnp.where(self.first_x, low, top)
        sent = narrow(jnp.where(self.first_x, top, low))
        self.held["mix", i] = kept, over_seq(sent, 2)
        self.last = sent

    def far_out(self, i):
        kept, got = self.held["mix", i]
        got = self.now(got)
        sent = jnp.where(self.same_half, got, narrow(kept))
        kept = jnp.where(self.same_half, kept, wide(got))
        self.held["far_out", i] = kept, over_tp(sent, 2)
        self.last = sent

    def end(self, i):
        kept, got = self.held["far_out", i]
        before = [self.held["end", k] for k in range(i)] if i == len(ROWS) - 1 else ()
        self.held["end", i] = end(kept, self.now(got), before)
        self.last = self.held["end", i][0]


def four_shards(*arrays):
    return Steps(*arrays).run(ORDER)


def solution(mesh):
    placed = (
        P(("groups", "seq"), "tp"),
        P(("groups", "seq"), "tp"),
        P("seq", "tp"),
        P("seq", "tp"),
        P("tp", "seq"),
    )
    fours = mesh.shape["tp"] == 4 and mesh.shape["seq"] == 4
    return jax.shard_map(
        four_shards if fours else any_shards,
        mesh=mesh,
        in_specs=placed,
        out_specs=(P(("groups", "seq"), "tp"), P(("groups", "seq"), "tp")),
        check_vma=False,
    )
```

```python
import functools

import jax
import jax.numpy as jnp
from jax import lax
from jax.experimental import pallas as pl
from jax.experimental.pallas import tpu as pltpu
from jax.sharding import PartitionSpec as P

ROWS = (32, 64, 32)
ORDER = (
    "far0", "load3", "sel0", "far1", "load1", "arr0", "load2", "load0", "sel1", "far2", "take0", "a0", "c0",
    "b0", "arr1", "d0", "sel2", "take1", "a1", "c1", "b1", "d1", "hide0", "arr2", "take2", "a2", "c2",
    "down0", "forward0", "own0", "hide1", "b2", "d2", "down2", "rest0", "out0", "own1", "forward1", "hide2",
    "rest1", "out1", "mix0", "own2", "far_out0", "forward2", "mix1", "rest2", "out2", "end0", "mix2",
    "far_out1", "far_out2", "end1", "end2",
)
TILE = 256
COST = 1 << 34
LOAD_COST = 1 << 30
VMEM = 6 << 20


def blocks(array):
    return array.reshape(array.shape[0], array.shape[1] // 128, 128)


def block_scale(array):
    return jnp.max(jnp.abs(blocks(array)), axis=2) + 1e-06


def expand(values, scales):
    return (blocks(values.astype(jnp.float32)) * scales[:, :, None]).reshape(values.shape)


def scaled(total):
    scales = block_scale(total)
    values = (blocks(total) / scales[:, :, None]).reshape(total.shape).astype(jnp.bfloat16)
    return values, scales


def wide(array):
    return array.astype(jnp.float32)


def narrow(array):
    return array.astype(jnp.bfloat16)


def dot(a, b):
    return jnp.dot(a, b, preferred_element_type=jnp.float32)


def any_shards(tokens_values, tokens_scales, gate_weight, up_weight, down_weight):
    mine = narrow(expand(tokens_values, tokens_scales))
    mine = lax.all_gather(mine, "tp", axis=1, tiled=True)
    inputs = lax.all_to_all(mine, "seq", split_axis=1, concat_axis=0, tiled=True)
    gate = narrow(dot(inputs, gate_weight))
    up = narrow(dot(inputs, up_weight))
    gate = wide(lax.psum_scatter(gate, "seq", scatter_dimension=0, tiled=True))
    up = wide(lax.psum_scatter(up, "seq", scatter_dimension=0, tiled=True))
    hidden = narrow(jax.nn.silu(gate) * up)
    hidden = lax.all_gather(hidden, "seq", axis=0, tiled=True)
    partial_sum = narrow(dot(hidden, down_weight))
    partial_sum = lax.all_to_all(partial_sum, "seq", split_axis=0, concat_axis=1, tiled=True)
    return scaled(wide(lax.psum_scatter(partial_sum, "tp", scatter_dimension=1, tiled=True)))


def over_seq(array, bit):
    return lax.ppermute(array, "seq", [(i, i ^ bit) for i in range(4)])


def over_tp(array, bit):
    return lax.ppermute(array, "tp", [(i, i ^ bit) for i in range(4)])


def device(tp, seq):
    return tp * 4 + seq


FIRST_IN, SECOND, FIRST_OUT = [], [], []
for tp in range(4):
    for seq in range(4):
        if (tp ^ seq) & 1:
            FIRST_IN.append((device(tp, seq), device(tp, seq ^ 1)))
            SECOND.append((device(tp, seq), device(tp ^ 1, seq ^ 1)))
            FIRST_OUT.append((device(tp, seq), device(tp ^ 1, seq)))
        else:
            FIRST_IN.append((device(tp, seq), device(tp ^ 1, seq)))
            FIRST_OUT.append((device(tp, seq), device(tp, seq ^ 1)))


def over_both(array, pairs):
    return lax.ppermute(array, ("tp", "seq"), pairs)


def arrange(low_first, one, other):
    return jnp.concatenate([jnp.where(low_first, one, other), jnp.where(low_first, other, one)], axis=0)


def load_kernel(quarter, gate_weight, up_weight, out, done):
    width = out.shape[2]
    here = pl.ds(pl.multiple_of(quarter[0] * width, width), width)
    pieces = done.shape[1]
    rows = out.shape[1] // pieces
    copies = [
        pltpu.make_async_copy(weight.at[pl.ds(i * rows, rows), here], out.at[k, pl.ds(i * rows, rows)], done.at[k, i])
        for k, weight in enumerate((gate_weight, up_weight))
        for i in range(pieces)
    ]
    for copy in copies:
        copy.start()
    for copy in copies:
        copy.wait()


def load(gate_weight, up_weight, quarter):
    deep, width = gate_weight.shape
    far = pl.BlockSpec(memory_space=pl.ANY)
    return pl.pallas_call(
        load_kernel,
        out_shape=jax.ShapeDtypeStruct((2, deep, width // 4), gate_weight.dtype),
        in_specs=[pl.BlockSpec(memory_space=pltpu.SMEM), far, far],
        out_specs=pl.BlockSpec(memory_space=pltpu.VMEM),
        scratch_shapes=[pltpu.SemaphoreType.DMA((2, 4))],
        compiler_params=pltpu.CompilerParams(vmem_limit_bytes=VMEM),
        cost_estimate=pl.CostEstimate(flops=LOAD_COST, bytes_accessed=1, transcendentals=0),
    )(quarter, gate_weight, up_weight)


def sums_kernel(has_got, split, some, weights, *rest):
    def value(k):
        product = dot(some[...], weights[k])
        return product + wide(rest[0][k]) if has_got else product

    if split:
        for k, out in enumerate(rest[-2:]):
            out[...] = value(k).astype(out.dtype)
    else:

        @pl.loop(0, 2)
        def side(k):
            rest[-1][k] = value(k).astype(rest[-1].dtype)


def sums(some, weights, got=None, kind=jnp.bfloat16, split=False):
    near = pl.BlockSpec(memory_space=pltpu.VMEM)
    shape = some.shape[0], weights.shape[2]
    return pl.pallas_call(
        functools.partial(sums_kernel, got is not None, split),
        out_shape=(jax.ShapeDtypeStruct(shape, kind),) * 2 if split else jax.ShapeDtypeStruct((2,) + shape, kind),
        in_specs=[near] * (2 + (got is not None)),
        out_specs=(near, near) if split else near,
        compiler_params=pltpu.CompilerParams(vmem_limit_bytes=VMEM),
        cost_estimate=pl.CostEstimate(flops=COST, bytes_accessed=1, transcendentals=0),
    )(some, weights, *([] if got is None else [got]))


def load_rows_kernel(quarters, weight, out, done):
    rows = out.shape[1]
    pieces = done.shape[1]
    part = rows // pieces
    copies = [
        pltpu.make_async_copy(
            weight.at[pl.ds(pl.multiple_of(quarters[k] * rows + i * part, part), part)],
            out.at[k, pl.ds(i * part, part)],
            done.at[k, i],
        )
        for k in range(2)
        for i in range(pieces)
    ]
    for copy in copies:
        copy.start()
    for copy in copies:
        copy.wait()


def load_rows(weight, quarters):
    deep, width = weight.shape
    return pl.pallas_call(
        load_rows_kernel,
        out_shape=jax.ShapeDtypeStruct((2, deep // 4, width), weight.dtype),
        in_specs=[pl.BlockSpec(memory_space=pltpu.SMEM), pl.BlockSpec(memory_space=pl.ANY)],
        out_specs=pl.BlockSpec(memory_space=pltpu.VMEM),
        scratch_shapes=[pltpu.SemaphoreType.DMA((2, 4))],
        compiler_params=pltpu.CompilerParams(vmem_limit_bytes=VMEM),
        cost_estimate=pl.CostEstimate(flops=COST, bytes_accessed=1, transcendentals=0),
    )(quarters, weight)


def products_kernel(has_total, one, two, weights, *rest):
    tile = 4 * TILE

    @pl.loop(0, weights.shape[2] // tile)
    def strip(j):
        here = pl.ds(pl.multiple_of(j * tile, tile), tile)
        value = dot(one[...], weights[0, :, here]) + dot(two[...], weights[1, :, here])
        rest[-1][:, here] = value + rest[0][:, here] if has_total else value


def products(pieces, weights, total=None):
    near = pl.BlockSpec(memory_space=pltpu.VMEM)
    return pl.pallas_call(
        functools.partial(products_kernel, total is not None),
        out_shape=jax.ShapeDtypeStruct((pieces[0].shape[0], weights.shape[2]), jnp.float32),
        in_specs=[near] * (3 + (total is not None)),
        out_specs=near,
        compiler_params=pltpu.CompilerParams(vmem_limit_bytes=VMEM),
        cost_estimate=pl.CostEstimate(flops=COST, bytes_accessed=1, transcendentals=0),
    )(*pieces, weights, *([] if total is None else [total]))


def begin_kernel(starts, values, turned_scales, *outs):
    scales = turned_scales[...].T
    for j in range(scales.shape[1]):
        here = pl.ds(j * 128, 128)
        scaled_values = narrow(wide(values[:, here]) * scales[:, j : j + 1])
        for i, out in enumerate(outs):
            out[:, here] = scaled_values[starts[i] : starts[i + 1]]


def begin(values, scales, starts):
    near = pl.BlockSpec(memory_space=pltpu.VMEM)
    count = len(starts) - 1
    return pl.pallas_call(
        functools.partial(begin_kernel, starts),
        out_shape=[jax.ShapeDtypeStruct((starts[i + 1] - starts[i], values.shape[1]), values.dtype) for i in range(count)],
        in_specs=[near] * 2,
        out_specs=[near] * count,
        compiler_params=pltpu.CompilerParams(vmem_limit_bytes=VMEM),
        cost_estimate=pl.CostEstimate(flops=LOAD_COST, bytes_accessed=1, transcendentals=0),
    )(values, scales.T)


def hide_kernel(held, got_gate, got_up, out):
    rows = 32

    @pl.loop(0, out.shape[0] // rows)
    def strip(i):
        here = pl.ds(pl.multiple_of(i * rows, rows), rows)
        gate = held[0, here] + wide(got_gate[here])
        up = held[1, here] + wide(got_up[here])
        out[here] = narrow(jax.nn.silu(gate) * up)


def hide(held, got_gate, got_up):
    near = pl.BlockSpec(memory_space=pltpu.VMEM)
    return pl.pallas_call(
        hide_kernel,
        out_shape=jax.ShapeDtypeStruct(held.shape[1:], got_up.dtype),
        in_specs=[near] * 3,
        out_specs=near,
        compiler_params=pltpu.CompilerParams(vmem_limit_bytes=VMEM),
        cost_estimate=pl.CostEstimate(flops=COST, bytes_accessed=1, transcendentals=0),
    )(held, got_gate, got_up)


def end_kernel(count, kept, got, *rest):
    before, (values, scales) = rest[: 2 * count], rest[2 * count :]
    first = sum(part.shape[0] for part in before[::2])
    rows = pl.ds(first, kept.shape[0])
    columns = []
    for j in range(kept.shape[1] // 128):
        here = pl.ds(j * 128, 128)
        total = kept[:, here] + wide(got[:, here])
        scale = jnp.max(jnp.abs(total), axis=1, keepdims=True) + 1e-06
        values[rows, here] = narrow(total / scale)
        columns.append(scale)
    ended = jnp.concatenate(columns, axis=1)
    if not count:
        scales[...] = ended
        return
    row = 0
    for part in before[::2]:
        values[pl.ds(row, part.shape[0])] = part[...]
        row += part.shape[0]
    scales[...] = jnp.concatenate([part[...] for part in before[1::2]] + [ended], axis=0).T


def end(kept, got, before=()):
    rows, width = kept.shape
    count = len(before)
    rows += sum(values.shape[0] for values, scales in before)
    near = pl.BlockSpec(memory_space=pltpu.VMEM)
    shape = (width // 128, rows) if count else (rows, width // 128)
    return pl.pallas_call(
        functools.partial(end_kernel, count),
        out_shape=(jax.ShapeDtypeStruct((rows, width), got.dtype), jax.ShapeDtypeStruct(shape, kept.dtype)),
        in_specs=[near] * (2 + 2 * count),
        out_specs=(near, near),
        compiler_params=pltpu.CompilerParams(vmem_limit_bytes=VMEM),
        cost_estimate=pl.CostEstimate(flops=COST, bytes_accessed=1, transcendentals=0),
    )(kept, got, *(array for pair in before for array in pair))


class Steps:

    def __init__(self, tokens_values, tokens_scales, gate_weight, up_weight, down_weight):
        tp, seq = lax.axis_index("tp"), lax.axis_index("seq")
        x, core, high = seq >> 1, seq & 1, tp >> 1
        facts = x == 0, core == 0, (tp ^ seq) & 1 == 0, high == x
        quarters = [(seq ^ bits).reshape(1) for bits in range(4)]
        pairs = [jnp.stack([seq ^ bits, seq ^ bits ^ 1]) for bits in (0, 2)]
        facts, self.quarters, self.pairs, gate_weight = lax.optimization_barrier((facts, quarters, pairs, gate_weight))
        self.first_x, self.first_core, self.even, self.same_half = facts
        self.gate_weight = pltpu.with_memory_space_constraint(gate_weight, pltpu.HBM)
        self.up_weight = pltpu.with_memory_space_constraint(up_weight, pltpu.HBM)
        self.down_weight = pltpu.with_memory_space_constraint(down_weight, pltpu.HBM)
        unit = tokens_values.shape[0] // sum(ROWS)
        self.mine = begin(tokens_values, tokens_scales, [sum(ROWS[:i]) * unit for i in range(len(ROWS) + 1)])
        self.last = self.mine[0]
        self.held = {}

    def run(self, order):
        for step in order:
            with jax.named_scope(step):
                getattr(self, step[:-1])(int(step[-1]))
        values, scales = self.held["end", len(ROWS) - 1]
        return values, scales.T

    def now(self, array):
        return lax.optimization_barrier((array, self.last))[0]

    def far(self, i):
        part = self.now(self.mine[i])
        self.held["far", i] = part, over_tp(part, 2)

    def sel(self, i):
        part, other = self.held["far", i]
        other = self.now(other)
        sent = jnp.where(self.same_half, other, part)
        kept = jnp.where(self.same_half, part, other)
        self.held["sel", i] = kept, over_seq(sent, 2)
        self.last = sent

    def arr(self, i):
        kept, got = self.held["sel", i]
        pair = arrange(self.first_x, kept, self.now(got))
        self.held["arr", i] = pair, over_both(pair, FIRST_IN), over_both(pair, SECOND)
        self.last = pair

    def take(self, i):
        pair, first, second = self.held["arr", i]
        first = self.now(first)
        own = jnp.where(self.even, pair, first)
        others = jnp.where(self.even, first, second)
        self.held["take", i] = self.last = arrange(self.first_core, own, others)

    def load(self, bits):
        gate_weight = self.now(self.gate_weight)
        self.held["load", bits] = self.last = load(gate_weight, self.up_weight, self.quarters[bits])

    def part(self, i, bits, got=None, kind=jnp.bfloat16, split=False):
        some = self.now(self.held["take", i])
        result = sums(some, self.held["load", bits], got, kind, split)
        self.last = result[0] if split else result
        return result

    def a(self, i):
        self.held["a", i] = over_seq(self.part(i, 3), 1)

    def c(self, i):
        self.held["c", i] = over_seq(self.part(i, 1), 1)

    def b(self, i):
        both = self.part(i, 2, self.held["a", i], split=True)
        self.held["b", i] = over_seq(both[0], 2), over_seq(both[1], 2)

    def d(self, i):
        self.held["d", i] = self.part(i, 0, self.held["c", i], jnp.float32)

    def hide(self, i):
        hidden = hide(self.held["d", i], *(self.now(got) for got in self.held["b", i]))
        far = over_seq(hidden, 2)
        self.held["hide", i] = hidden, far, over_seq(hidden, 1)
        self.last = hidden

    def down(self, bits):
        self.held["down", bits] = self.last = load_rows(self.now(self.down_weight), self.pairs[bits // 2])

    def own(self, i):
        hidden, far, near = self.held["hide", i]
        self.held["own", i] = self.last = products((self.now(hidden), near), self.held["down", 0])

    def forward(self, i):
        far = self.now(self.held["hide", i][1])
        self.held["pass", i] = far, over_seq(far, 1)

    def rest(self, i):
        far, last = self.held["pass", i]
        self.held["rest", i] = self.last = products((self.now(far), last), self.held["down", 2], self.held["own", i])

    def out(self, i):
        partial_sum = self.now(self.held["rest", i])
        half = partial_sum.shape[0] // 2
        low, top = partial_sum[:half], partial_sum[half:]
        own = jnp.where(self.first_core, low, top)
        others = jnp.where(self.first_core, top, low)
        one, two = narrow(jnp.where(self.even, others, own)), narrow(others)
        self.held["out", i] = own, over_both(one, FIRST_OUT), over_both(two, SECOND)
        self.last = one

    def mix(self, i):
        own, first, second = self.held["out", i]
        pair = wide(self.now(first)) + jnp.where(self.even, own, wide(second))
        rows = pair.shape[0] // 2
        low, top = pair[:rows], pair[rows:]
        kept = jnp.where(self.first_x, low, top)
        sent = narrow(jnp.where(self.first_x, top, low))
        self.held["mix", i] = kept, over_seq(sent, 2)
        self.last = sent

    def far_out(self, i):
        kept, got = self.held["mix", i]
        got = self.now(got)
        sent = jnp.where(self.same_half, got, narrow(kept))
        kept = jnp.where(self.same_half, kept, wide(got))
        self.held["far_out", i] = kept, over_tp(sent, 2)
        self.last = sent

    def end(self, i):
        kept, got = self.held["far_out", i]
        before = [self.held["end", k] for k in range(i)] if i == len(ROWS) - 1 else ()
        self.held["end", i] = end(kept, self.now(got), before)
        self.last = self.held["end", i][0]


def four_shards(*arrays):
    return Steps(*arrays).run(ORDER)


def solution(mesh):
    placed = (
        P(("groups", "seq"), "tp"),
        P(("groups", "seq"), "tp"),
        P("seq", "tp"),
        P("seq", "tp"),
        P("tp", "seq"),
    )
    fours = mesh.shape["tp"] == 4 and mesh.shape["seq"] == 4
    return jax.shard_map(
        four_shards if fours else any_shards,
        mesh=mesh,
        in_specs=placed,
        out_specs=(P(("groups", "seq"), "tp"), P(("groups", "seq"), "tp")),
        check_vma=False,
    )
```

```python
import functools

import jax
import jax.numpy as jnp
from jax import lax
from jax.experimental import pallas as pl
from jax.experimental.pallas import tpu as pltpu
from jax.sharding import PartitionSpec as P

ROWS = (48, 48, 32)
ORDER = (
    "far0", "load3", "sel0", "far1", "load1", "arr0", "load2", "load0", "sel1", "far2", "take0", "a0", "c0",
    "b0", "arr1", "d0", "sel2", "take1", "a1", "c1", "hide0", "b1", "arr2", "d1", "take2", "a2", "c2",
    "down0", "own0", "forward0", "hide1", "b2", "d2", "down2", "rest0", "out0", "own1", "forward1", "hide2",
    "rest1", "out1", "mix0", "own2", "far_out0", "forward2", "rest2", "out2", "mix1", "end0", "mix2",
    "far_out1", "far_out2", "end1", "end2",
)
TILE = 256
COST = 1 << 34
LOAD_COST = 1 << 30
VMEM = 6 << 20


def blocks(array):
    return array.reshape(array.shape[0], array.shape[1] // 128, 128)


def block_scale(array):
    return jnp.max(jnp.abs(blocks(array)), axis=2) + 1e-06


def expand(values, scales):
    return (blocks(values.astype(jnp.float32)) * scales[:, :, None]).reshape(values.shape)


def scaled(total):
    scales = block_scale(total)
    values = (blocks(total) / scales[:, :, None]).reshape(total.shape).astype(jnp.bfloat16)
    return values, scales


def wide(array):
    return array.astype(jnp.float32)


def narrow(array):
    return array.astype(jnp.bfloat16)


def dot(a, b):
    return jnp.dot(a, b, preferred_element_type=jnp.float32)


def any_shards(tokens_values, tokens_scales, gate_weight, up_weight, down_weight):
    mine = narrow(expand(tokens_values, tokens_scales))
    mine = lax.all_gather(mine, "tp", axis=1, tiled=True)
    inputs = lax.all_to_all(mine, "seq", split_axis=1, concat_axis=0, tiled=True)
    gate = narrow(dot(inputs, gate_weight))
    up = narrow(dot(inputs, up_weight))
    gate = wide(lax.psum_scatter(gate, "seq", scatter_dimension=0, tiled=True))
    up = wide(lax.psum_scatter(up, "seq", scatter_dimension=0, tiled=True))
    hidden = narrow(jax.nn.silu(gate) * up)
    hidden = lax.all_gather(hidden, "seq", axis=0, tiled=True)
    partial_sum = narrow(dot(hidden, down_weight))
    partial_sum = lax.all_to_all(partial_sum, "seq", split_axis=0, concat_axis=1, tiled=True)
    return scaled(wide(lax.psum_scatter(partial_sum, "tp", scatter_dimension=1, tiled=True)))


def over_seq(array, bit):
    return lax.ppermute(array, "seq", [(i, i ^ bit) for i in range(4)])


def over_tp(array, bit):
    return lax.ppermute(array, "tp", [(i, i ^ bit) for i in range(4)])


def device(tp, seq):
    return tp * 4 + seq


FIRST_IN, SECOND, FIRST_OUT = [], [], []
for tp in range(4):
    for seq in range(4):
        if (tp ^ seq) & 1:
            FIRST_IN.append((device(tp, seq), device(tp, seq ^ 1)))
            SECOND.append((device(tp, seq), device(tp ^ 1, seq ^ 1)))
            FIRST_OUT.append((device(tp, seq), device(tp ^ 1, seq)))
        else:
            FIRST_IN.append((device(tp, seq), device(tp ^ 1, seq)))
            FIRST_OUT.append((device(tp, seq), device(tp, seq ^ 1)))


def over_both(array, pairs):
    return lax.ppermute(array, ("tp", "seq"), pairs)


def arrange(low_first, one, other):
    return jnp.concatenate([jnp.where(low_first, one, other), jnp.where(low_first, other, one)], axis=0)


def load_kernel(quarter, gate_weight, up_weight, out, done):
    width = out.shape[2]
    here = pl.ds(pl.multiple_of(quarter[0] * width, width), width)
    pieces = done.shape[1]
    rows = out.shape[1] // pieces
    copies = [
        pltpu.make_async_copy(weight.at[pl.ds(i * rows, rows), here], out.at[k, pl.ds(i * rows, rows)], done.at[k, i])
        for k, weight in enumerate((gate_weight, up_weight))
        for i in range(pieces)
    ]
    for copy in copies:
        copy.start()
    for copy in copies:
        copy.wait()


def load(gate_weight, up_weight, quarter):
    deep, width = gate_weight.shape
    far = pl.BlockSpec(memory_space=pl.ANY)
    return pl.pallas_call(
        load_kernel,
        out_shape=jax.ShapeDtypeStruct((2, deep, width // 4), gate_weight.dtype),
        in_specs=[pl.BlockSpec(memory_space=pltpu.SMEM), far, far],
        out_specs=pl.BlockSpec(memory_space=pltpu.VMEM),
        scratch_shapes=[pltpu.SemaphoreType.DMA((2, 4))],
        compiler_params=pltpu.CompilerParams(vmem_limit_bytes=VMEM),
        cost_estimate=pl.CostEstimate(flops=LOAD_COST, bytes_accessed=1, transcendentals=0),
    )(quarter, gate_weight, up_weight)


def sums_kernel(has_got, split, some, weights, *rest):
    def value(k):
        product = dot(some[...], weights[k])
        return product + wide(rest[0][k]) if has_got else product

    if split:
        for k, out in enumerate(rest[-2:]):
            out[...] = value(k).astype(out.dtype)
    else:

        @pl.loop(0, 2)
        def side(k):
            rest[-1][k] = value(k).astype(rest[-1].dtype)


def sums(some, weights, got=None, kind=jnp.bfloat16, split=False):
    near = pl.BlockSpec(memory_space=pltpu.VMEM)
    shape = some.shape[0], weights.shape[2]
    return pl.pallas_call(
        functools.partial(sums_kernel, got is not None, split),
        out_shape=(jax.ShapeDtypeStruct(shape, kind),) * 2 if split else jax.ShapeDtypeStruct((2,) + shape, kind),
        in_specs=[near] * (2 + (got is not None)),
        out_specs=(near, near) if split else near,
        compiler_params=pltpu.CompilerParams(vmem_limit_bytes=VMEM),
        cost_estimate=pl.CostEstimate(flops=COST, bytes_accessed=1, transcendentals=0),
    )(some, weights, *([] if got is None else [got]))


def load_rows_kernel(quarters, weight, out, done):
    rows = out.shape[1]
    pieces = done.shape[1]
    part = rows // pieces
    copies = [
        pltpu.make_async_copy(
            weight.at[pl.ds(pl.multiple_of(quarters[k] * rows + i * part, part), part)],
            out.at[k, pl.ds(i * part, part)],
            done.at[k, i],
        )
        for k in range(2)
        for i in range(pieces)
    ]
    for copy in copies:
        copy.start()
    for copy in copies:
        copy.wait()


def load_rows(weight, quarters):
    deep, width = weight.shape
    return pl.pallas_call(
        load_rows_kernel,
        out_shape=jax.ShapeDtypeStruct((2, deep // 4, width), weight.dtype),
        in_specs=[pl.BlockSpec(memory_space=pltpu.SMEM), pl.BlockSpec(memory_space=pl.ANY)],
        out_specs=pl.BlockSpec(memory_space=pltpu.VMEM),
        scratch_shapes=[pltpu.SemaphoreType.DMA((2, 4))],
        compiler_params=pltpu.CompilerParams(vmem_limit_bytes=VMEM),
        cost_estimate=pl.CostEstimate(flops=COST, bytes_accessed=1, transcendentals=0),
    )(quarters, weight)


def products_kernel(has_total, one, two, weights, *rest):
    tile = 4 * TILE

    @pl.loop(0, weights.shape[2] // tile)
    def strip(j):
        here = pl.ds(pl.multiple_of(j * tile, tile), tile)
        value = dot(one[...], weights[0, :, here]) + dot(two[...], weights[1, :, here])
        rest[-1][:, here] = value + rest[0][:, here] if has_total else value


def products(pieces, weights, total=None):
    near = pl.BlockSpec(memory_space=pltpu.VMEM)
    return pl.pallas_call(
        functools.partial(products_kernel, total is not None),
        out_shape=jax.ShapeDtypeStruct((pieces[0].shape[0], weights.shape[2]), jnp.float32),
        in_specs=[near] * (3 + (total is not None)),
        out_specs=near,
        compiler_params=pltpu.CompilerParams(vmem_limit_bytes=VMEM),
        cost_estimate=pl.CostEstimate(flops=COST, bytes_accessed=1, transcendentals=0),
    )(*pieces, weights, *([] if total is None else [total]))


def begin_kernel(starts, values, turned_scales, *outs):
    scales = turned_scales[...].T
    for j in range(scales.shape[1]):
        here = pl.ds(j * 128, 128)
        scaled_values = narrow(wide(values[:, here]) * scales[:, j : j + 1])
        for i, out in enumerate(outs):
            out[:, here] = scaled_values[starts[i] : starts[i + 1]]


def begin(values, scales, starts):
    near = pl.BlockSpec(memory_space=pltpu.VMEM)
    count = len(starts) - 1
    return pl.pallas_call(
        functools.partial(begin_kernel, starts),
        out_shape=[jax.ShapeDtypeStruct((starts[i + 1] - starts[i], values.shape[1]), values.dtype) for i in range(count)],
        in_specs=[near] * 2,
        out_specs=[near] * count,
        compiler_params=pltpu.CompilerParams(vmem_limit_bytes=VMEM),
        cost_estimate=pl.CostEstimate(flops=LOAD_COST, bytes_accessed=1, transcendentals=0),
    )(values, scales.T)


def hide_kernel(held, got_gate, got_up, out):
    rows = 32

    @pl.loop(0, out.shape[0] // rows)
    def strip(i):
        here = pl.ds(pl.multiple_of(i * rows, rows), rows)
        gate = held[0, here] + wide(got_gate[here])
        up = held[1, here] + wide(got_up[here])
        out[here] = narrow(jax.nn.silu(gate) * up)


def hide(held, got_gate, got_up):
    near = pl.BlockSpec(memory_space=pltpu.VMEM)
    return pl.pallas_call(
        hide_kernel,
        out_shape=jax.ShapeDtypeStruct(held.shape[1:], got_up.dtype),
        in_specs=[near] * 3,
        out_specs=near,
        compiler_params=pltpu.CompilerParams(vmem_limit_bytes=VMEM),
        cost_estimate=pl.CostEstimate(flops=COST, bytes_accessed=1, transcendentals=0),
    )(held, got_gate, got_up)


def end_kernel(count, kept, got, *rest):
    before, (values, scales) = rest[: 2 * count], rest[2 * count :]
    first = sum(part.shape[0] for part in before[::2])
    rows = pl.ds(first, kept.shape[0])
    columns = []
    for j in range(kept.shape[1] // 128):
        here = pl.ds(j * 128, 128)
        total = kept[:, here] + wide(got[:, here])
        scale = jnp.max(jnp.abs(total), axis=1, keepdims=True) + 1e-06
        values[rows, here] = narrow(total / scale)
        columns.append(scale)
    ended = jnp.concatenate(columns, axis=1)
    if not count:
        scales[...] = ended
        return
    row = 0
    for part in before[::2]:
        values[pl.ds(row, part.shape[0])] = part[...]
        row += part.shape[0]
    scales[...] = jnp.concatenate([part[...] for part in before[1::2]] + [ended], axis=0).T


def end(kept, got, before=()):
    rows, width = kept.shape
    count = len(before)
    rows += sum(values.shape[0] for values, scales in before)
    near = pl.BlockSpec(memory_space=pltpu.VMEM)
    shape = (width // 128, rows) if count else (rows, width // 128)
    return pl.pallas_call(
        functools.partial(end_kernel, count),
        out_shape=(jax.ShapeDtypeStruct((rows, width), got.dtype), jax.ShapeDtypeStruct(shape, kept.dtype)),
        in_specs=[near] * (2 + 2 * count),
        out_specs=(near, near),
        compiler_params=pltpu.CompilerParams(vmem_limit_bytes=VMEM),
        cost_estimate=pl.CostEstimate(flops=COST, bytes_accessed=1, transcendentals=0),
    )(kept, got, *(array for pair in before for array in pair))


class Steps:

    def __init__(self, tokens_values, tokens_scales, gate_weight, up_weight, down_weight):
        tp, seq = lax.axis_index("tp"), lax.axis_index("seq")
        x, core, high = seq >> 1, seq & 1, tp >> 1
        facts = x == 0, core == 0, (tp ^ seq) & 1 == 0, high == x
        quarters = [(seq ^ bits).reshape(1) for bits in range(4)]
        pairs = [jnp.stack([seq ^ bits, seq ^ bits ^ 1]) for bits in (0, 2)]
        facts, self.quarters, self.pairs, gate_weight = lax.optimization_barrier((facts, quarters, pairs, gate_weight))
        self.first_x, self.first_core, self.even, self.same_half = facts
        self.gate_weight = pltpu.with_memory_space_constraint(gate_weight, pltpu.HBM)
        self.up_weight = pltpu.with_memory_space_constraint(up_weight, pltpu.HBM)
        self.down_weight = pltpu.with_memory_space_constraint(down_weight, pltpu.HBM)
        unit = tokens_values.shape[0] // sum(ROWS)
        self.mine = begin(tokens_values, tokens_scales, [sum(ROWS[:i]) * unit for i in range(len(ROWS) + 1)])
        self.last = self.mine[0]
        self.held = {}

    def run(self, order):
        for step in order:
            with jax.named_scope(step):
                getattr(self, step[:-1])(int(step[-1]))
        values, scales = self.held["end", len(ROWS) - 1]
        return values, scales.T

    def now(self, array):
        return lax.optimization_barrier((array, self.last))[0]

    def far(self, i):
        part = self.now(self.mine[i])
        self.held["far", i] = part, over_tp(part, 2)

    def sel(self, i):
        part, other = self.held["far", i]
        other = self.now(other)
        sent = jnp.where(self.same_half, other, part)
        kept = jnp.where(self.same_half, part, other)
        self.held["sel", i] = kept, over_seq(sent, 2)
        self.last = sent

    def arr(self, i):
        kept, got = self.held["sel", i]
        pair = arrange(self.first_x, kept, self.now(got))
        self.held["arr", i] = pair, over_both(pair, FIRST_IN), over_both(pair, SECOND)
        self.last = pair

    def take(self, i):
        pair, first, second = self.held["arr", i]
        first = self.now(first)
        own = jnp.where(self.even, pair, first)
        others = jnp.where(self.even, first, second)
        self.held["take", i] = self.last = arrange(self.first_core, own, others)

    def load(self, bits):
        gate_weight = self.now(self.gate_weight)
        self.held["load", bits] = self.last = load(gate_weight, self.up_weight, self.quarters[bits])

    def part(self, i, bits, got=None, kind=jnp.bfloat16, split=False):
        some = self.now(self.held["take", i])
        result = sums(some, self.held["load", bits], got, kind, split)
        self.last = result[0] if split else result
        return result

    def a(self, i):
        self.held["a", i] = over_seq(self.part(i, 3), 1)

    def c(self, i):
        self.held["c", i] = over_seq(self.part(i, 1), 1)

    def b(self, i):
        both = self.part(i, 2, self.held["a", i], split=True)
        self.held["b", i] = over_seq(both[0], 2), over_seq(both[1], 2)

    def d(self, i):
        self.held["d", i] = self.part(i, 0, self.held["c", i], jnp.float32)

    def hide(self, i):
        hidden = hide(self.held["d", i], *(self.now(got) for got in self.held["b", i]))
        far = over_seq(hidden, 2)
        self.held["hide", i] = hidden, far, over_seq(hidden, 1)
        self.last = hidden

    def down(self, bits):
        self.held["down", bits] = self.last = load_rows(self.now(self.down_weight), self.pairs[bits // 2])

    def own(self, i):
        hidden, far, near = self.held["hide", i]
        self.held["own", i] = self.last = products((self.now(hidden), near), self.held["down", 0])

    def forward(self, i):
        far = self.now(self.held["hide", i][1])
        self.held["pass", i] = far, over_seq(far, 1)

    def rest(self, i):
        far, last = self.held["pass", i]
        self.held["rest", i] = self.last = products((self.now(far), last), self.held["down", 2], self.held["own", i])

    def out(self, i):
        partial_sum = self.now(self.held["rest", i])
        half = partial_sum.shape[0] // 2
        low, top = partial_sum[:half], partial_sum[half:]
        own = jnp.where(self.first_core, low, top)
        others = jnp.where(self.first_core, top, low)
        one, two = narrow(jnp.where(self.even, others, own)), narrow(others)
        self.held["out", i] = own, over_both(one, FIRST_OUT), over_both(two, SECOND)
        self.last = one

    def mix(self, i):
        own, first, second = self.held["out", i]
        pair = wide(self.now(first)) + jnp.where(self.even, own, wide(second))
        rows = pair.shape[0] // 2
        low, top = pair[:rows], pair[rows:]
        kept = jnp.where(self.first_x, low, top)
        sent = narrow(jnp.where(self.first_x, top, low))
        self.held["mix", i] = kept, over_seq(sent, 2)
        self.last = sent

    def far_out(self, i):
        kept, got = self.held["mix", i]
        got = self.now(got)
        sent = jnp.where(self.same_half, got, narrow(kept))
        kept = jnp.where(self.same_half, kept, wide(got))
        self.held["far_out", i] = kept, over_tp(sent, 2)
        self.last = sent

    def end(self, i):
        kept, got = self.held["far_out", i]
        before = [self.held["end", k] for k in range(i)] if i == len(ROWS) - 1 else ()
        self.held["end", i] = end(kept, self.now(got), before)
        self.last = self.held["end", i][0]


def four_shards(*arrays):
    return Steps(*arrays).run(ORDER)


def solution(mesh):
    placed = (
        P(("groups", "seq"), "tp"),
        P(("groups", "seq"), "tp"),
        P("seq", "tp"),
        P("seq", "tp"),
        P("tp", "seq"),
    )
    fours = mesh.shape["tp"] == 4 and mesh.shape["seq"] == 4
    return jax.shard_map(
        four_shards if fours else any_shards,
        mesh=mesh,
        in_specs=placed,
        out_specs=(P(("groups", "seq"), "tp"), P(("groups", "seq"), "tp")),
        check_vma=False,
    )
```

```python
import functools

import jax
import jax.numpy as jnp
from jax import lax
from jax.experimental import pallas as pl
from jax.experimental.pallas import tpu as pltpu
from jax.sharding import PartitionSpec as P

ROWS = (48, 48, 32)
ORDER = (
    "far0", "load3", "sel0", "far1", "load1", "arr0", "load2", "load0", "sel1", "far2", "take0", "a0", "c0",
    "b0", "arr1", "d0", "sel2", "take1", "a1", "c1", "b1", "arr2", "d1", "hide0", "take2", "a2", "c2",
    "down0", "own0", "b2", "d2", "forward0", "down2", "hide1", "rest0", "out0", "own1", "forward1", "hide2",
    "mix0", "rest1", "out1", "forward2", "own2", "rest2", "out2", "far_out0", "mix1", "mix2", "end0",
    "far_out1", "far_out2", "end1", "end2",
)
TILE = 256
SPLIT = ()
COST = 1 << 34
LOAD_COST = 1 << 30
VMEM = 6 << 20


def blocks(array):
    return array.reshape(array.shape[0], array.shape[1] // 128, 128)


def block_scale(array):
    return jnp.max(jnp.abs(blocks(array)), axis=2) + 1e-06


def expand(values, scales):
    return (blocks(values.astype(jnp.float32)) * scales[:, :, None]).reshape(values.shape)


def scaled(total):
    scales = block_scale(total)
    values = (blocks(total) / scales[:, :, None]).reshape(total.shape).astype(jnp.bfloat16)
    return values, scales


def wide(array):
    return array.astype(jnp.float32)


def narrow(array):
    return array.astype(jnp.bfloat16)


def dot(a, b):
    return jnp.dot(a, b, preferred_element_type=jnp.float32)


def any_shards(tokens_values, tokens_scales, gate_weight, up_weight, down_weight):
    mine = narrow(expand(tokens_values, tokens_scales))
    mine = lax.all_gather(mine, "tp", axis=1, tiled=True)
    inputs = lax.all_to_all(mine, "seq", split_axis=1, concat_axis=0, tiled=True)
    gate = narrow(dot(inputs, gate_weight))
    up = narrow(dot(inputs, up_weight))
    gate = wide(lax.psum_scatter(gate, "seq", scatter_dimension=0, tiled=True))
    up = wide(lax.psum_scatter(up, "seq", scatter_dimension=0, tiled=True))
    hidden = narrow(jax.nn.silu(gate) * up)
    hidden = lax.all_gather(hidden, "seq", axis=0, tiled=True)
    partial_sum = narrow(dot(hidden, down_weight))
    partial_sum = lax.all_to_all(partial_sum, "seq", split_axis=0, concat_axis=1, tiled=True)
    return scaled(wide(lax.psum_scatter(partial_sum, "tp", scatter_dimension=1, tiled=True)))


def over_seq(array, bit):
    return lax.ppermute(array, "seq", [(i, i ^ bit) for i in range(4)])


def over_tp(array, bit):
    return lax.ppermute(array, "tp", [(i, i ^ bit) for i in range(4)])


def device(tp, seq):
    return tp * 4 + seq


FIRST_IN, SECOND, FIRST_OUT = [], [], []
for tp in range(4):
    for seq in range(4):
        if (tp ^ seq) & 1:
            FIRST_IN.append((device(tp, seq), device(tp, seq ^ 1)))
            SECOND.append((device(tp, seq), device(tp ^ 1, seq ^ 1)))
            FIRST_OUT.append((device(tp, seq), device(tp ^ 1, seq)))
        else:
            FIRST_IN.append((device(tp, seq), device(tp ^ 1, seq)))
            FIRST_OUT.append((device(tp, seq), device(tp, seq ^ 1)))


def over_both(array, pairs):
    return lax.ppermute(array, ("tp", "seq"), pairs)


def arrange(low_first, one, other):
    return jnp.concatenate([jnp.where(low_first, one, other), jnp.where(low_first, other, one)], axis=0)


def load_kernel(quarter, gate_weight, up_weight, out, done):
    width = out.shape[2]
    here = pl.ds(pl.multiple_of(quarter[0] * width, width), width)
    pieces = done.shape[1]
    rows = out.shape[1] // pieces
    copies = [
        pltpu.make_async_copy(weight.at[pl.ds(i * rows, rows), here], out.at[k, pl.ds(i * rows, rows)], done.at[k, i])
        for k, weight in enumerate((gate_weight, up_weight))
        for i in range(pieces)
    ]
    for copy in copies:
        copy.start()
    for copy in copies:
        copy.wait()


def load(gate_weight, up_weight, quarter):
    deep, width = gate_weight.shape
    far = pl.BlockSpec(memory_space=pl.ANY)
    return pl.pallas_call(
        load_kernel,
        out_shape=jax.ShapeDtypeStruct((2, deep, width // 4), gate_weight.dtype),
        in_specs=[pl.BlockSpec(memory_space=pltpu.SMEM), far, far],
        out_specs=pl.BlockSpec(memory_space=pltpu.VMEM),
        scratch_shapes=[pltpu.SemaphoreType.DMA((2, 4))],
        compiler_params=pltpu.CompilerParams(vmem_limit_bytes=VMEM),
        cost_estimate=pl.CostEstimate(flops=LOAD_COST, bytes_accessed=1, transcendentals=0),
    )(quarter, gate_weight, up_weight)


def sums_kernel(has_got, split, some, weights, *rest):
    def value(k):
        product = dot(some[...], weights[k])
        return product + wide(rest[0][k]) if has_got else product

    if split:
        for k, out in enumerate(rest[-2:]):
            out[...] = value(k).astype(out.dtype)
    else:

        @pl.loop(0, 2)
        def side(k):
            rest[-1][k] = value(k).astype(rest[-1].dtype)


def sums(some, weights, got=None, kind=jnp.bfloat16, split=False):
    near = pl.BlockSpec(memory_space=pltpu.VMEM)
    shape = some.shape[0], weights.shape[2]
    return pl.pallas_call(
        functools.partial(sums_kernel, got is not None, split),
        out_shape=(jax.ShapeDtypeStruct(shape, kind),) * 2 if split else jax.ShapeDtypeStruct((2,) + shape, kind),
        in_specs=[near] * (2 + (got is not None)),
        out_specs=(near, near) if split else near,
        compiler_params=pltpu.CompilerParams(vmem_limit_bytes=VMEM),
        cost_estimate=pl.CostEstimate(flops=COST, bytes_accessed=1, transcendentals=0),
    )(some, weights, *([] if got is None else [got]))


def load_rows_kernel(quarters, weight, out, done):
    rows = out.shape[1]
    pieces = done.shape[1]
    part = rows // pieces
    copies = [
        pltpu.make_async_copy(
            weight.at[pl.ds(pl.multiple_of(quarters[k] * rows + i * part, part), part)],
            out.at[k, pl.ds(i * part, part)],
            done.at[k, i],
        )
        for k in range(2)
        for i in range(pieces)
    ]
    for copy in copies:
        copy.start()
    for copy in copies:
        copy.wait()


def load_rows(weight, quarters):
    deep, width = weight.shape
    return pl.pallas_call(
        load_rows_kernel,
        out_shape=jax.ShapeDtypeStruct((2, deep // 4, width), weight.dtype),
        in_specs=[pl.BlockSpec(memory_space=pltpu.SMEM), pl.BlockSpec(memory_space=pl.ANY)],
        out_specs=pl.BlockSpec(memory_space=pltpu.VMEM),
        scratch_shapes=[pltpu.SemaphoreType.DMA((2, 4))],
        compiler_params=pltpu.CompilerParams(vmem_limit_bytes=VMEM),
        cost_estimate=pl.CostEstimate(flops=COST, bytes_accessed=1, transcendentals=0),
    )(quarters, weight)


def products_kernel(has_total, one, two, weights, *rest):
    tile = 4 * TILE

    @pl.loop(0, weights.shape[2] // tile)
    def strip(j):
        here = pl.ds(pl.multiple_of(j * tile, tile), tile)
        value = dot(one[...], weights[0, :, here]) + dot(two[...], weights[1, :, here])
        rest[-1][:, here] = value + rest[0][:, here] if has_total else value


def products(pieces, weights, total=None):
    near = pl.BlockSpec(memory_space=pltpu.VMEM)
    return pl.pallas_call(
        functools.partial(products_kernel, total is not None),
        out_shape=jax.ShapeDtypeStruct((pieces[0].shape[0], weights.shape[2]), jnp.float32),
        in_specs=[near] * (3 + (total is not None)),
        out_specs=near,
        compiler_params=pltpu.CompilerParams(vmem_limit_bytes=VMEM),
        cost_estimate=pl.CostEstimate(flops=COST, bytes_accessed=1, transcendentals=0),
    )(*pieces, weights, *([] if total is None else [total]))


def begin_kernel(starts, values, turned_scales, *outs):
    scales = turned_scales[...].T
    for j in range(scales.shape[1]):
        here = pl.ds(j * 128, 128)
        scaled_values = narrow(wide(values[:, here]) * scales[:, j : j + 1])
        for i, out in enumerate(outs):
            out[:, here] = scaled_values[starts[i] : starts[i + 1]]


def begin(values, scales, starts):
    near = pl.BlockSpec(memory_space=pltpu.VMEM)
    count = len(starts) - 1
    return pl.pallas_call(
        functools.partial(begin_kernel, starts),
        out_shape=[jax.ShapeDtypeStruct((starts[i + 1] - starts[i], values.shape[1]), values.dtype) for i in range(count)],
        in_specs=[near] * 2,
        out_specs=[near] * count,
        compiler_params=pltpu.CompilerParams(vmem_limit_bytes=VMEM),
        cost_estimate=pl.CostEstimate(flops=LOAD_COST, bytes_accessed=1, transcendentals=0),
    )(values, scales.T)


def hide_kernel(held, *rest):
    got, out = rest[:-1], rest[-1]
    got_gate, got_up = got if len(got) == 2 else (got[0].at[0], got[0].at[1])
    rows = 32

    @pl.loop(0, out.shape[0] // rows)
    def strip(i):
        here = pl.ds(pl.multiple_of(i * rows, rows), rows)
        gate = held[0, here] + wide(got_gate[here])
        up = held[1, here] + wide(got_up[here])
        out[here] = narrow(jax.nn.silu(gate) * up)


def hide(held, *got):
    near = pl.BlockSpec(memory_space=pltpu.VMEM)
    return pl.pallas_call(
        hide_kernel,
        out_shape=jax.ShapeDtypeStruct(held.shape[1:], got[0].dtype),
        in_specs=[near] * (1 + len(got)),
        out_specs=near,
        compiler_params=pltpu.CompilerParams(vmem_limit_bytes=VMEM),
        cost_estimate=pl.CostEstimate(flops=COST, bytes_accessed=1, transcendentals=0),
    )(held, *got)


def end_kernel(count, kept, got, *rest):
    before, (values, scales) = rest[: 2 * count], rest[2 * count :]
    first = sum(part.shape[0] for part in before[::2])
    rows = pl.ds(first, kept.shape[0])
    columns = []
    for j in range(kept.shape[1] // 128):
        here = pl.ds(j * 128, 128)
        total = kept[:, here] + wide(got[:, here])
        scale = jnp.max(jnp.abs(total), axis=1, keepdims=True) + 1e-06
        values[rows, here] = narrow(total / scale)
        columns.append(scale)
    ended = jnp.concatenate(columns, axis=1)
    if not count:
        scales[...] = ended
        return
    row = 0
    for part in before[::2]:
        values[pl.ds(row, part.shape[0])] = part[...]
        row += part.shape[0]
    scales[...] = jnp.concatenate([part[...] for part in before[1::2]] + [ended], axis=0).T


def end(kept, got, before=()):
    rows, width = kept.shape
    count = len(before)
    rows += sum(values.shape[0] for values, scales in before)
    near = pl.BlockSpec(memory_space=pltpu.VMEM)
    shape = (width // 128, rows) if count else (rows, width // 128)
    return pl.pallas_call(
        functools.partial(end_kernel, count),
        out_shape=(jax.ShapeDtypeStruct((rows, width), got.dtype), jax.ShapeDtypeStruct(shape, kept.dtype)),
        in_specs=[near] * (2 + 2 * count),
        out_specs=(near, near),
        compiler_params=pltpu.CompilerParams(vmem_limit_bytes=VMEM),
        cost_estimate=pl.CostEstimate(flops=COST, bytes_accessed=1, transcendentals=0),
    )(kept, got, *(array for pair in before for array in pair))


class Steps:

    def __init__(self, tokens_values, tokens_scales, gate_weight, up_weight, down_weight):
        tp, seq = lax.axis_index("tp"), lax.axis_index("seq")
        x, core, high = seq >> 1, seq & 1, tp >> 1
        facts = x == 0, core == 0, (tp ^ seq) & 1 == 0, high == x
        quarters = [(seq ^ bits).reshape(1) for bits in range(4)]
        pairs = [jnp.stack([seq ^ bits, seq ^ bits ^ 1]) for bits in (0, 2)]
        facts, self.quarters, self.pairs, gate_weight = lax.optimization_barrier((facts, quarters, pairs, gate_weight))
        self.first_x, self.first_core, self.even, self.same_half = facts
        self.gate_weight = pltpu.with_memory_space_constraint(gate_weight, pltpu.HBM)
        self.up_weight = pltpu.with_memory_space_constraint(up_weight, pltpu.HBM)
        self.down_weight = pltpu.with_memory_space_constraint(down_weight, pltpu.HBM)
        unit = tokens_values.shape[0] // sum(ROWS)
        self.mine = begin(tokens_values, tokens_scales, [sum(ROWS[:i]) * unit for i in range(len(ROWS) + 1)])
        self.last = self.mine[0]
        self.held = {}

    def run(self, order):
        for step in order:
            with jax.named_scope(step):
                getattr(self, step[:-1])(int(step[-1]))
        values, scales = self.held["end", len(ROWS) - 1]
        return values, scales.T

    def now(self, array):
        return lax.optimization_barrier((array, self.last))[0]

    def far(self, i):
        part = self.now(self.mine[i])
        self.held["far", i] = part, over_tp(part, 2)

    def sel(self, i):
        part, other = self.held["far", i]
        other = self.now(other)
        sent = jnp.where(self.same_half, other, part)
        kept = jnp.where(self.same_half, part, other)
        self.held["sel", i] = kept, over_seq(sent, 2)
        self.last = sent

    def arr(self, i):
        kept, got = self.held["sel", i]
        pair = arrange(self.first_x, kept, self.now(got))
        self.held["arr", i] = pair, over_both(pair, FIRST_IN), over_both(pair, SECOND)
        self.last = pair

    def take(self, i):
        pair, first, second = self.held["arr", i]
        first = self.now(first)
        own = jnp.where(self.even, pair, first)
        others = jnp.where(self.even, first, second)
        self.held["take", i] = self.last = arrange(self.first_core, own, others)

    def load(self, bits):
        gate_weight = self.now(self.gate_weight)
        self.held["load", bits] = self.last = load(gate_weight, self.up_weight, self.quarters[bits])

    def part(self, i, bits, got=None, kind=jnp.bfloat16, split=False):
        some = self.now(self.held["take", i])
        result = sums(some, self.held["load", bits], got, kind, split)
        self.last = result[0] if split else result
        return result

    def a(self, i):
        self.held["a", i] = over_seq(self.part(i, 3), 1)

    def c(self, i):
        self.held["c", i] = over_seq(self.part(i, 1), 1)

    def b(self, i):
        sent = self.part(i, 2, self.held["a", i], split=i in SPLIT)
        self.held["b", i] = [over_seq(part, 2) for part in (sent if i in SPLIT else (sent,))]

    def d(self, i):
        self.held["d", i] = self.part(i, 0, self.held["c", i], jnp.float32)

    def hide(self, i):
        hidden = hide(self.held["d", i], *(self.now(got) for got in self.held["b", i]))
        far = over_seq(hidden, 2)
        self.held["hide", i] = hidden, far, over_seq(hidden, 1)
        self.last = hidden

    def down(self, bits):
        self.held["down", bits] = self.last = load_rows(self.now(self.down_weight), self.pairs[bits // 2])

    def own(self, i):
        hidden, far, near = self.held["hide", i]
        self.held["own", i] = self.last = products((self.now(hidden), near), self.held["down", 0])

    def forward(self, i):
        far = self.now(self.held["hide", i][1])
        self.held["pass", i] = far, over_seq(far, 1)

    def rest(self, i):
        far, last = self.held["pass", i]
        self.held["rest", i] = self.last = products((self.now(far), last), self.held["down", 2], self.held["own", i])

    def out(self, i):
        partial_sum = self.now(self.held["rest", i])
        half = partial_sum.shape[0] // 2
        low, top = partial_sum[:half], partial_sum[half:]
        own = jnp.where(self.first_core, low, top)
        others = jnp.where(self.first_core, top, low)
        one, two = narrow(jnp.where(self.even, others, own)), narrow(others)
        self.held["out", i] = own, over_both(one, FIRST_OUT), over_both(two, SECOND)
        self.last = one

    def mix(self, i):
        own, first, second = self.held["out", i]
        pair = wide(self.now(first)) + jnp.where(self.even, own, wide(second))
        rows = pair.shape[0] // 2
        low, top = pair[:rows], pair[rows:]
        kept = jnp.where(self.first_x, low, top)
        sent = narrow(jnp.where(self.first_x, top, low))
        self.held["mix", i] = kept, over_seq(sent, 2)
        self.last = sent

    def far_out(self, i):
        kept, got = self.held["mix", i]
        got = self.now(got)
        sent = jnp.where(self.same_half, got, narrow(kept))
        kept = jnp.where(self.same_half, kept, wide(got))
        self.held["far_out", i] = kept, over_tp(sent, 2)
        self.last = sent

    def end(self, i):
        kept, got = self.held["far_out", i]
        before = [self.held["end", k] for k in range(i)] if i == len(ROWS) - 1 else ()
        self.held["end", i] = end(kept, self.now(got), before)
        self.last = self.held["end", i][0]


def four_shards(*arrays):
    return Steps(*arrays).run(ORDER)


def solution(mesh):
    placed = (
        P(("groups", "seq"), "tp"),
        P(("groups", "seq"), "tp"),
        P("seq", "tp"),
        P("seq", "tp"),
        P("tp", "seq"),
    )
    fours = mesh.shape["tp"] == 4 and mesh.shape["seq"] == 4
    return jax.shard_map(
        four_shards if fours else any_shards,
        mesh=mesh,
        in_specs=placed,
        out_specs=(P(("groups", "seq"), "tp"), P(("groups", "seq"), "tp")),
        check_vma=False,
    )
```

```python
import functools

import jax
import jax.numpy as jnp
from jax import lax
from jax.experimental import pallas as pl
from jax.experimental.pallas import tpu as pltpu
from jax.sharding import PartitionSpec as P

ROWS = (48, 48, 32)
ORDER = (
    "far0", "load3", "sel0", "far1", "load1", "arr0", "load2", "load0", "sel1", "far2", "take0", "a0", "c0",
    "b0", "arr1", "d0", "sel2", "take1", "a1", "c1", "hide0", "b1", "arr2", "d1", "take2", "a2", "c2",
    "down0", "own0", "forward0", "hide1", "b2", "d2", "down2", "rest0", "out0", "forward1", "own1", "rest1",
    "out1", "hide2", "mix0", "mix1", "forward2", "own2", "rest2", "out2", "far_out0", "mix2", "far_out1",
    "far_out2", "end0", "end1", "end2",
)
TILE = 256
SPLIT = (0, 1)
COST = 1 << 34
LOAD_COST = 1 << 30
VMEM = 6 << 20


def blocks(array):
    return array.reshape(array.shape[0], array.shape[1] // 128, 128)


def block_scale(array):
    return jnp.max(jnp.abs(blocks(array)), axis=2) + 1e-06


def expand(values, scales):
    return (blocks(values.astype(jnp.float32)) * scales[:, :, None]).reshape(values.shape)


def scaled(total):
    scales = block_scale(total)
    values = (blocks(total) / scales[:, :, None]).reshape(total.shape).astype(jnp.bfloat16)
    return values, scales


def wide(array):
    return array.astype(jnp.float32)


def narrow(array):
    return array.astype(jnp.bfloat16)


def dot(a, b):
    return jnp.dot(a, b, preferred_element_type=jnp.float32)


def any_shards(tokens_values, tokens_scales, gate_weight, up_weight, down_weight):
    mine = narrow(expand(tokens_values, tokens_scales))
    mine = lax.all_gather(mine, "tp", axis=1, tiled=True)
    inputs = lax.all_to_all(mine, "seq", split_axis=1, concat_axis=0, tiled=True)
    gate = narrow(dot(inputs, gate_weight))
    up = narrow(dot(inputs, up_weight))
    gate = wide(lax.psum_scatter(gate, "seq", scatter_dimension=0, tiled=True))
    up = wide(lax.psum_scatter(up, "seq", scatter_dimension=0, tiled=True))
    hidden = narrow(jax.nn.silu(gate) * up)
    hidden = lax.all_gather(hidden, "seq", axis=0, tiled=True)
    partial_sum = narrow(dot(hidden, down_weight))
    partial_sum = lax.all_to_all(partial_sum, "seq", split_axis=0, concat_axis=1, tiled=True)
    return scaled(wide(lax.psum_scatter(partial_sum, "tp", scatter_dimension=1, tiled=True)))


def over_seq(array, bit):
    return lax.ppermute(array, "seq", [(i, i ^ bit) for i in range(4)])


def over_tp(array, bit):
    return lax.ppermute(array, "tp", [(i, i ^ bit) for i in range(4)])


def device(tp, seq):
    return tp * 4 + seq


FIRST_IN, SECOND, FIRST_OUT = [], [], []
for tp in range(4):
    for seq in range(4):
        if (tp ^ seq) & 1:
            FIRST_IN.append((device(tp, seq), device(tp, seq ^ 1)))
            SECOND.append((device(tp, seq), device(tp ^ 1, seq ^ 1)))
            FIRST_OUT.append((device(tp, seq), device(tp ^ 1, seq)))
        else:
            FIRST_IN.append((device(tp, seq), device(tp ^ 1, seq)))
            FIRST_OUT.append((device(tp, seq), device(tp, seq ^ 1)))


def over_both(array, pairs):
    return lax.ppermute(array, ("tp", "seq"), pairs)


def arrange(low_first, one, other):
    return jnp.concatenate([jnp.where(low_first, one, other), jnp.where(low_first, other, one)], axis=0)


def load_kernel(quarter, gate_weight, up_weight, out, done):
    width = out.shape[2]
    here = pl.ds(pl.multiple_of(quarter[0] * width, width), width)
    pieces = done.shape[1]
    rows = out.shape[1] // pieces
    copies = [
        pltpu.make_async_copy(weight.at[pl.ds(i * rows, rows), here], out.at[k, pl.ds(i * rows, rows)], done.at[k, i])
        for k, weight in enumerate((gate_weight, up_weight))
        for i in range(pieces)
    ]
    for copy in copies:
        copy.start()
    for copy in copies:
        copy.wait()


def load(gate_weight, up_weight, quarter):
    deep, width = gate_weight.shape
    far = pl.BlockSpec(memory_space=pl.ANY)
    return pl.pallas_call(
        load_kernel,
        out_shape=jax.ShapeDtypeStruct((2, deep, width // 4), gate_weight.dtype),
        in_specs=[pl.BlockSpec(memory_space=pltpu.SMEM), far, far],
        out_specs=pl.BlockSpec(memory_space=pltpu.VMEM),
        scratch_shapes=[pltpu.SemaphoreType.DMA((2, 4))],
        compiler_params=pltpu.CompilerParams(vmem_limit_bytes=VMEM),
        cost_estimate=pl.CostEstimate(flops=LOAD_COST, bytes_accessed=1, transcendentals=0),
    )(quarter, gate_weight, up_weight)


def sums_kernel(has_got, split, some, weights, *rest):
    def value(k):
        product = dot(some[...], weights[k])
        return product + wide(rest[0][k]) if has_got else product

    if split:
        for k, out in enumerate(rest[-2:]):
            out[...] = value(k).astype(out.dtype)
    else:

        @pl.loop(0, 2)
        def side(k):
            rest[-1][k] = value(k).astype(rest[-1].dtype)


def sums(some, weights, got=None, kind=jnp.bfloat16, split=False):
    near = pl.BlockSpec(memory_space=pltpu.VMEM)
    shape = some.shape[0], weights.shape[2]
    return pl.pallas_call(
        functools.partial(sums_kernel, got is not None, split),
        out_shape=(jax.ShapeDtypeStruct(shape, kind),) * 2 if split else jax.ShapeDtypeStruct((2,) + shape, kind),
        in_specs=[near] * (2 + (got is not None)),
        out_specs=(near, near) if split else near,
        compiler_params=pltpu.CompilerParams(vmem_limit_bytes=VMEM),
        cost_estimate=pl.CostEstimate(flops=COST, bytes_accessed=1, transcendentals=0),
    )(some, weights, *([] if got is None else [got]))


def load_rows_kernel(quarters, weight, out, done):
    rows = out.shape[1]
    pieces = done.shape[1]
    part = rows // pieces
    copies = [
        pltpu.make_async_copy(
            weight.at[pl.ds(pl.multiple_of(quarters[k] * rows + i * part, part), part)],
            out.at[k, pl.ds(i * part, part)],
            done.at[k, i],
        )
        for k in range(2)
        for i in range(pieces)
    ]
    for copy in copies:
        copy.start()
    for copy in copies:
        copy.wait()


def load_rows(weight, quarters):
    deep, width = weight.shape
    return pl.pallas_call(
        load_rows_kernel,
        out_shape=jax.ShapeDtypeStruct((2, deep // 4, width), weight.dtype),
        in_specs=[pl.BlockSpec(memory_space=pltpu.SMEM), pl.BlockSpec(memory_space=pl.ANY)],
        out_specs=pl.BlockSpec(memory_space=pltpu.VMEM),
        scratch_shapes=[pltpu.SemaphoreType.DMA((2, 4))],
        compiler_params=pltpu.CompilerParams(vmem_limit_bytes=VMEM),
        cost_estimate=pl.CostEstimate(flops=COST, bytes_accessed=1, transcendentals=0),
    )(quarters, weight)


def products_kernel(has_total, one, two, weights, *rest):
    tile = 4 * TILE

    @pl.loop(0, weights.shape[2] // tile)
    def strip(j):
        here = pl.ds(pl.multiple_of(j * tile, tile), tile)
        value = dot(one[...], weights[0, :, here]) + dot(two[...], weights[1, :, here])
        rest[-1][:, here] = value + rest[0][:, here] if has_total else value


def products(pieces, weights, total=None):
    near = pl.BlockSpec(memory_space=pltpu.VMEM)
    return pl.pallas_call(
        functools.partial(products_kernel, total is not None),
        out_shape=jax.ShapeDtypeStruct((pieces[0].shape[0], weights.shape[2]), jnp.float32),
        in_specs=[near] * (3 + (total is not None)),
        out_specs=near,
        compiler_params=pltpu.CompilerParams(vmem_limit_bytes=VMEM),
        cost_estimate=pl.CostEstimate(flops=COST, bytes_accessed=1, transcendentals=0),
    )(*pieces, weights, *([] if total is None else [total]))


def begin_kernel(starts, values, turned_scales, *outs):
    scales = turned_scales[...].T
    for j in range(scales.shape[1]):
        here = pl.ds(j * 128, 128)
        scaled_values = narrow(wide(values[:, here]) * scales[:, j : j + 1])
        for i, out in enumerate(outs):
            out[:, here] = scaled_values[starts[i] : starts[i + 1]]


def begin(values, scales, starts):
    near = pl.BlockSpec(memory_space=pltpu.VMEM)
    count = len(starts) - 1
    return pl.pallas_call(
        functools.partial(begin_kernel, starts),
        out_shape=[jax.ShapeDtypeStruct((starts[i + 1] - starts[i], values.shape[1]), values.dtype) for i in range(count)],
        in_specs=[near] * 2,
        out_specs=[near] * count,
        compiler_params=pltpu.CompilerParams(vmem_limit_bytes=VMEM),
        cost_estimate=pl.CostEstimate(flops=LOAD_COST, bytes_accessed=1, transcendentals=0),
    )(values, scales.T)


def hide_kernel(held, *rest):
    got, out = rest[:-1], rest[-1]
    got_gate, got_up = got if len(got) == 2 else (got[0].at[0], got[0].at[1])
    rows = 32

    @pl.loop(0, out.shape[0] // rows)
    def strip(i):
        here = pl.ds(pl.multiple_of(i * rows, rows), rows)
        gate = held[0, here] + wide(got_gate[here])
        up = held[1, here] + wide(got_up[here])
        out[here] = narrow(jax.nn.silu(gate) * up)


def hide(held, *got):
    near = pl.BlockSpec(memory_space=pltpu.VMEM)
    return pl.pallas_call(
        hide_kernel,
        out_shape=jax.ShapeDtypeStruct(held.shape[1:], got[0].dtype),
        in_specs=[near] * (1 + len(got)),
        out_specs=near,
        compiler_params=pltpu.CompilerParams(vmem_limit_bytes=VMEM),
        cost_estimate=pl.CostEstimate(flops=COST, bytes_accessed=1, transcendentals=0),
    )(held, *got)


def end_kernel(count, kept, got, *rest):
    before, (values, scales) = rest[: 2 * count], rest[2 * count :]
    first = sum(part.shape[0] for part in before[::2])
    rows = pl.ds(first, kept.shape[0])
    columns = []
    for j in range(kept.shape[1] // 128):
        here = pl.ds(j * 128, 128)
        total = kept[:, here] + wide(got[:, here])
        scale = jnp.max(jnp.abs(total), axis=1, keepdims=True) + 1e-06
        values[rows, here] = narrow(total / scale)
        columns.append(scale)
    ended = jnp.concatenate(columns, axis=1)
    if not count:
        scales[...] = ended
        return
    row = 0
    for part in before[::2]:
        values[pl.ds(row, part.shape[0])] = part[...]
        row += part.shape[0]
    scales[...] = jnp.concatenate([part[...] for part in before[1::2]] + [ended], axis=0).T


def end(kept, got, before=()):
    rows, width = kept.shape
    count = len(before)
    rows += sum(values.shape[0] for values, scales in before)
    near = pl.BlockSpec(memory_space=pltpu.VMEM)
    shape = (width // 128, rows) if count else (rows, width // 128)
    return pl.pallas_call(
        functools.partial(end_kernel, count),
        out_shape=(jax.ShapeDtypeStruct((rows, width), got.dtype), jax.ShapeDtypeStruct(shape, kept.dtype)),
        in_specs=[near] * (2 + 2 * count),
        out_specs=(near, near),
        compiler_params=pltpu.CompilerParams(vmem_limit_bytes=VMEM),
        cost_estimate=pl.CostEstimate(flops=COST, bytes_accessed=1, transcendentals=0),
    )(kept, got, *(array for pair in before for array in pair))


def small(kernel, outs, flags, *arrays):
    near = pl.BlockSpec(memory_space=pltpu.VMEM)
    return pl.pallas_call(
        kernel,
        out_shape=[jax.ShapeDtypeStruct(*out) for out in outs],
        in_specs=[pl.BlockSpec(memory_space=pltpu.SMEM)] + [near] * len(arrays),
        out_specs=[near] * len(outs),
        compiler_params=pltpu.CompilerParams(vmem_limit_bytes=VMEM),
        cost_estimate=pl.CostEstimate(flops=COST, bytes_accessed=1, transcendentals=0),
    )(flags, *arrays)


def strips(array):
    return pl.loop(0, array.shape[1] // TILE)


def out_kernel(flags, partial_sum, own, one, two):
    half = own.shape[0]
    low, top = pl.ds(0, half), pl.ds(half, half)

    @strips(own)
    def strip(j):
        here = pl.ds(pl.multiple_of(j * TILE, TILE), TILE)
        first, last = partial_sum[low, here], partial_sum[top, here]
        mine = jnp.where(flags[1] == 1, first, last)
        others = jnp.where(flags[1] == 1, last, first)
        own[:, here] = mine
        one[:, here] = narrow(jnp.where(flags[2] == 1, others, mine))
        two[:, here] = narrow(others)


def mix_kernel(flags, own, got_one, got_two, kept, sent):
    rows = kept.shape[0]

    @strips(own)
    def strip(j):
        here = pl.ds(pl.multiple_of(j * TILE, TILE), TILE)
        pair = wide(got_one[:, here]) + jnp.where(flags[2] == 1, own[:, here], wide(got_two[:, here]))
        kept[:, here] = jnp.where(flags[0] == 1, pair[:rows], pair[rows:])
        sent[:, here] = narrow(jnp.where(flags[0] == 1, pair[rows:], pair[:rows]))


def far_out_kernel(flags, kept, got, still, sent):
    @strips(kept)
    def strip(j):
        here = pl.ds(pl.multiple_of(j * TILE, TILE), TILE)
        mine, other = kept[:, here], wide(got[:, here])
        still[:, here] = jnp.where(flags[3] == 1, mine, other)
        sent[:, here] = narrow(jnp.where(flags[3] == 1, other, mine))


class Steps:

    def __init__(self, tokens_values, tokens_scales, gate_weight, up_weight, down_weight):
        tp, seq = lax.axis_index("tp"), lax.axis_index("seq")
        x, core, high = seq >> 1, seq & 1, tp >> 1
        facts = x == 0, core == 0, (tp ^ seq) & 1 == 0, high == x
        quarters = [(seq ^ bits).reshape(1) for bits in range(4)]
        pairs = [jnp.stack([seq ^ bits, seq ^ bits ^ 1]) for bits in (0, 2)]
        flags = jnp.stack(facts).astype(jnp.int32)
        facts, self.flags, self.quarters, self.pairs, gate_weight = lax.optimization_barrier(
            (facts, flags, quarters, pairs, gate_weight)
        )
        self.first_x, self.first_core, self.even, self.same_half = facts
        self.gate_weight = pltpu.with_memory_space_constraint(gate_weight, pltpu.HBM)
        self.up_weight = pltpu.with_memory_space_constraint(up_weight, pltpu.HBM)
        self.down_weight = pltpu.with_memory_space_constraint(down_weight, pltpu.HBM)
        unit = tokens_values.shape[0] // sum(ROWS)
        self.mine = begin(tokens_values, tokens_scales, [sum(ROWS[:i]) * unit for i in range(len(ROWS) + 1)])
        self.last = self.mine[0]
        self.held = {}

    def run(self, order):
        for step in order:
            with jax.named_scope(step):
                getattr(self, step[:-1])(int(step[-1]))
        values, scales = self.held["end", len(ROWS) - 1]
        return values, scales.T

    def now(self, array):
        return lax.optimization_barrier((array, self.last))[0]

    def far(self, i):
        part = self.now(self.mine[i])
        self.held["far", i] = part, over_tp(part, 2)

    def sel(self, i):
        part, other = self.held["far", i]
        other = self.now(other)
        sent = jnp.where(self.same_half, other, part)
        kept = jnp.where(self.same_half, part, other)
        self.held["sel", i] = kept, over_seq(sent, 2)
        self.last = sent

    def arr(self, i):
        kept, got = self.held["sel", i]
        pair = arrange(self.first_x, kept, self.now(got))
        self.held["arr", i] = pair, over_both(pair, FIRST_IN), over_both(pair, SECOND)
        self.last = pair

    def take(self, i):
        pair, first, second = self.held["arr", i]
        first = self.now(first)
        own = jnp.where(self.even, pair, first)
        others = jnp.where(self.even, first, second)
        self.held["take", i] = self.last = arrange(self.first_core, own, others)

    def load(self, bits):
        gate_weight = self.now(self.gate_weight)
        self.held["load", bits] = self.last = load(gate_weight, self.up_weight, self.quarters[bits])

    def part(self, i, bits, got=None, kind=jnp.bfloat16, split=False):
        some = self.now(self.held["take", i])
        result = sums(some, self.held["load", bits], got, kind, split)
        self.last = result[0] if split else result
        return result

    def a(self, i):
        self.held["a", i] = over_seq(self.part(i, 3), 1)

    def c(self, i):
        self.held["c", i] = over_seq(self.part(i, 1), 1)

    def b(self, i):
        sent = self.part(i, 2, self.held["a", i], split=i in SPLIT)
        self.held["b", i] = [over_seq(part, 2) for part in (sent if i in SPLIT else (sent,))]

    def d(self, i):
        self.held["d", i] = self.part(i, 0, self.held["c", i], jnp.float32)

    def hide(self, i):
        hidden = hide(self.held["d", i], *(self.now(got) for got in self.held["b", i]))
        far = over_seq(hidden, 2)
        self.held["hide", i] = hidden, far, over_seq(hidden, 1)
        self.last = hidden

    def down(self, bits):
        self.held["down", bits] = self.last = load_rows(self.now(self.down_weight), self.pairs[bits // 2])

    def own(self, i):
        hidden, far, near = self.held["hide", i]
        self.held["own", i] = self.last = products((self.now(hidden), near), self.held["down", 0])

    def forward(self, i):
        far = self.now(self.held["hide", i][1])
        self.held["pass", i] = far, over_seq(far, 1)

    def rest(self, i):
        far, last = self.held["pass", i]
        self.held["rest", i] = self.last = products((self.now(far), last), self.held["down", 2], self.held["own", i])

    def out(self, i):
        partial_sum = self.now(self.held["rest", i])
        half = partial_sum.shape[0] // 2, partial_sum.shape[1]
        outs = (half, jnp.float32), (half, jnp.bfloat16), (half, jnp.bfloat16)
        own, one, two = small(out_kernel, outs, self.flags, partial_sum)
        self.held["out", i] = own, over_both(one, FIRST_OUT), over_both(two, SECOND)
        self.last = one

    def mix(self, i):
        own, first, second = self.held["out", i]
        shape = own.shape[0] // 2, own.shape[1]
        outs = (shape, jnp.float32), (shape, jnp.bfloat16)
        kept, sent = small(mix_kernel, outs, self.flags, own, self.now(first), second)
        self.held["mix", i] = kept, over_seq(sent, 2)
        self.last = sent

    def far_out(self, i):
        kept, got = self.held["mix", i]
        outs = (kept.shape, jnp.float32), (kept.shape, jnp.bfloat16)
        kept, sent = small(far_out_kernel, outs, self.flags, kept, self.now(got))
        self.held["far_out", i] = kept, over_tp(sent, 2)
        self.last = sent

    def end(self, i):
        kept, got = self.held["far_out", i]
        before = [self.held["end", k] for k in range(i)] if i == len(ROWS) - 1 else ()
        self.held["end", i] = end(kept, self.now(got), before)
        self.last = self.held["end", i][0]


def four_shards(*arrays):
    return Steps(*arrays).run(ORDER)


def solution(mesh):
    placed = (
        P(("groups", "seq"), "tp"),
        P(("groups", "seq"), "tp"),
        P("seq", "tp"),
        P("seq", "tp"),
        P("tp", "seq"),
    )
    fours = mesh.shape["tp"] == 4 and mesh.shape["seq"] == 4
    return jax.shard_map(
        four_shards if fours else any_shards,
        mesh=mesh,
        in_specs=placed,
        out_specs=(P(("groups", "seq"), "tp"), P(("groups", "seq"), "tp")),
        check_vma=False,
    )
```

```python
import functools

import jax
import jax.numpy as jnp
from jax import lax
from jax.experimental import pallas as pl
from jax.experimental.pallas import tpu as pltpu
from jax.sharding import PartitionSpec as P

ROWS = (48, 48, 32)
ORDER = (
    "far0", "load3", "sel0", "far1", "load1", "arr0", "load2", "load0", "sel1", "far2", "take0", "a0", "c0",
    "b0", "arr1", "d0", "sel2", "take1", "a1", "c1", "hide0", "b1", "arr2", "d1", "take2", "a2", "c2",
    "down0", "own0", "forward0", "hide1", "b2", "d2", "down2", "rest0", "out0", "forward1", "own1", "rest1",
    "out1", "hide2", "mix0", "mix1", "far_out0", "forward2", "own2", "rest2", "out2", "far_out1", "mix2",
    "end0", "far_out2", "end1", "end2",
)
TILE = 256
SPLIT = (0, 1)
COST = 1 << 34
LOAD_COST = 1 << 30
VMEM = 6 << 20


def blocks(array):
    return array.reshape(array.shape[0], array.shape[1] // 128, 128)


def block_scale(array):
    return jnp.max(jnp.abs(blocks(array)), axis=2) + 1e-06


def expand(values, scales):
    return (blocks(values.astype(jnp.float32)) * scales[:, :, None]).reshape(values.shape)


def scaled(total):
    scales = block_scale(total)
    values = (blocks(total) / scales[:, :, None]).reshape(total.shape).astype(jnp.bfloat16)
    return values, scales


def wide(array):
    return array.astype(jnp.float32)


def narrow(array):
    return array.astype(jnp.bfloat16)


def dot(a, b):
    return jnp.dot(a, b, preferred_element_type=jnp.float32)


def any_shards(tokens_values, tokens_scales, gate_weight, up_weight, down_weight):
    mine = narrow(expand(tokens_values, tokens_scales))
    mine = lax.all_gather(mine, "tp", axis=1, tiled=True)
    inputs = lax.all_to_all(mine, "seq", split_axis=1, concat_axis=0, tiled=True)
    gate = narrow(dot(inputs, gate_weight))
    up = narrow(dot(inputs, up_weight))
    gate = wide(lax.psum_scatter(gate, "seq", scatter_dimension=0, tiled=True))
    up = wide(lax.psum_scatter(up, "seq", scatter_dimension=0, tiled=True))
    hidden = narrow(jax.nn.silu(gate) * up)
    hidden = lax.all_gather(hidden, "seq", axis=0, tiled=True)
    partial_sum = narrow(dot(hidden, down_weight))
    partial_sum = lax.all_to_all(partial_sum, "seq", split_axis=0, concat_axis=1, tiled=True)
    return scaled(wide(lax.psum_scatter(partial_sum, "tp", scatter_dimension=1, tiled=True)))


def over_seq(array, bit):
    return lax.ppermute(array, "seq", [(i, i ^ bit) for i in range(4)])


def over_tp(array, bit):
    return lax.ppermute(array, "tp", [(i, i ^ bit) for i in range(4)])


def device(tp, seq):
    return tp * 4 + seq


FIRST_IN, SECOND, FIRST_OUT = [], [], []
for tp in range(4):
    for seq in range(4):
        if (tp ^ seq) & 1:
            FIRST_IN.append((device(tp, seq), device(tp, seq ^ 1)))
            SECOND.append((device(tp, seq), device(tp ^ 1, seq ^ 1)))
            FIRST_OUT.append((device(tp, seq), device(tp ^ 1, seq)))
        else:
            FIRST_IN.append((device(tp, seq), device(tp ^ 1, seq)))
            FIRST_OUT.append((device(tp, seq), device(tp, seq ^ 1)))


def over_both(array, pairs):
    return lax.ppermute(array, ("tp", "seq"), pairs)


def arrange(low_first, one, other):
    return jnp.concatenate([jnp.where(low_first, one, other), jnp.where(low_first, other, one)], axis=0)


def load_kernel(quarter, gate_weight, up_weight, out, done):
    width = out.shape[2]
    here = pl.ds(pl.multiple_of(quarter[0] * width, width), width)
    pieces = done.shape[1]
    rows = out.shape[1] // pieces
    copies = [
        pltpu.make_async_copy(weight.at[pl.ds(i * rows, rows), here], out.at[k, pl.ds(i * rows, rows)], done.at[k, i])
        for k, weight in enumerate((gate_weight, up_weight))
        for i in range(pieces)
    ]
    for copy in copies:
        copy.start()
    for copy in copies:
        copy.wait()


def load(gate_weight, up_weight, quarter):
    deep, width = gate_weight.shape
    far = pl.BlockSpec(memory_space=pl.ANY)
    return pl.pallas_call(
        load_kernel,
        out_shape=jax.ShapeDtypeStruct((2, deep, width // 4), gate_weight.dtype),
        in_specs=[pl.BlockSpec(memory_space=pltpu.SMEM), far, far],
        out_specs=pl.BlockSpec(memory_space=pltpu.VMEM),
        scratch_shapes=[pltpu.SemaphoreType.DMA((2, 4))],
        compiler_params=pltpu.CompilerParams(vmem_limit_bytes=VMEM),
        cost_estimate=pl.CostEstimate(flops=LOAD_COST, bytes_accessed=1, transcendentals=0),
    )(quarter, gate_weight, up_weight)


def sums_kernel(has_got, split, some, weights, *rest):
    def value(k):
        product = dot(some[...], weights[k])
        return product + wide(rest[0][k]) if has_got else product

    if split:
        for k, out in enumerate(rest[-2:]):
            out[...] = value(k).astype(out.dtype)
    else:

        @pl.loop(0, 2)
        def side(k):
            rest[-1][k] = value(k).astype(rest[-1].dtype)


def sums(some, weights, got=None, kind=jnp.bfloat16, split=False):
    near = pl.BlockSpec(memory_space=pltpu.VMEM)
    shape = some.shape[0], weights.shape[2]
    return pl.pallas_call(
        functools.partial(sums_kernel, got is not None, split),
        out_shape=(jax.ShapeDtypeStruct(shape, kind),) * 2 if split else jax.ShapeDtypeStruct((2,) + shape, kind),
        in_specs=[near] * (2 + (got is not None)),
        out_specs=(near, near) if split else near,
        compiler_params=pltpu.CompilerParams(vmem_limit_bytes=VMEM),
        cost_estimate=pl.CostEstimate(flops=COST, bytes_accessed=1, transcendentals=0),
    )(some, weights, *([] if got is None else [got]))


def load_rows_kernel(quarters, weight, out, done):
    rows = out.shape[1]
    pieces = done.shape[1]
    part = rows // pieces
    copies = [
        pltpu.make_async_copy(
            weight.at[pl.ds(pl.multiple_of(quarters[k] * rows + i * part, part), part)],
            out.at[k, pl.ds(i * part, part)],
            done.at[k, i],
        )
        for k in range(2)
        for i in range(pieces)
    ]
    for copy in copies:
        copy.start()
    for copy in copies:
        copy.wait()


def load_rows(weight, quarters):
    deep, width = weight.shape
    return pl.pallas_call(
        load_rows_kernel,
        out_shape=jax.ShapeDtypeStruct((2, deep // 4, width), weight.dtype),
        in_specs=[pl.BlockSpec(memory_space=pltpu.SMEM), pl.BlockSpec(memory_space=pl.ANY)],
        out_specs=pl.BlockSpec(memory_space=pltpu.VMEM),
        scratch_shapes=[pltpu.SemaphoreType.DMA((2, 4))],
        compiler_params=pltpu.CompilerParams(vmem_limit_bytes=VMEM),
        cost_estimate=pl.CostEstimate(flops=COST, bytes_accessed=1, transcendentals=0),
    )(quarters, weight)


def products_kernel(has_total, one, two, weights, *rest):
    tile = 4 * TILE

    @pl.loop(0, weights.shape[2] // tile)
    def strip(j):
        here = pl.ds(pl.multiple_of(j * tile, tile), tile)
        value = dot(one[...], weights[0, :, here]) + dot(two[...], weights[1, :, here])
        rest[-1][:, here] = value + rest[0][:, here] if has_total else value


def products(pieces, weights, total=None):
    near = pl.BlockSpec(memory_space=pltpu.VMEM)
    return pl.pallas_call(
        functools.partial(products_kernel, total is not None),
        out_shape=jax.ShapeDtypeStruct((pieces[0].shape[0], weights.shape[2]), jnp.float32),
        in_specs=[near] * (3 + (total is not None)),
        out_specs=near,
        compiler_params=pltpu.CompilerParams(vmem_limit_bytes=VMEM),
        cost_estimate=pl.CostEstimate(flops=COST, bytes_accessed=1, transcendentals=0),
    )(*pieces, weights, *([] if total is None else [total]))


def begin_kernel(starts, values, turned_scales, *outs):
    scales = turned_scales[...].T
    for j in range(scales.shape[1]):
        here = pl.ds(j * 128, 128)
        scaled_values = narrow(wide(values[:, here]) * scales[:, j : j + 1])
        for i, out in enumerate(outs):
            out[:, here] = scaled_values[starts[i] : starts[i + 1]]


def begin(values, scales, starts):
    near = pl.BlockSpec(memory_space=pltpu.VMEM)
    count = len(starts) - 1
    return pl.pallas_call(
        functools.partial(begin_kernel, starts),
        out_shape=[jax.ShapeDtypeStruct((starts[i + 1] - starts[i], values.shape[1]), values.dtype) for i in range(count)],
        in_specs=[near] * 2,
        out_specs=[near] * count,
        compiler_params=pltpu.CompilerParams(vmem_limit_bytes=VMEM),
        cost_estimate=pl.CostEstimate(flops=LOAD_COST, bytes_accessed=1, transcendentals=0),
    )(values, scales.T)


def hide_kernel(held, *rest):
    got, out = rest[:-1], rest[-1]
    got_gate, got_up = got if len(got) == 2 else (got[0].at[0], got[0].at[1])
    rows = 32

    @pl.loop(0, out.shape[0] // rows)
    def strip(i):
        here = pl.ds(pl.multiple_of(i * rows, rows), rows)
        gate = held[0, here] + wide(got_gate[here])
        up = held[1, here] + wide(got_up[here])
        out[here] = narrow(jax.nn.silu(gate) * up)


def hide(held, *got):
    near = pl.BlockSpec(memory_space=pltpu.VMEM)
    return pl.pallas_call(
        hide_kernel,
        out_shape=jax.ShapeDtypeStruct(held.shape[1:], got[0].dtype),
        in_specs=[near] * (1 + len(got)),
        out_specs=near,
        compiler_params=pltpu.CompilerParams(vmem_limit_bytes=VMEM),
        cost_estimate=pl.CostEstimate(flops=COST, bytes_accessed=1, transcendentals=0),
    )(held, *got)


def end_kernel(count, kept, got, *rest):
    before, (values, scales) = rest[: 2 * count], rest[2 * count :]
    first = sum(part.shape[0] for part in before[::2])
    rows = pl.ds(first, kept.shape[0])
    columns = []
    for j in range(kept.shape[1] // 128):
        here = pl.ds(j * 128, 128)
        total = kept[:, here] + wide(got[:, here])
        scale = jnp.max(jnp.abs(total), axis=1, keepdims=True) + 1e-06
        values[rows, here] = narrow(total / scale)
        columns.append(scale)
    ended = jnp.concatenate(columns, axis=1)
    if not count:
        scales[...] = ended
        return
    row = 0
    for part in before[::2]:
        values[pl.ds(row, part.shape[0])] = part[...]
        row += part.shape[0]
    scales[...] = jnp.concatenate([part[...] for part in before[1::2]] + [ended], axis=0).T


def end(kept, got, before=()):
    rows, width = kept.shape
    count = len(before)
    rows += sum(values.shape[0] for values, scales in before)
    near = pl.BlockSpec(memory_space=pltpu.VMEM)
    shape = (width // 128, rows) if count else (rows, width // 128)
    return pl.pallas_call(
        functools.partial(end_kernel, count),
        out_shape=(jax.ShapeDtypeStruct((rows, width), got.dtype), jax.ShapeDtypeStruct(shape, kept.dtype)),
        in_specs=[near] * (2 + 2 * count),
        out_specs=(near, near),
        compiler_params=pltpu.CompilerParams(vmem_limit_bytes=VMEM),
        cost_estimate=pl.CostEstimate(flops=COST, bytes_accessed=1, transcendentals=0),
    )(kept, got, *(array for pair in before for array in pair))


def small(kernel, outs, flags, *arrays):
    near = pl.BlockSpec(memory_space=pltpu.VMEM)
    return pl.pallas_call(
        kernel,
        out_shape=[jax.ShapeDtypeStruct(*out) for out in outs],
        in_specs=[pl.BlockSpec(memory_space=pltpu.SMEM)] + [near] * len(arrays),
        out_specs=[near] * len(outs),
        compiler_params=pltpu.CompilerParams(vmem_limit_bytes=VMEM),
        cost_estimate=pl.CostEstimate(flops=COST, bytes_accessed=1, transcendentals=0),
    )(flags, *arrays)


def strips(array):
    return pl.loop(0, array.shape[1] // TILE)


def out_kernel(flags, partial_sum, own, one, two):
    half = own.shape[0]
    low, top = pl.ds(0, half), pl.ds(half, half)

    @strips(own)
    def strip(j):
        here = pl.ds(pl.multiple_of(j * TILE, TILE), TILE)
        first, last = partial_sum[low, here], partial_sum[top, here]
        mine = jnp.where(flags[1] == 1, first, last)
        others = jnp.where(flags[1] == 1, last, first)
        own[:, here] = mine
        one[:, here] = narrow(jnp.where(flags[2] == 1, others, mine))
        two[:, here] = narrow(others)


def mix_kernel(flags, own, got_one, got_two, kept, sent):
    rows = kept.shape[0]

    @strips(own)
    def strip(j):
        here = pl.ds(pl.multiple_of(j * TILE, TILE), TILE)
        pair = wide(got_one[:, here]) + jnp.where(flags[2] == 1, own[:, here], wide(got_two[:, here]))
        kept[:, here] = jnp.where(flags[0] == 1, pair[:rows], pair[rows:])
        sent[:, here] = narrow(jnp.where(flags[0] == 1, pair[rows:], pair[:rows]))


def far_out_kernel(flags, kept, got, still, sent):
    @strips(kept)
    def strip(j):
        here = pl.ds(pl.multiple_of(j * TILE, TILE), TILE)
        mine, other = kept[:, here], wide(got[:, here])
        still[:, here] = jnp.where(flags[3] == 1, mine, other)
        sent[:, here] = narrow(jnp.where(flags[3] == 1, other, mine))


class Steps:

    def __init__(self, tokens_values, tokens_scales, gate_weight, up_weight, down_weight):
        tp, seq = lax.axis_index("tp"), lax.axis_index("seq")
        x, core, high = seq >> 1, seq & 1, tp >> 1
        facts = x == 0, core == 0, (tp ^ seq) & 1 == 0, high == x
        quarters = [(seq ^ bits).reshape(1) for bits in range(4)]
        pairs = [jnp.stack([seq ^ bits, seq ^ bits ^ 1]) for bits in (0, 2)]
        flags = jnp.stack(facts).astype(jnp.int32)
        facts, self.flags, self.quarters, self.pairs, gate_weight = lax.optimization_barrier(
            (facts, flags, quarters, pairs, gate_weight)
        )
        self.first_x, self.first_core, self.even, self.same_half = facts
        self.gate_weight = pltpu.with_memory_space_constraint(gate_weight, pltpu.HBM)
        self.up_weight = pltpu.with_memory_space_constraint(up_weight, pltpu.HBM)
        self.down_weight = pltpu.with_memory_space_constraint(down_weight, pltpu.HBM)
        unit = tokens_values.shape[0] // sum(ROWS)
        self.mine = begin(tokens_values, tokens_scales, [sum(ROWS[:i]) * unit for i in range(len(ROWS) + 1)])
        self.last = self.mine[0]
        self.held = {}

    def run(self, order):
        for step in order:
            with jax.named_scope(step):
                getattr(self, step[:-1])(int(step[-1]))
        values, scales = self.held["end", len(ROWS) - 1]
        return values, scales.T

    def now(self, array):
        return lax.optimization_barrier((array, self.last))[0]

    def far(self, i):
        part = self.now(self.mine[i])
        self.held["far", i] = part, over_tp(part, 2)

    def sel(self, i):
        part, other = self.held["far", i]
        other = self.now(other)
        sent = jnp.where(self.same_half, other, part)
        kept = jnp.where(self.same_half, part, other)
        self.held["sel", i] = kept, over_seq(sent, 2)
        self.last = sent

    def arr(self, i):
        kept, got = self.held["sel", i]
        pair = arrange(self.first_x, kept, self.now(got))
        self.held["arr", i] = pair, over_both(pair, FIRST_IN), over_both(pair, SECOND)
        self.last = pair

    def take(self, i):
        pair, first, second = self.held["arr", i]
        first = self.now(first)
        own = jnp.where(self.even, pair, first)
        others = jnp.where(self.even, first, second)
        self.held["take", i] = self.last = arrange(self.first_core, own, others)

    def load(self, bits):
        gate_weight = self.now(self.gate_weight)
        self.held["load", bits] = self.last = load(gate_weight, self.up_weight, self.quarters[bits])

    def part(self, i, bits, got=None, kind=jnp.bfloat16, split=False):
        some = self.now(self.held["take", i])
        result = sums(some, self.held["load", bits], got, kind, split)
        self.last = result[0] if split else result
        return result

    def a(self, i):
        self.held["a", i] = over_seq(self.part(i, 3), 1)

    def c(self, i):
        self.held["c", i] = over_seq(self.part(i, 1), 1)

    def b(self, i):
        sent = self.part(i, 2, self.held["a", i], split=i in SPLIT)
        self.held["b", i] = [over_seq(part, 2) for part in (sent if i in SPLIT else (sent,))]

    def d(self, i):
        self.held["d", i] = self.part(i, 0, self.held["c", i], jnp.float32)

    def hide(self, i):
        hidden = hide(self.held["d", i], *(self.now(got) for got in self.held["b", i]))
        far = over_seq(hidden, 2)
        self.held["hide", i] = hidden, far, over_seq(hidden, 1)
        self.last = hidden

    def down(self, bits):
        self.held["down", bits] = self.last = load_rows(self.now(self.down_weight), self.pairs[bits // 2])

    def own(self, i):
        hidden, far, near = self.held["hide", i]
        self.held["own", i] = self.last = products((self.now(hidden), near), self.held["down", 0])

    def forward(self, i):
        far = self.now(self.held["hide", i][1])
        self.held["pass", i] = far, over_seq(far, 1)

    def rest(self, i):
        far, last = self.held["pass", i]
        self.held["rest", i] = self.last = products((self.now(far), last), self.held["down", 2], self.held["own", i])

    def out(self, i):
        partial_sum = self.now(self.held["rest", i])
        half = partial_sum.shape[0] // 2, partial_sum.shape[1]
        outs = (half, jnp.float32), (half, jnp.bfloat16), (half, jnp.bfloat16)
        own, one, two = small(out_kernel, outs, self.flags, partial_sum)
        self.held["out", i] = own, over_both(one, FIRST_OUT), over_both(two, SECOND)
        self.last = one

    def mix(self, i):
        own, first, second = self.held["out", i]
        shape = own.shape[0] // 2, own.shape[1]
        outs = (shape, jnp.float32), (shape, jnp.bfloat16)
        kept, sent = small(mix_kernel, outs, self.flags, own, self.now(first), second)
        self.held["mix", i] = kept, over_seq(sent, 2)
        self.last = sent

    def far_out(self, i):
        kept, got = self.held["mix", i]
        outs = (kept.shape, jnp.float32), (kept.shape, jnp.bfloat16)
        kept, sent = small(far_out_kernel, outs, self.flags, kept, self.now(got))
        self.held["far_out", i] = kept, over_tp(sent, 2)
        self.last = sent

    def end(self, i):
        kept, got = self.held["far_out", i]
        before = [self.held["end", k] for k in range(i)] if i == len(ROWS) - 1 else ()
        self.held["end", i] = end(kept, self.now(got), before)
        self.last = self.held["end", i][0]


def four_shards(*arrays):
    return Steps(*arrays).run(ORDER)


def solution(mesh):
    placed = (
        P(("groups", "seq"), "tp"),
        P(("groups", "seq"), "tp"),
        P("seq", "tp"),
        P("seq", "tp"),
        P("tp", "seq"),
    )
    fours = mesh.shape["tp"] == 4 and mesh.shape["seq"] == 4
    return jax.shard_map(
        four_shards if fours else any_shards,
        mesh=mesh,
        in_specs=placed,
        out_specs=(P(("groups", "seq"), "tp"), P(("groups", "seq"), "tp")),
        check_vma=False,
    )
```

```python
import functools

import jax
import jax.numpy as jnp
from jax import lax
from jax.experimental import pallas as pl
from jax.experimental.pallas import tpu as pltpu
from jax.sharding import PartitionSpec as P

ROWS = (48, 48, 32)
ORDER = (
    "far0", "load3", "sel0", "far1", "load1", "arr0", "load2", "load0", "sel1", "far2", "take0", "a0", "c0",
    "b0", "arr1", "d0", "sel2", "take1", "a1", "c1", "hide0", "b1", "arr2", "d1", "take2", "a2", "c2",
    "down0", "own0", "forward0", "down2", "rest0", "out0", "hide1", "b2", "d2", "forward1", "own1", "mix0",
    "rest1", "out1", "hide2", "far_out0", "mix1", "forward2", "own2", "rest2", "out2", "far_out1", "mix2",
    "end0", "far_out2", "end1", "end2",
)
TILE = 256
SPLIT = (0, 1)
COST = 1 << 34
LOAD_COST = 1 << 30
VMEM = 6 << 20


def blocks(array):
    return array.reshape(array.shape[0], array.shape[1] // 128, 128)


def block_scale(array):
    return jnp.max(jnp.abs(blocks(array)), axis=2) + 1e-06


def expand(values, scales):
    return (blocks(values.astype(jnp.float32)) * scales[:, :, None]).reshape(values.shape)


def scaled(total):
    scales = block_scale(total)
    values = (blocks(total) / scales[:, :, None]).reshape(total.shape).astype(jnp.bfloat16)
    return values, scales


def wide(array):
    return array.astype(jnp.float32)


def narrow(array):
    return array.astype(jnp.bfloat16)


def dot(a, b):
    return jnp.dot(a, b, preferred_element_type=jnp.float32)


def any_shards(tokens_values, tokens_scales, gate_weight, up_weight, down_weight):
    mine = narrow(expand(tokens_values, tokens_scales))
    mine = lax.all_gather(mine, "tp", axis=1, tiled=True)
    inputs = lax.all_to_all(mine, "seq", split_axis=1, concat_axis=0, tiled=True)
    gate = narrow(dot(inputs, gate_weight))
    up = narrow(dot(inputs, up_weight))
    gate = wide(lax.psum_scatter(gate, "seq", scatter_dimension=0, tiled=True))
    up = wide(lax.psum_scatter(up, "seq", scatter_dimension=0, tiled=True))
    hidden = narrow(jax.nn.silu(gate) * up)
    hidden = lax.all_gather(hidden, "seq", axis=0, tiled=True)
    partial_sum = narrow(dot(hidden, down_weight))
    partial_sum = lax.all_to_all(partial_sum, "seq", split_axis=0, concat_axis=1, tiled=True)
    return scaled(wide(lax.psum_scatter(partial_sum, "tp", scatter_dimension=1, tiled=True)))


def over_seq(array, bit):
    return lax.ppermute(array, "seq", [(i, i ^ bit) for i in range(4)])


def over_tp(array, bit):
    return lax.ppermute(array, "tp", [(i, i ^ bit) for i in range(4)])


def device(tp, seq):
    return tp * 4 + seq


FIRST_IN, SECOND, FIRST_OUT = [], [], []
for tp in range(4):
    for seq in range(4):
        if (tp ^ seq) & 1:
            FIRST_IN.append((device(tp, seq), device(tp, seq ^ 1)))
            SECOND.append((device(tp, seq), device(tp ^ 1, seq ^ 1)))
            FIRST_OUT.append((device(tp, seq), device(tp ^ 1, seq)))
        else:
            FIRST_IN.append((device(tp, seq), device(tp ^ 1, seq)))
            FIRST_OUT.append((device(tp, seq), device(tp, seq ^ 1)))


def over_both(array, pairs):
    return lax.ppermute(array, ("tp", "seq"), pairs)


def arrange(low_first, one, other):
    return jnp.concatenate([jnp.where(low_first, one, other), jnp.where(low_first, other, one)], axis=0)


def load_kernel(quarter, gate_weight, up_weight, out, done):
    width = out.shape[2]
    here = pl.ds(pl.multiple_of(quarter[0] * width, width), width)
    pieces = done.shape[1]
    rows = out.shape[1] // pieces
    copies = [
        pltpu.make_async_copy(weight.at[pl.ds(i * rows, rows), here], out.at[k, pl.ds(i * rows, rows)], done.at[k, i])
        for k, weight in enumerate((gate_weight, up_weight))
        for i in range(pieces)
    ]
    for copy in copies:
        copy.start()
    for copy in copies:
        copy.wait()


def load(gate_weight, up_weight, quarter):
    deep, width = gate_weight.shape
    far = pl.BlockSpec(memory_space=pl.ANY)
    return pl.pallas_call(
        load_kernel,
        out_shape=jax.ShapeDtypeStruct((2, deep, width // 4), gate_weight.dtype),
        in_specs=[pl.BlockSpec(memory_space=pltpu.SMEM), far, far],
        out_specs=pl.BlockSpec(memory_space=pltpu.VMEM),
        scratch_shapes=[pltpu.SemaphoreType.DMA((2, 4))],
        compiler_params=pltpu.CompilerParams(vmem_limit_bytes=VMEM),
        cost_estimate=pl.CostEstimate(flops=LOAD_COST, bytes_accessed=1, transcendentals=0),
    )(quarter, gate_weight, up_weight)


def sums_kernel(has_got, split, some, weights, *rest):
    def value(k):
        product = dot(some[...], weights[k])
        return product + wide(rest[0][k]) if has_got else product

    if split:
        for k, out in enumerate(rest[-2:]):
            out[...] = value(k).astype(out.dtype)
    else:

        @pl.loop(0, 2)
        def side(k):
            rest[-1][k] = value(k).astype(rest[-1].dtype)


def sums(some, weights, got=None, kind=jnp.bfloat16, split=False):
    near = pl.BlockSpec(memory_space=pltpu.VMEM)
    shape = some.shape[0], weights.shape[2]
    return pl.pallas_call(
        functools.partial(sums_kernel, got is not None, split),
        out_shape=(jax.ShapeDtypeStruct(shape, kind),) * 2 if split else jax.ShapeDtypeStruct((2,) + shape, kind),
        in_specs=[near] * (2 + (got is not None)),
        out_specs=(near, near) if split else near,
        compiler_params=pltpu.CompilerParams(vmem_limit_bytes=VMEM),
        cost_estimate=pl.CostEstimate(flops=COST, bytes_accessed=1, transcendentals=0),
    )(some, weights, *([] if got is None else [got]))


def load_rows_kernel(quarters, weight, out, done):
    rows = out.shape[1]
    pieces = done.shape[1]
    part = rows // pieces
    copies = [
        pltpu.make_async_copy(
            weight.at[pl.ds(pl.multiple_of(quarters[k] * rows + i * part, part), part)],
            out.at[k, pl.ds(i * part, part)],
            done.at[k, i],
        )
        for k in range(2)
        for i in range(pieces)
    ]
    for copy in copies:
        copy.start()
    for copy in copies:
        copy.wait()


def load_rows(weight, quarters):
    deep, width = weight.shape
    return pl.pallas_call(
        load_rows_kernel,
        out_shape=jax.ShapeDtypeStruct((2, deep // 4, width), weight.dtype),
        in_specs=[pl.BlockSpec(memory_space=pltpu.SMEM), pl.BlockSpec(memory_space=pl.ANY)],
        out_specs=pl.BlockSpec(memory_space=pltpu.VMEM),
        scratch_shapes=[pltpu.SemaphoreType.DMA((2, 4))],
        compiler_params=pltpu.CompilerParams(vmem_limit_bytes=VMEM),
        cost_estimate=pl.CostEstimate(flops=COST, bytes_accessed=1, transcendentals=0),
    )(quarters, weight)


def products_kernel(has_total, one, two, weights, *rest):
    tile = 4 * TILE

    @pl.loop(0, weights.shape[2] // tile)
    def strip(j):
        here = pl.ds(pl.multiple_of(j * tile, tile), tile)
        value = dot(one[...], weights[0, :, here]) + dot(two[...], weights[1, :, here])
        rest[-1][:, here] = value + rest[0][:, here] if has_total else value


def products(pieces, weights, total=None):
    near = pl.BlockSpec(memory_space=pltpu.VMEM)
    return pl.pallas_call(
        functools.partial(products_kernel, total is not None),
        out_shape=jax.ShapeDtypeStruct((pieces[0].shape[0], weights.shape[2]), jnp.float32),
        in_specs=[near] * (3 + (total is not None)),
        out_specs=near,
        compiler_params=pltpu.CompilerParams(vmem_limit_bytes=VMEM),
        cost_estimate=pl.CostEstimate(flops=COST, bytes_accessed=1, transcendentals=0),
    )(*pieces, weights, *([] if total is None else [total]))


def begin_kernel(starts, values, turned_scales, *outs):
    scales = turned_scales[...].T
    for j in range(scales.shape[1]):
        here = pl.ds(j * 128, 128)
        scaled_values = narrow(wide(values[:, here]) * scales[:, j : j + 1])
        for i, out in enumerate(outs):
            out[:, here] = scaled_values[starts[i] : starts[i + 1]]


def begin(values, scales, starts):
    near = pl.BlockSpec(memory_space=pltpu.VMEM)
    count = len(starts) - 1
    return pl.pallas_call(
        functools.partial(begin_kernel, starts),
        out_shape=[jax.ShapeDtypeStruct((starts[i + 1] - starts[i], values.shape[1]), values.dtype) for i in range(count)],
        in_specs=[near] * 2,
        out_specs=[near] * count,
        compiler_params=pltpu.CompilerParams(vmem_limit_bytes=VMEM),
        cost_estimate=pl.CostEstimate(flops=LOAD_COST, bytes_accessed=1, transcendentals=0),
    )(values, scales.T)


def hide_kernel(held, *rest):
    got, out = rest[:-1], rest[-1]
    got_gate, got_up = got if len(got) == 2 else (got[0].at[0], got[0].at[1])
    rows = 32

    @pl.loop(0, out.shape[0] // rows)
    def strip(i):
        here = pl.ds(pl.multiple_of(i * rows, rows), rows)
        gate = held[0, here] + wide(got_gate[here])
        up = held[1, here] + wide(got_up[here])
        out[here] = narrow(jax.nn.silu(gate) * up)


def hide(held, *got):
    near = pl.BlockSpec(memory_space=pltpu.VMEM)
    return pl.pallas_call(
        hide_kernel,
        out_shape=jax.ShapeDtypeStruct(held.shape[1:], got[0].dtype),
        in_specs=[near] * (1 + len(got)),
        out_specs=near,
        compiler_params=pltpu.CompilerParams(vmem_limit_bytes=VMEM),
        cost_estimate=pl.CostEstimate(flops=COST, bytes_accessed=1, transcendentals=0),
    )(held, *got)


def end_kernel(count, kept, got, *rest):
    before, (values, scales) = rest[: 2 * count], rest[2 * count :]
    first = sum(part.shape[0] for part in before[::2])
    rows = pl.ds(first, kept.shape[0])
    columns = []
    for j in range(kept.shape[1] // 128):
        here = pl.ds(j * 128, 128)
        total = kept[:, here] + wide(got[:, here])
        scale = jnp.max(jnp.abs(total), axis=1, keepdims=True) + 1e-06
        values[rows, here] = narrow(total / scale)
        columns.append(scale)
    ended = jnp.concatenate(columns, axis=1)
    if not count:
        scales[...] = ended
        return
    row = 0
    for part in before[::2]:
        values[pl.ds(row, part.shape[0])] = part[...]
        row += part.shape[0]
    scales[...] = jnp.concatenate([part[...] for part in before[1::2]] + [ended], axis=0).T


def end(kept, got, before=()):
    rows, width = kept.shape
    count = len(before)
    rows += sum(values.shape[0] for values, scales in before)
    near = pl.BlockSpec(memory_space=pltpu.VMEM)
    shape = (width // 128, rows) if count else (rows, width // 128)
    return pl.pallas_call(
        functools.partial(end_kernel, count),
        out_shape=(jax.ShapeDtypeStruct((rows, width), got.dtype), jax.ShapeDtypeStruct(shape, kept.dtype)),
        in_specs=[near] * (2 + 2 * count),
        out_specs=(near, near),
        compiler_params=pltpu.CompilerParams(vmem_limit_bytes=VMEM),
        cost_estimate=pl.CostEstimate(flops=COST, bytes_accessed=1, transcendentals=0),
    )(kept, got, *(array for pair in before for array in pair))


def small(kernel, outs, flags, *arrays):
    near = pl.BlockSpec(memory_space=pltpu.VMEM)
    return pl.pallas_call(
        kernel,
        out_shape=[jax.ShapeDtypeStruct(*out) for out in outs],
        in_specs=[pl.BlockSpec(memory_space=pltpu.SMEM)] + [near] * len(arrays),
        out_specs=[near] * len(outs),
        compiler_params=pltpu.CompilerParams(vmem_limit_bytes=VMEM),
        cost_estimate=pl.CostEstimate(flops=COST, bytes_accessed=1, transcendentals=0),
    )(flags, *arrays)


def strips(array):
    return pl.loop(0, array.shape[1] // TILE)


def out_kernel(flags, partial_sum, own, one, two):
    half = own.shape[0]
    low, top = pl.ds(0, half), pl.ds(half, half)

    @strips(own)
    def strip(j):
        here = pl.ds(pl.multiple_of(j * TILE, TILE), TILE)
        first, last = partial_sum[low, here], partial_sum[top, here]
        mine = jnp.where(flags[1] == 1, first, last)
        others = jnp.where(flags[1] == 1, last, first)
        own[:, here] = mine
        one[:, here] = narrow(jnp.where(flags[2] == 1, others, mine))
        two[:, here] = narrow(others)


def mix_kernel(flags, own, got_one, got_two, kept, sent):
    rows = kept.shape[0]

    @strips(own)
    def strip(j):
        here = pl.ds(pl.multiple_of(j * TILE, TILE), TILE)
        pair = wide(got_one[:, here]) + jnp.where(flags[2] == 1, own[:, here], wide(got_two[:, here]))
        kept[:, here] = jnp.where(flags[0] == 1, pair[:rows], pair[rows:])
        sent[:, here] = narrow(jnp.where(flags[0] == 1, pair[rows:], pair[:rows]))


def far_out_kernel(flags, kept, got, still, sent):
    @strips(kept)
    def strip(j):
        here = pl.ds(pl.multiple_of(j * TILE, TILE), TILE)
        mine, other = kept[:, here], wide(got[:, here])
        still[:, here] = jnp.where(flags[3] == 1, mine, other)
        sent[:, here] = narrow(jnp.where(flags[3] == 1, other, mine))


class Steps:

    def __init__(self, tokens_values, tokens_scales, gate_weight, up_weight, down_weight):
        tp, seq = lax.axis_index("tp"), lax.axis_index("seq")
        x, core, high = seq >> 1, seq & 1, tp >> 1
        facts = x == 0, core == 0, (tp ^ seq) & 1 == 0, high == x
        quarters = [(seq ^ bits).reshape(1) for bits in range(4)]
        pairs = [jnp.stack([seq ^ bits, seq ^ bits ^ 1]) for bits in (0, 2)]
        flags = jnp.stack(facts).astype(jnp.int32)
        facts, self.flags, self.quarters, self.pairs, gate_weight = lax.optimization_barrier(
            (facts, flags, quarters, pairs, gate_weight)
        )
        self.first_x, self.first_core, self.even, self.same_half = facts
        self.gate_weight = pltpu.with_memory_space_constraint(gate_weight, pltpu.HBM)
        self.up_weight = pltpu.with_memory_space_constraint(up_weight, pltpu.HBM)
        self.down_weight = pltpu.with_memory_space_constraint(down_weight, pltpu.HBM)
        unit = tokens_values.shape[0] // sum(ROWS)
        self.mine = begin(tokens_values, tokens_scales, [sum(ROWS[:i]) * unit for i in range(len(ROWS) + 1)])
        self.last = self.mine[0]
        self.held = {}

    def run(self, order):
        for step in order:
            with jax.named_scope(step):
                getattr(self, step[:-1])(int(step[-1]))
        values, scales = self.held["end", len(ROWS) - 1]
        return values, scales.T

    def now(self, array):
        return lax.optimization_barrier((array, self.last))[0]

    def far(self, i):
        part = self.now(self.mine[i])
        self.held["far", i] = part, over_tp(part, 2)

    def sel(self, i):
        part, other = self.held["far", i]
        other = self.now(other)
        sent = jnp.where(self.same_half, other, part)
        kept = jnp.where(self.same_half, part, other)
        self.held["sel", i] = kept, over_seq(sent, 2)
        self.last = sent

    def arr(self, i):
        kept, got = self.held["sel", i]
        pair = arrange(self.first_x, kept, self.now(got))
        self.held["arr", i] = pair, over_both(pair, FIRST_IN), over_both(pair, SECOND)
        self.last = pair

    def take(self, i):
        pair, first, second = self.held["arr", i]
        first = self.now(first)
        own = jnp.where(self.even, pair, first)
        others = jnp.where(self.even, first, second)
        self.held["take", i] = self.last = arrange(self.first_core, own, others)

    def load(self, bits):
        gate_weight = self.now(self.gate_weight)
        self.held["load", bits] = self.last = load(gate_weight, self.up_weight, self.quarters[bits])

    def part(self, i, bits, got=None, kind=jnp.bfloat16, split=False):
        some = self.now(self.held["take", i])
        result = sums(some, self.held["load", bits], got, kind, split)
        self.last = result[0] if split else result
        return result

    def a(self, i):
        self.held["a", i] = over_seq(self.part(i, 3), 1)

    def c(self, i):
        self.held["c", i] = over_seq(self.part(i, 1), 1)

    def b(self, i):
        sent = self.part(i, 2, self.held["a", i], split=i in SPLIT)
        self.held["b", i] = [over_seq(part, 2) for part in (sent if i in SPLIT else (sent,))]

    def d(self, i):
        self.held["d", i] = self.part(i, 0, self.held["c", i], jnp.float32)

    def hide(self, i):
        hidden = hide(self.held["d", i], *(self.now(got) for got in self.held["b", i]))
        far = over_seq(hidden, 2)
        self.held["hide", i] = hidden, far, over_seq(hidden, 1)
        self.last = hidden

    def down(self, bits):
        self.held["down", bits] = self.last = load_rows(self.now(self.down_weight), self.pairs[bits // 2])

    def own(self, i):
        hidden, far, near = self.held["hide", i]
        self.held["own", i] = self.last = products((self.now(hidden), near), self.held["down", 0])

    def forward(self, i):
        far = self.now(self.held["hide", i][1])
        self.held["pass", i] = far, over_seq(far, 1)

    def rest(self, i):
        far, last = self.held["pass", i]
        self.held["rest", i] = self.last = products((self.now(far), last), self.held["down", 2], self.held["own", i])

    def out(self, i):
        partial_sum = self.now(self.held["rest", i])
        half = partial_sum.shape[0] // 2, partial_sum.shape[1]
        outs = (half, jnp.float32), (half, jnp.bfloat16), (half, jnp.bfloat16)
        own, one, two = small(out_kernel, outs, self.flags, partial_sum)
        self.held["out", i] = own, over_both(one, FIRST_OUT), over_both(two, SECOND)
        self.last = one

    def mix(self, i):
        own, first, second = self.held["out", i]
        shape = own.shape[0] // 2, own.shape[1]
        outs = (shape, jnp.float32), (shape, jnp.bfloat16)
        kept, sent = small(mix_kernel, outs, self.flags, own, self.now(first), second)
        self.held["mix", i] = kept, over_seq(sent, 2)
        self.last = sent

    def far_out(self, i):
        kept, got = self.held["mix", i]
        outs = (kept.shape, jnp.float32), (kept.shape, jnp.bfloat16)
        kept, sent = small(far_out_kernel, outs, self.flags, kept, self.now(got))
        self.held["far_out", i] = kept, over_tp(sent, 2)
        self.last = sent

    def end(self, i):
        kept, got = self.held["far_out", i]
        before = [self.held["end", k] for k in range(i)] if i == len(ROWS) - 1 else ()
        self.held["end", i] = end(kept, self.now(got), before)
        self.last = self.held["end", i][0]


def four_shards(*arrays):
    return Steps(*arrays).run(ORDER)


def solution(mesh):
    placed = (
        P(("groups", "seq"), "tp"),
        P(("groups", "seq"), "tp"),
        P("seq", "tp"),
        P("seq", "tp"),
        P("tp", "seq"),
    )
    fours = mesh.shape["tp"] == 4 and mesh.shape["seq"] == 4
    return jax.shard_map(
        four_shards if fours else any_shards,
        mesh=mesh,
        in_specs=placed,
        out_specs=(P(("groups", "seq"), "tp"), P(("groups", "seq"), "tp")),
        check_vma=False,
    )
```

```python
import functools

import jax
import jax.numpy as jnp
from jax import lax
from jax.experimental import pallas as pl
from jax.experimental.pallas import tpu as pltpu
from jax.sharding import PartitionSpec as P

ROWS = (48, 48, 32)
ORDER = (
    "far0", "load3", "sel0", "far1", "load1", "arr0", "load2", "load0", "sel1", "far2", "take0", "a0", "c0",
    "b0", "arr1", "d0", "sel2", "take1", "a1", "c1", "hide0", "b1", "arr2", "d1", "take2", "a2", "c2",
    "down0", "own0", "forward0", "hide1", "b2", "d2", "down2", "own1", "rest0", "forward1", "out0", "rest1",
    "out1", "hide2", "mix0", "mix1", "forward2", "own2", "rest2", "out2", "far_out0", "mix2", "far_out1",
    "far_out2", "end0", "end1", "end2",
)
TILE = 256
SPLIT = (0, 1)
COST = 1 << 34
LOAD_COST = 1 << 30
VMEM = 6 << 20


def blocks(array):
    return array.reshape(array.shape[0], array.shape[1] // 128, 128)


def block_scale(array):
    return jnp.max(jnp.abs(blocks(array)), axis=2) + 1e-06


def expand(values, scales):
    return (blocks(values.astype(jnp.float32)) * scales[:, :, None]).reshape(values.shape)


def scaled(total):
    scales = block_scale(total)
    values = (blocks(total) / scales[:, :, None]).reshape(total.shape).astype(jnp.bfloat16)
    return values, scales


def wide(array):
    return array.astype(jnp.float32)


def narrow(array):
    return array.astype(jnp.bfloat16)


def dot(a, b):
    return jnp.dot(a, b, preferred_element_type=jnp.float32)


def any_shards(tokens_values, tokens_scales, gate_weight, up_weight, down_weight):
    mine = narrow(expand(tokens_values, tokens_scales))
    mine = lax.all_gather(mine, "tp", axis=1, tiled=True)
    inputs = lax.all_to_all(mine, "seq", split_axis=1, concat_axis=0, tiled=True)
    gate = narrow(dot(inputs, gate_weight))
    up = narrow(dot(inputs, up_weight))
    gate = wide(lax.psum_scatter(gate, "seq", scatter_dimension=0, tiled=True))
    up = wide(lax.psum_scatter(up, "seq", scatter_dimension=0, tiled=True))
    hidden = narrow(jax.nn.silu(gate) * up)
    hidden = lax.all_gather(hidden, "seq", axis=0, tiled=True)
    partial_sum = narrow(dot(hidden, down_weight))
    partial_sum = lax.all_to_all(partial_sum, "seq", split_axis=0, concat_axis=1, tiled=True)
    return scaled(wide(lax.psum_scatter(partial_sum, "tp", scatter_dimension=1, tiled=True)))


def over_seq(array, bit):
    return lax.ppermute(array, "seq", [(i, i ^ bit) for i in range(4)])


def over_tp(array, bit):
    return lax.ppermute(array, "tp", [(i, i ^ bit) for i in range(4)])


def device(tp, seq):
    return tp * 4 + seq


FIRST_IN, SECOND, FIRST_OUT = [], [], []
for tp in range(4):
    for seq in range(4):
        if (tp ^ seq) & 1:
            FIRST_IN.append((device(tp, seq), device(tp, seq ^ 1)))
            SECOND.append((device(tp, seq), device(tp ^ 1, seq ^ 1)))
            FIRST_OUT.append((device(tp, seq), device(tp ^ 1, seq)))
        else:
            FIRST_IN.append((device(tp, seq), device(tp ^ 1, seq)))
            FIRST_OUT.append((device(tp, seq), device(tp, seq ^ 1)))


def over_both(array, pairs):
    return lax.ppermute(array, ("tp", "seq"), pairs)


def arrange(low_first, one, other):
    return jnp.concatenate([jnp.where(low_first, one, other), jnp.where(low_first, other, one)], axis=0)


def load_kernel(quarter, gate_weight, up_weight, out, done):
    width = out.shape[2]
    here = pl.ds(pl.multiple_of(quarter[0] * width, width), width)
    pieces = done.shape[1]
    rows = out.shape[1] // pieces
    copies = [
        pltpu.make_async_copy(weight.at[pl.ds(i * rows, rows), here], out.at[k, pl.ds(i * rows, rows)], done.at[k, i])
        for k, weight in enumerate((gate_weight, up_weight))
        for i in range(pieces)
    ]
    for copy in copies:
        copy.start()
    for copy in copies:
        copy.wait()


def load(gate_weight, up_weight, quarter):
    deep, width = gate_weight.shape
    far = pl.BlockSpec(memory_space=pl.ANY)
    return pl.pallas_call(
        load_kernel,
        out_shape=jax.ShapeDtypeStruct((2, deep, width // 4), gate_weight.dtype),
        in_specs=[pl.BlockSpec(memory_space=pltpu.SMEM), far, far],
        out_specs=pl.BlockSpec(memory_space=pltpu.VMEM),
        scratch_shapes=[pltpu.SemaphoreType.DMA((2, 4))],
        compiler_params=pltpu.CompilerParams(vmem_limit_bytes=VMEM),
        cost_estimate=pl.CostEstimate(flops=LOAD_COST, bytes_accessed=1, transcendentals=0),
    )(quarter, gate_weight, up_weight)


def sums_kernel(has_got, split, some, weights, *rest):
    def value(k):
        product = dot(some[...], weights[k])
        return product + wide(rest[0][k]) if has_got else product

    if split:
        for k, out in enumerate(rest[-2:]):
            out[...] = value(k).astype(out.dtype)
    else:

        @pl.loop(0, 2)
        def side(k):
            rest[-1][k] = value(k).astype(rest[-1].dtype)


def sums(some, weights, got=None, kind=jnp.bfloat16, split=False):
    near = pl.BlockSpec(memory_space=pltpu.VMEM)
    shape = some.shape[0], weights.shape[2]
    return pl.pallas_call(
        functools.partial(sums_kernel, got is not None, split),
        out_shape=(jax.ShapeDtypeStruct(shape, kind),) * 2 if split else jax.ShapeDtypeStruct((2,) + shape, kind),
        in_specs=[near] * (2 + (got is not None)),
        out_specs=(near, near) if split else near,
        compiler_params=pltpu.CompilerParams(vmem_limit_bytes=VMEM),
        cost_estimate=pl.CostEstimate(flops=COST, bytes_accessed=1, transcendentals=0),
    )(some, weights, *([] if got is None else [got]))


def load_rows_kernel(quarters, weight, out, done):
    rows = out.shape[1]
    pieces = done.shape[1]
    part = rows // pieces
    copies = [
        pltpu.make_async_copy(
            weight.at[pl.ds(pl.multiple_of(quarters[k] * rows + i * part, part), part)],
            out.at[k, pl.ds(i * part, part)],
            done.at[k, i],
        )
        for k in range(2)
        for i in range(pieces)
    ]
    for copy in copies:
        copy.start()
    for copy in copies:
        copy.wait()


def load_rows(weight, quarters):
    deep, width = weight.shape
    return pl.pallas_call(
        load_rows_kernel,
        out_shape=jax.ShapeDtypeStruct((2, deep // 4, width), weight.dtype),
        in_specs=[pl.BlockSpec(memory_space=pltpu.SMEM), pl.BlockSpec(memory_space=pl.ANY)],
        out_specs=pl.BlockSpec(memory_space=pltpu.VMEM),
        scratch_shapes=[pltpu.SemaphoreType.DMA((2, 4))],
        compiler_params=pltpu.CompilerParams(vmem_limit_bytes=VMEM),
        cost_estimate=pl.CostEstimate(flops=COST, bytes_accessed=1, transcendentals=0),
    )(quarters, weight)


def products_kernel(has_total, one, two, weights, *rest):
    tile = 4 * TILE

    @pl.loop(0, weights.shape[2] // tile)
    def strip(j):
        here = pl.ds(pl.multiple_of(j * tile, tile), tile)
        value = dot(one[...], weights[0, :, here]) + dot(two[...], weights[1, :, here])
        rest[-1][:, here] = value + rest[0][:, here] if has_total else value


def products(pieces, weights, total=None):
    near = pl.BlockSpec(memory_space=pltpu.VMEM)
    return pl.pallas_call(
        functools.partial(products_kernel, total is not None),
        out_shape=jax.ShapeDtypeStruct((pieces[0].shape[0], weights.shape[2]), jnp.float32),
        in_specs=[near] * (3 + (total is not None)),
        out_specs=near,
        compiler_params=pltpu.CompilerParams(vmem_limit_bytes=VMEM),
        cost_estimate=pl.CostEstimate(flops=COST, bytes_accessed=1, transcendentals=0),
    )(*pieces, weights, *([] if total is None else [total]))


def begin_kernel(starts, values, turned_scales, *outs):
    scales = turned_scales[...].T
    for j in range(scales.shape[1]):
        here = pl.ds(j * 128, 128)
        scaled_values = narrow(wide(values[:, here]) * scales[:, j : j + 1])
        for i, out in enumerate(outs):
            out[:, here] = scaled_values[starts[i] : starts[i + 1]]


def begin(values, scales, starts):
    near = pl.BlockSpec(memory_space=pltpu.VMEM)
    count = len(starts) - 1
    return pl.pallas_call(
        functools.partial(begin_kernel, starts),
        out_shape=[jax.ShapeDtypeStruct((starts[i + 1] - starts[i], values.shape[1]), values.dtype) for i in range(count)],
        in_specs=[near] * 2,
        out_specs=[near] * count,
        compiler_params=pltpu.CompilerParams(vmem_limit_bytes=VMEM),
        cost_estimate=pl.CostEstimate(flops=LOAD_COST, bytes_accessed=1, transcendentals=0),
    )(values, scales.T)


def hide_kernel(held, *rest):
    got, out = rest[:-1], rest[-1]
    got_gate, got_up = got if len(got) == 2 else (got[0].at[0], got[0].at[1])
    rows = 32

    @pl.loop(0, out.shape[0] // rows)
    def strip(i):
        here = pl.ds(pl.multiple_of(i * rows, rows), rows)
        gate = held[0, here] + wide(got_gate[here])
        up = held[1, here] + wide(got_up[here])
        out[here] = narrow(jax.nn.silu(gate) * up)


def hide(held, *got):
    near = pl.BlockSpec(memory_space=pltpu.VMEM)
    return pl.pallas_call(
        hide_kernel,
        out_shape=jax.ShapeDtypeStruct(held.shape[1:], got[0].dtype),
        in_specs=[near] * (1 + len(got)),
        out_specs=near,
        compiler_params=pltpu.CompilerParams(vmem_limit_bytes=VMEM),
        cost_estimate=pl.CostEstimate(flops=COST, bytes_accessed=1, transcendentals=0),
    )(held, *got)


def end_kernel(count, kept, got, *rest):
    before, (values, scales) = rest[: 2 * count], rest[2 * count :]
    first = sum(part.shape[0] for part in before[::2])
    rows = pl.ds(first, kept.shape[0])
    columns = []
    for j in range(kept.shape[1] // 128):
        here = pl.ds(j * 128, 128)
        total = kept[:, here] + wide(got[:, here])
        scale = jnp.max(jnp.abs(total), axis=1, keepdims=True) + 1e-06
        values[rows, here] = narrow(total / scale)
        columns.append(scale)
    ended = jnp.concatenate(columns, axis=1)
    if not count:
        scales[...] = ended
        return
    row = 0
    for part in before[::2]:
        values[pl.ds(row, part.shape[0])] = part[...]
        row += part.shape[0]
    scales[...] = jnp.concatenate([part[...] for part in before[1::2]] + [ended], axis=0).T


def end(kept, got, before=()):
    rows, width = kept.shape
    count = len(before)
    rows += sum(values.shape[0] for values, scales in before)
    near = pl.BlockSpec(memory_space=pltpu.VMEM)
    shape = (width // 128, rows) if count else (rows, width // 128)
    return pl.pallas_call(
        functools.partial(end_kernel, count),
        out_shape=(jax.ShapeDtypeStruct((rows, width), got.dtype), jax.ShapeDtypeStruct(shape, kept.dtype)),
        in_specs=[near] * (2 + 2 * count),
        out_specs=(near, near),
        compiler_params=pltpu.CompilerParams(vmem_limit_bytes=VMEM),
        cost_estimate=pl.CostEstimate(flops=COST, bytes_accessed=1, transcendentals=0),
    )(kept, got, *(array for pair in before for array in pair))


def small(kernel, outs, flags, *arrays):
    near = pl.BlockSpec(memory_space=pltpu.VMEM)
    return pl.pallas_call(
        kernel,
        out_shape=[jax.ShapeDtypeStruct(*out) for out in outs],
        in_specs=[pl.BlockSpec(memory_space=pltpu.SMEM)] + [near] * len(arrays),
        out_specs=[near] * len(outs),
        compiler_params=pltpu.CompilerParams(vmem_limit_bytes=VMEM),
        cost_estimate=pl.CostEstimate(flops=COST, bytes_accessed=1, transcendentals=0),
    )(flags, *arrays)


def strips(array):
    return pl.loop(0, array.shape[1] // TILE)


def out_kernel(flags, partial_sum, own, one, two):
    half = own.shape[0]
    low, top = pl.ds(0, half), pl.ds(half, half)

    @strips(own)
    def strip(j):
        here = pl.ds(pl.multiple_of(j * TILE, TILE), TILE)
        first, last = partial_sum[low, here], partial_sum[top, here]
        mine = jnp.where(flags[1] == 1, first, last)
        others = jnp.where(flags[1] == 1, last, first)
        own[:, here] = mine
        one[:, here] = narrow(jnp.where(flags[2] == 1, others, mine))
        two[:, here] = narrow(others)


def mix_kernel(flags, own, got_one, got_two, kept, sent):
    rows = kept.shape[0]

    @strips(own)
    def strip(j):
        here = pl.ds(pl.multiple_of(j * TILE, TILE), TILE)
        pair = wide(got_one[:, here]) + jnp.where(flags[2] == 1, own[:, here], wide(got_two[:, here]))
        kept[:, here] = jnp.where(flags[0] == 1, pair[:rows], pair[rows:])
        sent[:, here] = narrow(jnp.where(flags[0] == 1, pair[rows:], pair[:rows]))


def far_out_kernel(flags, kept, got, still, sent):
    @strips(kept)
    def strip(j):
        here = pl.ds(pl.multiple_of(j * TILE, TILE), TILE)
        mine, other = kept[:, here], wide(got[:, here])
        still[:, here] = jnp.where(flags[3] == 1, mine, other)
        sent[:, here] = narrow(jnp.where(flags[3] == 1, other, mine))


class Steps:

    def __init__(self, tokens_values, tokens_scales, gate_weight, up_weight, down_weight):
        tp, seq = lax.axis_index("tp"), lax.axis_index("seq")
        x, core, high = seq >> 1, seq & 1, tp >> 1
        facts = x == 0, core == 0, (tp ^ seq) & 1 == 0, high == x
        quarters = [(seq ^ bits).reshape(1) for bits in range(4)]
        pairs = [jnp.stack([seq ^ bits, seq ^ bits ^ 1]) for bits in (0, 2)]
        flags = jnp.stack(facts).astype(jnp.int32)
        facts, self.flags, self.quarters, self.pairs, gate_weight = lax.optimization_barrier(
            (facts, flags, quarters, pairs, gate_weight)
        )
        self.first_x, self.first_core, self.even, self.same_half = facts
        self.gate_weight = pltpu.with_memory_space_constraint(gate_weight, pltpu.HBM)
        self.up_weight = pltpu.with_memory_space_constraint(up_weight, pltpu.HBM)
        self.down_weight = pltpu.with_memory_space_constraint(down_weight, pltpu.HBM)
        unit = tokens_values.shape[0] // sum(ROWS)
        self.mine = begin(tokens_values, tokens_scales, [sum(ROWS[:i]) * unit for i in range(len(ROWS) + 1)])
        self.last = self.mine[0]
        self.held = {}

    def run(self, order):
        for step in order:
            with jax.named_scope(step):
                getattr(self, step[:-1])(int(step[-1]))
        values, scales = self.held["end", len(ROWS) - 1]
        return values, scales.T

    def now(self, array):
        return lax.optimization_barrier((array, self.last))[0]

    def far(self, i):
        part = self.now(self.mine[i])
        self.held["far", i] = part, over_tp(part, 2)

    def sel(self, i):
        part, other = self.held["far", i]
        other = self.now(other)
        sent = jnp.where(self.same_half, other, part)
        kept = jnp.where(self.same_half, part, other)
        self.held["sel", i] = kept, over_seq(sent, 2)
        self.last = sent

    def arr(self, i):
        kept, got = self.held["sel", i]
        pair = arrange(self.first_x, kept, self.now(got))
        self.held["arr", i] = pair, over_both(pair, FIRST_IN), over_both(pair, SECOND)
        self.last = pair

    def take(self, i):
        pair, first, second = self.held["arr", i]
        first = self.now(first)
        own = jnp.where(self.even, pair, first)
        others = jnp.where(self.even, first, second)
        self.held["take", i] = self.last = arrange(self.first_core, own, others)

    def load(self, bits):
        gate_weight = self.now(self.gate_weight)
        self.held["load", bits] = self.last = load(gate_weight, self.up_weight, self.quarters[bits])

    def part(self, i, bits, got=None, kind=jnp.bfloat16, split=False):
        some = self.now(self.held["take", i])
        result = sums(some, self.held["load", bits], got, kind, split)
        self.last = result[0] if split else result
        return result

    def a(self, i):
        self.held["a", i] = over_seq(self.part(i, 3), 1)

    def c(self, i):
        self.held["c", i] = over_seq(self.part(i, 1), 1)

    def b(self, i):
        sent = self.part(i, 2, self.held["a", i], split=i in SPLIT)
        self.held["b", i] = [over_seq(part, 2) for part in (sent if i in SPLIT else (sent,))]

    def d(self, i):
        self.held["d", i] = self.part(i, 0, self.held["c", i], jnp.float32)

    def hide(self, i):
        hidden = hide(self.held["d", i], *(self.now(got) for got in self.held["b", i]))
        far = over_seq(hidden, 2)
        self.held["hide", i] = hidden, far, over_seq(hidden, 1)
        self.last = hidden

    def down(self, bits):
        self.held["down", bits] = self.last = load_rows(self.now(self.down_weight), self.pairs[bits // 2])

    def own(self, i):
        hidden, far, near = self.held["hide", i]
        self.held["own", i] = self.last = products((self.now(hidden), near), self.held["down", 0])

    def forward(self, i):
        far = self.now(self.held["hide", i][1])
        self.held["pass", i] = far, over_seq(far, 1)

    def rest(self, i):
        far, last = self.held["pass", i]
        self.held["rest", i] = self.last = products((self.now(far), last), self.held["down", 2], self.held["own", i])

    def out(self, i):
        partial_sum = self.now(self.held["rest", i])
        half = partial_sum.shape[0] // 2, partial_sum.shape[1]
        outs = (half, jnp.float32), (half, jnp.bfloat16), (half, jnp.bfloat16)
        own, one, two = small(out_kernel, outs, self.flags, partial_sum)
        self.held["out", i] = own, over_both(one, FIRST_OUT), over_both(two, SECOND)
        self.last = one

    def mix(self, i):
        own, first, second = self.held["out", i]
        shape = own.shape[0] // 2, own.shape[1]
        outs = (shape, jnp.float32), (shape, jnp.bfloat16)
        kept, sent = small(mix_kernel, outs, self.flags, own, self.now(first), second)
        self.held["mix", i] = kept, over_seq(sent, 2)
        self.last = sent

    def far_out(self, i):
        kept, got = self.held["mix", i]
        outs = (kept.shape, jnp.float32), (kept.shape, jnp.bfloat16)
        kept, sent = small(far_out_kernel, outs, self.flags, kept, self.now(got))
        self.held["far_out", i] = kept, over_tp(sent, 2)
        self.last = sent

    def end(self, i):
        kept, got = self.held["far_out", i]
        before = [self.held["end", k] for k in range(i)] if i == len(ROWS) - 1 else ()
        self.held["end", i] = end(kept, self.now(got), before)
        self.last = self.held["end", i][0]


def four_shards(*arrays):
    return Steps(*arrays).run(ORDER)


def solution(mesh):
    placed = (
        P(("groups", "seq"), "tp"),
        P(("groups", "seq"), "tp"),
        P("seq", "tp"),
        P("seq", "tp"),
        P("tp", "seq"),
    )
    fours = mesh.shape["tp"] == 4 and mesh.shape["seq"] == 4
    return jax.shard_map(
        four_shards if fours else any_shards,
        mesh=mesh,
        in_specs=placed,
        out_specs=(P(("groups", "seq"), "tp"), P(("groups", "seq"), "tp")),
        check_vma=False,
    )
```

```python
import functools

import jax
import jax.numpy as jnp
from jax import lax
from jax.experimental import pallas as pl
from jax.experimental.pallas import tpu as pltpu
from jax.sharding import PartitionSpec as P

ROWS = (32, 48, 48)
ORDER = (
    "far0", "load3", "sel0", "far1", "load1", "arr0", "load2", "load0", "sel1", "far2", "take0", "a0", "c0",
    "b0", "arr1", "d0", "sel2", "take1", "a1", "c1", "hide0", "b1", "arr2", "d1", "take2", "a2", "c2",
    "down0", "own0", "forward0", "hide1", "b2", "d2", "down2", "rest0", "out0", "forward1", "own1", "rest1",
    "out1", "hide2", "mix0", "mix1", "forward2", "own2", "rest2", "out2", "far_out0", "mix2", "far_out1",
    "far_out2", "end0", "end1", "end2",
)
TILE = 256
SPLIT = (0, 1)
COST = 1 << 34
LOAD_COST = 1 << 30
VMEM = 6 << 20


def blocks(array):
    return array.reshape(array.shape[0], array.shape[1] // 128, 128)


def block_scale(array):
    return jnp.max(jnp.abs(blocks(array)), axis=2) + 1e-06


def expand(values, scales):
    return (blocks(values.astype(jnp.float32)) * scales[:, :, None]).reshape(values.shape)


def scaled(total):
    scales = block_scale(total)
    values = (blocks(total) / scales[:, :, None]).reshape(total.shape).astype(jnp.bfloat16)
    return values, scales


def wide(array):
    return array.astype(jnp.float32)


def narrow(array):
    return array.astype(jnp.bfloat16)


def dot(a, b):
    return jnp.dot(a, b, preferred_element_type=jnp.float32)


def any_shards(tokens_values, tokens_scales, gate_weight, up_weight, down_weight):
    mine = narrow(expand(tokens_values, tokens_scales))
    mine = lax.all_gather(mine, "tp", axis=1, tiled=True)
    inputs = lax.all_to_all(mine, "seq", split_axis=1, concat_axis=0, tiled=True)
    gate = narrow(dot(inputs, gate_weight))
    up = narrow(dot(inputs, up_weight))
    gate = wide(lax.psum_scatter(gate, "seq", scatter_dimension=0, tiled=True))
    up = wide(lax.psum_scatter(up, "seq", scatter_dimension=0, tiled=True))
    hidden = narrow(jax.nn.silu(gate) * up)
    hidden = lax.all_gather(hidden, "seq", axis=0, tiled=True)
    partial_sum = narrow(dot(hidden, down_weight))
    partial_sum = lax.all_to_all(partial_sum, "seq", split_axis=0, concat_axis=1, tiled=True)
    return scaled(wide(lax.psum_scatter(partial_sum, "tp", scatter_dimension=1, tiled=True)))


def over_seq(array, bit):
    return lax.ppermute(array, "seq", [(i, i ^ bit) for i in range(4)])


def over_tp(array, bit):
    return lax.ppermute(array, "tp", [(i, i ^ bit) for i in range(4)])


def device(tp, seq):
    return tp * 4 + seq


FIRST_IN, SECOND, FIRST_OUT = [], [], []
for tp in range(4):
    for seq in range(4):
        if (tp ^ seq) & 1:
            FIRST_IN.append((device(tp, seq), device(tp, seq ^ 1)))
            SECOND.append((device(tp, seq), device(tp ^ 1, seq ^ 1)))
            FIRST_OUT.append((device(tp, seq), device(tp ^ 1, seq)))
        else:
            FIRST_IN.append((device(tp, seq), device(tp ^ 1, seq)))
            FIRST_OUT.append((device(tp, seq), device(tp, seq ^ 1)))


def over_both(array, pairs):
    return lax.ppermute(array, ("tp", "seq"), pairs)


def arrange(low_first, one, other):
    return jnp.concatenate([jnp.where(low_first, one, other), jnp.where(low_first, other, one)], axis=0)


def load_kernel(quarter, gate_weight, up_weight, out, done):
    width = out.shape[2]
    here = pl.ds(pl.multiple_of(quarter[0] * width, width), width)
    pieces = done.shape[1]
    rows = out.shape[1] // pieces
    copies = [
        pltpu.make_async_copy(weight.at[pl.ds(i * rows, rows), here], out.at[k, pl.ds(i * rows, rows)], done.at[k, i])
        for k, weight in enumerate((gate_weight, up_weight))
        for i in range(pieces)
    ]
    for copy in copies:
        copy.start()
    for copy in copies:
        copy.wait()


def load(gate_weight, up_weight, quarter):
    deep, width = gate_weight.shape
    far = pl.BlockSpec(memory_space=pl.ANY)
    return pl.pallas_call(
        load_kernel,
        out_shape=jax.ShapeDtypeStruct((2, deep, width // 4), gate_weight.dtype),
        in_specs=[pl.BlockSpec(memory_space=pltpu.SMEM), far, far],
        out_specs=pl.BlockSpec(memory_space=pltpu.VMEM),
        scratch_shapes=[pltpu.SemaphoreType.DMA((2, 4))],
        compiler_params=pltpu.CompilerParams(vmem_limit_bytes=VMEM),
        cost_estimate=pl.CostEstimate(flops=LOAD_COST, bytes_accessed=1, transcendentals=0),
    )(quarter, gate_weight, up_weight)


def sums_kernel(has_got, split, some, weights, *rest):
    def value(k):
        product = dot(some[...], weights[k])
        return product + wide(rest[0][k]) if has_got else product

    if split:
        for k, out in enumerate(rest[-2:]):
            out[...] = value(k).astype(out.dtype)
    else:

        @pl.loop(0, 2)
        def side(k):
            rest[-1][k] = value(k).astype(rest[-1].dtype)


def sums(some, weights, got=None, kind=jnp.bfloat16, split=False):
    near = pl.BlockSpec(memory_space=pltpu.VMEM)
    shape = some.shape[0], weights.shape[2]
    return pl.pallas_call(
        functools.partial(sums_kernel, got is not None, split),
        out_shape=(jax.ShapeDtypeStruct(shape, kind),) * 2 if split else jax.ShapeDtypeStruct((2,) + shape, kind),
        in_specs=[near] * (2 + (got is not None)),
        out_specs=(near, near) if split else near,
        compiler_params=pltpu.CompilerParams(vmem_limit_bytes=VMEM),
        cost_estimate=pl.CostEstimate(flops=COST, bytes_accessed=1, transcendentals=0),
    )(some, weights, *([] if got is None else [got]))


def load_rows_kernel(quarters, weight, out, done):
    rows = out.shape[1]
    pieces = done.shape[1]
    part = rows // pieces
    copies = [
        pltpu.make_async_copy(
            weight.at[pl.ds(pl.multiple_of(quarters[k] * rows + i * part, part), part)],
            out.at[k, pl.ds(i * part, part)],
            done.at[k, i],
        )
        for k in range(2)
        for i in range(pieces)
    ]
    for copy in copies:
        copy.start()
    for copy in copies:
        copy.wait()


def load_rows(weight, quarters):
    deep, width = weight.shape
    return pl.pallas_call(
        load_rows_kernel,
        out_shape=jax.ShapeDtypeStruct((2, deep // 4, width), weight.dtype),
        in_specs=[pl.BlockSpec(memory_space=pltpu.SMEM), pl.BlockSpec(memory_space=pl.ANY)],
        out_specs=pl.BlockSpec(memory_space=pltpu.VMEM),
        scratch_shapes=[pltpu.SemaphoreType.DMA((2, 4))],
        compiler_params=pltpu.CompilerParams(vmem_limit_bytes=VMEM),
        cost_estimate=pl.CostEstimate(flops=COST, bytes_accessed=1, transcendentals=0),
    )(quarters, weight)


def products_kernel(has_total, one, two, weights, *rest):
    tile = 4 * TILE

    @pl.loop(0, weights.shape[2] // tile)
    def strip(j):
        here = pl.ds(pl.multiple_of(j * tile, tile), tile)
        value = dot(one[...], weights[0, :, here]) + dot(two[...], weights[1, :, here])
        rest[-1][:, here] = value + rest[0][:, here] if has_total else value


def products(pieces, weights, total=None):
    near = pl.BlockSpec(memory_space=pltpu.VMEM)
    return pl.pallas_call(
        functools.partial(products_kernel, total is not None),
        out_shape=jax.ShapeDtypeStruct((pieces[0].shape[0], weights.shape[2]), jnp.float32),
        in_specs=[near] * (3 + (total is not None)),
        out_specs=near,
        compiler_params=pltpu.CompilerParams(vmem_limit_bytes=VMEM),
        cost_estimate=pl.CostEstimate(flops=COST, bytes_accessed=1, transcendentals=0),
    )(*pieces, weights, *([] if total is None else [total]))


def begin_kernel(starts, values, turned_scales, *outs):
    scales = turned_scales[...].T
    for j in range(scales.shape[1]):
        here = pl.ds(j * 128, 128)
        scaled_values = narrow(wide(values[:, here]) * scales[:, j : j + 1])
        for i, out in enumerate(outs):
            out[:, here] = scaled_values[starts[i] : starts[i + 1]]


def begin(values, scales, starts):
    near = pl.BlockSpec(memory_space=pltpu.VMEM)
    count = len(starts) - 1
    return pl.pallas_call(
        functools.partial(begin_kernel, starts),
        out_shape=[jax.ShapeDtypeStruct((starts[i + 1] - starts[i], values.shape[1]), values.dtype) for i in range(count)],
        in_specs=[near] * 2,
        out_specs=[near] * count,
        compiler_params=pltpu.CompilerParams(vmem_limit_bytes=VMEM),
        cost_estimate=pl.CostEstimate(flops=LOAD_COST, bytes_accessed=1, transcendentals=0),
    )(values, scales.T)


def hide_kernel(held, *rest):
    got, out = rest[:-1], rest[-1]
    got_gate, got_up = got if len(got) == 2 else (got[0].at[0], got[0].at[1])
    rows = 32

    @pl.loop(0, out.shape[0] // rows)
    def strip(i):
        here = pl.ds(pl.multiple_of(i * rows, rows), rows)
        gate = held[0, here] + wide(got_gate[here])
        up = held[1, here] + wide(got_up[here])
        out[here] = narrow(jax.nn.silu(gate) * up)


def hide(held, *got):
    near = pl.BlockSpec(memory_space=pltpu.VMEM)
    return pl.pallas_call(
        hide_kernel,
        out_shape=jax.ShapeDtypeStruct(held.shape[1:], got[0].dtype),
        in_specs=[near] * (1 + len(got)),
        out_specs=near,
        compiler_params=pltpu.CompilerParams(vmem_limit_bytes=VMEM),
        cost_estimate=pl.CostEstimate(flops=COST, bytes_accessed=1, transcendentals=0),
    )(held, *got)


def end_kernel(count, kept, got, *rest):
    before, (values, scales) = rest[: 2 * count], rest[2 * count :]
    first = sum(part.shape[0] for part in before[::2])
    rows = pl.ds(first, kept.shape[0])
    columns = []
    for j in range(kept.shape[1] // 128):
        here = pl.ds(j * 128, 128)
        total = kept[:, here] + wide(got[:, here])
        scale = jnp.max(jnp.abs(total), axis=1, keepdims=True) + 1e-06
        values[rows, here] = narrow(total / scale)
        columns.append(scale)
    ended = jnp.concatenate(columns, axis=1)
    if not count:
        scales[...] = ended
        return
    row = 0
    for part in before[::2]:
        values[pl.ds(row, part.shape[0])] = part[...]
        row += part.shape[0]
    scales[...] = jnp.concatenate([part[...] for part in before[1::2]] + [ended], axis=0).T


def end(kept, got, before=()):
    rows, width = kept.shape
    count = len(before)
    rows += sum(values.shape[0] for values, scales in before)
    near = pl.BlockSpec(memory_space=pltpu.VMEM)
    shape = (width // 128, rows) if count else (rows, width // 128)
    return pl.pallas_call(
        functools.partial(end_kernel, count),
        out_shape=(jax.ShapeDtypeStruct((rows, width), got.dtype), jax.ShapeDtypeStruct(shape, kept.dtype)),
        in_specs=[near] * (2 + 2 * count),
        out_specs=(near, near),
        compiler_params=pltpu.CompilerParams(vmem_limit_bytes=VMEM),
        cost_estimate=pl.CostEstimate(flops=COST, bytes_accessed=1, transcendentals=0),
    )(kept, got, *(array for pair in before for array in pair))


def small(kernel, outs, flags, *arrays):
    near = pl.BlockSpec(memory_space=pltpu.VMEM)
    return pl.pallas_call(
        kernel,
        out_shape=[jax.ShapeDtypeStruct(*out) for out in outs],
        in_specs=[pl.BlockSpec(memory_space=pltpu.SMEM)] + [near] * len(arrays),
        out_specs=[near] * len(outs),
        compiler_params=pltpu.CompilerParams(vmem_limit_bytes=VMEM),
        cost_estimate=pl.CostEstimate(flops=COST, bytes_accessed=1, transcendentals=0),
    )(flags, *arrays)


def strips(array):
    return pl.loop(0, array.shape[1] // TILE)


def out_kernel(flags, partial_sum, own, one, two):
    half = own.shape[0]
    low, top = pl.ds(0, half), pl.ds(half, half)

    @strips(own)
    def strip(j):
        here = pl.ds(pl.multiple_of(j * TILE, TILE), TILE)
        first, last = partial_sum[low, here], partial_sum[top, here]
        mine = jnp.where(flags[1] == 1, first, last)
        others = jnp.where(flags[1] == 1, last, first)
        own[:, here] = mine
        one[:, here] = narrow(jnp.where(flags[2] == 1, others, mine))
        two[:, here] = narrow(others)


def mix_kernel(flags, own, got_one, got_two, kept, sent):
    rows = kept.shape[0]

    @strips(own)
    def strip(j):
        here = pl.ds(pl.multiple_of(j * TILE, TILE), TILE)
        pair = wide(got_one[:, here]) + jnp.where(flags[2] == 1, own[:, here], wide(got_two[:, here]))
        kept[:, here] = jnp.where(flags[0] == 1, pair[:rows], pair[rows:])
        sent[:, here] = narrow(jnp.where(flags[0] == 1, pair[rows:], pair[:rows]))


def far_out_kernel(flags, kept, got, still, sent):
    @strips(kept)
    def strip(j):
        here = pl.ds(pl.multiple_of(j * TILE, TILE), TILE)
        mine, other = kept[:, here], wide(got[:, here])
        still[:, here] = jnp.where(flags[3] == 1, mine, other)
        sent[:, here] = narrow(jnp.where(flags[3] == 1, other, mine))


class Steps:

    def __init__(self, tokens_values, tokens_scales, gate_weight, up_weight, down_weight):
        tp, seq = lax.axis_index("tp"), lax.axis_index("seq")
        x, core, high = seq >> 1, seq & 1, tp >> 1
        facts = x == 0, core == 0, (tp ^ seq) & 1 == 0, high == x
        quarters = [(seq ^ bits).reshape(1) for bits in range(4)]
        pairs = [jnp.stack([seq ^ bits, seq ^ bits ^ 1]) for bits in (0, 2)]
        flags = jnp.stack(facts).astype(jnp.int32)
        facts, self.flags, self.quarters, self.pairs, gate_weight = lax.optimization_barrier(
            (facts, flags, quarters, pairs, gate_weight)
        )
        self.first_x, self.first_core, self.even, self.same_half = facts
        self.gate_weight = pltpu.with_memory_space_constraint(gate_weight, pltpu.HBM)
        self.up_weight = pltpu.with_memory_space_constraint(up_weight, pltpu.HBM)
        self.down_weight = pltpu.with_memory_space_constraint(down_weight, pltpu.HBM)
        unit = tokens_values.shape[0] // sum(ROWS)
        self.mine = begin(tokens_values, tokens_scales, [sum(ROWS[:i]) * unit for i in range(len(ROWS) + 1)])
        self.last = self.mine[0]
        self.held = {}

    def run(self, order):
        for step in order:
            with jax.named_scope(step):
                getattr(self, step[:-1])(int(step[-1]))
        values, scales = self.held["end", len(ROWS) - 1]
        return values, scales.T

    def now(self, array):
        return lax.optimization_barrier((array, self.last))[0]

    def far(self, i):
        part = self.now(self.mine[i])
        self.held["far", i] = part, over_tp(part, 2)

    def sel(self, i):
        part, other = self.held["far", i]
        other = self.now(other)
        sent = jnp.where(self.same_half, other, part)
        kept = jnp.where(self.same_half, part, other)
        self.held["sel", i] = kept, over_seq(sent, 2)
        self.last = sent

    def arr(self, i):
        kept, got = self.held["sel", i]
        pair = arrange(self.first_x, kept, self.now(got))
        self.held["arr", i] = pair, over_both(pair, FIRST_IN), over_both(pair, SECOND)
        self.last = pair

    def take(self, i):
        pair, first, second = self.held["arr", i]
        first = self.now(first)
        own = jnp.where(self.even, pair, first)
        others = jnp.where(self.even, first, second)
        self.held["take", i] = self.last = arrange(self.first_core, own, others)

    def load(self, bits):
        gate_weight = self.now(self.gate_weight)
        self.held["load", bits] = self.last = load(gate_weight, self.up_weight, self.quarters[bits])

    def part(self, i, bits, got=None, kind=jnp.bfloat16, split=False):
        some = self.now(self.held["take", i])
        result = sums(some, self.held["load", bits], got, kind, split)
        self.last = result[0] if split else result
        return result

    def a(self, i):
        self.held["a", i] = over_seq(self.part(i, 3), 1)

    def c(self, i):
        self.held["c", i] = over_seq(self.part(i, 1), 1)

    def b(self, i):
        sent = self.part(i, 2, self.held["a", i], split=i in SPLIT)
        self.held["b", i] = [over_seq(part, 2) for part in (sent if i in SPLIT else (sent,))]

    def d(self, i):
        self.held["d", i] = self.part(i, 0, self.held["c", i], jnp.float32)

    def hide(self, i):
        hidden = hide(self.held["d", i], *(self.now(got) for got in self.held["b", i]))
        far = over_seq(hidden, 2)
        self.held["hide", i] = hidden, far, over_seq(hidden, 1)
        self.last = hidden

    def down(self, bits):
        self.held["down", bits] = self.last = load_rows(self.now(self.down_weight), self.pairs[bits // 2])

    def own(self, i):
        hidden, far, near = self.held["hide", i]
        self.held["own", i] = self.last = products((self.now(hidden), near), self.held["down", 0])

    def forward(self, i):
        far = self.now(self.held["hide", i][1])
        self.held["pass", i] = far, over_seq(far, 1)

    def rest(self, i):
        far, last = self.held["pass", i]
        self.held["rest", i] = self.last = products((self.now(far), last), self.held["down", 2], self.held["own", i])

    def out(self, i):
        partial_sum = self.now(self.held["rest", i])
        half = partial_sum.shape[0] // 2, partial_sum.shape[1]
        outs = (half, jnp.float32), (half, jnp.bfloat16), (half, jnp.bfloat16)
        own, one, two = small(out_kernel, outs, self.flags, partial_sum)
        self.held["out", i] = own, over_both(one, FIRST_OUT), over_both(two, SECOND)
        self.last = one

    def mix(self, i):
        own, first, second = self.held["out", i]
        shape = own.shape[0] // 2, own.shape[1]
        outs = (shape, jnp.float32), (shape, jnp.bfloat16)
        kept, sent = small(mix_kernel, outs, self.flags, own, self.now(first), second)
        self.held["mix", i] = kept, over_seq(sent, 2)
        self.last = sent

    def far_out(self, i):
        kept, got = self.held["mix", i]
        outs = (kept.shape, jnp.float32), (kept.shape, jnp.bfloat16)
        kept, sent = small(far_out_kernel, outs, self.flags, kept, self.now(got))
        self.held["far_out", i] = kept, over_tp(sent, 2)
        self.last = sent

    def end(self, i):
        kept, got = self.held["far_out", i]
        before = [self.held["end", k] for k in range(i)] if i == len(ROWS) - 1 else ()
        self.held["end", i] = end(kept, self.now(got), before)
        self.last = self.held["end", i][0]


def four_shards(*arrays):
    return Steps(*arrays).run(ORDER)


def solution(mesh):
    placed = (
        P(("groups", "seq"), "tp"),
        P(("groups", "seq"), "tp"),
        P("seq", "tp"),
        P("seq", "tp"),
        P("tp", "seq"),
    )
    fours = mesh.shape["tp"] == 4 and mesh.shape["seq"] == 4
    return jax.shard_map(
        four_shards if fours else any_shards,
        mesh=mesh,
        in_specs=placed,
        out_specs=(P(("groups", "seq"), "tp"), P(("groups", "seq"), "tp")),
        check_vma=False,
    )
```

```python
import functools

import jax
import jax.numpy as jnp
from jax import lax
from jax.experimental import pallas as pl
from jax.experimental.pallas import tpu as pltpu
from jax.sharding import PartitionSpec as P

ROWS = (32, 48, 48)
ORDER = (
    "far0", "load3", "sel0", "far1", "load1", "arr0", "load2", "load0", "sel1", "far2", "take0", "a0", "c0",
    "b0", "arr1", "d0", "sel2", "take1", "a1", "c1", "hide0", "b1", "arr2", "d1", "take2", "a2", "c2",
    "down0", "own0", "forward0", "hide1", "b2", "d2", "down2", "rest0", "out0", "forward1", "own1", "rest1",
    "out1", "hide2", "mix0", "mix1", "forward2", "own2", "rest2", "out2", "far_out1", "far_out0", "mix2",
    "end1", "far_out2", "end0", "end2",
)
TILE = 256
SPLIT = (0, 1)
COST = 1 << 34
LOAD_COST = 1 << 30
VMEM = 6 << 20


def blocks(array):
    return array.reshape(array.shape[0], array.shape[1] // 128, 128)


def block_scale(array):
    return jnp.max(jnp.abs(blocks(array)), axis=2) + 1e-06


def expand(values, scales):
    return (blocks(values.astype(jnp.float32)) * scales[:, :, None]).reshape(values.shape)


def scaled(total):
    scales = block_scale(total)
    values = (blocks(total) / scales[:, :, None]).reshape(total.shape).astype(jnp.bfloat16)
    return values, scales


def wide(array):
    return array.astype(jnp.float32)


def narrow(array):
    return array.astype(jnp.bfloat16)


def dot(a, b):
    return jnp.dot(a, b, preferred_element_type=jnp.float32)


def any_shards(tokens_values, tokens_scales, gate_weight, up_weight, down_weight):
    mine = narrow(expand(tokens_values, tokens_scales))
    mine = lax.all_gather(mine, "tp", axis=1, tiled=True)
    inputs = lax.all_to_all(mine, "seq", split_axis=1, concat_axis=0, tiled=True)
    gate = narrow(dot(inputs, gate_weight))
    up = narrow(dot(inputs, up_weight))
    gate = wide(lax.psum_scatter(gate, "seq", scatter_dimension=0, tiled=True))
    up = wide(lax.psum_scatter(up, "seq", scatter_dimension=0, tiled=True))
    hidden = narrow(jax.nn.silu(gate) * up)
    hidden = lax.all_gather(hidden, "seq", axis=0, tiled=True)
    partial_sum = narrow(dot(hidden, down_weight))
    partial_sum = lax.all_to_all(partial_sum, "seq", split_axis=0, concat_axis=1, tiled=True)
    return scaled(wide(lax.psum_scatter(partial_sum, "tp", scatter_dimension=1, tiled=True)))


def over_seq(array, bit):
    return lax.ppermute(array, "seq", [(i, i ^ bit) for i in range(4)])


def over_tp(array, bit):
    return lax.ppermute(array, "tp", [(i, i ^ bit) for i in range(4)])


def device(tp, seq):
    return tp * 4 + seq


FIRST_IN, SECOND, FIRST_OUT = [], [], []
for tp in range(4):
    for seq in range(4):
        if (tp ^ seq) & 1:
            FIRST_IN.append((device(tp, seq), device(tp, seq ^ 1)))
            SECOND.append((device(tp, seq), device(tp ^ 1, seq ^ 1)))
            FIRST_OUT.append((device(tp, seq), device(tp ^ 1, seq)))
        else:
            FIRST_IN.append((device(tp, seq), device(tp ^ 1, seq)))
            FIRST_OUT.append((device(tp, seq), device(tp, seq ^ 1)))


def over_both(array, pairs):
    return lax.ppermute(array, ("tp", "seq"), pairs)


def arrange(low_first, one, other):
    return jnp.concatenate([jnp.where(low_first, one, other), jnp.where(low_first, other, one)], axis=0)


def load_kernel(quarter, gate_weight, up_weight, out, done):
    width = out.shape[2]
    here = pl.ds(pl.multiple_of(quarter[0] * width, width), width)
    pieces = done.shape[1]
    rows = out.shape[1] // pieces
    copies = [
        pltpu.make_async_copy(weight.at[pl.ds(i * rows, rows), here], out.at[k, pl.ds(i * rows, rows)], done.at[k, i])
        for k, weight in enumerate((gate_weight, up_weight))
        for i in range(pieces)
    ]
    for copy in copies:
        copy.start()
    for copy in copies:
        copy.wait()


def load(gate_weight, up_weight, quarter):
    deep, width = gate_weight.shape
    far = pl.BlockSpec(memory_space=pl.ANY)
    return pl.pallas_call(
        load_kernel,
        out_shape=jax.ShapeDtypeStruct((2, deep, width // 4), gate_weight.dtype),
        in_specs=[pl.BlockSpec(memory_space=pltpu.SMEM), far, far],
        out_specs=pl.BlockSpec(memory_space=pltpu.VMEM),
        scratch_shapes=[pltpu.SemaphoreType.DMA((2, 4))],
        compiler_params=pltpu.CompilerParams(vmem_limit_bytes=VMEM),
        cost_estimate=pl.CostEstimate(flops=LOAD_COST, bytes_accessed=1, transcendentals=0),
    )(quarter, gate_weight, up_weight)


def sums_kernel(has_got, split, some, weights, *rest):
    def value(k):
        product = dot(some[...], weights[k])
        return product + wide(rest[0][k]) if has_got else product

    if split:
        for k, out in enumerate(rest[-2:]):
            out[...] = value(k).astype(out.dtype)
    else:

        @pl.loop(0, 2)
        def side(k):
            rest[-1][k] = value(k).astype(rest[-1].dtype)


def sums(some, weights, got=None, kind=jnp.bfloat16, split=False):
    near = pl.BlockSpec(memory_space=pltpu.VMEM)
    shape = some.shape[0], weights.shape[2]
    return pl.pallas_call(
        functools.partial(sums_kernel, got is not None, split),
        out_shape=(jax.ShapeDtypeStruct(shape, kind),) * 2 if split else jax.ShapeDtypeStruct((2,) + shape, kind),
        in_specs=[near] * (2 + (got is not None)),
        out_specs=(near, near) if split else near,
        compiler_params=pltpu.CompilerParams(vmem_limit_bytes=VMEM),
        cost_estimate=pl.CostEstimate(flops=COST, bytes_accessed=1, transcendentals=0),
    )(some, weights, *([] if got is None else [got]))


def load_rows_kernel(quarters, weight, out, done):
    rows = out.shape[1]
    pieces = done.shape[1]
    part = rows // pieces
    copies = [
        pltpu.make_async_copy(
            weight.at[pl.ds(pl.multiple_of(quarters[k] * rows + i * part, part), part)],
            out.at[k, pl.ds(i * part, part)],
            done.at[k, i],
        )
        for k in range(2)
        for i in range(pieces)
    ]
    for copy in copies:
        copy.start()
    for copy in copies:
        copy.wait()


def load_rows(weight, quarters):
    deep, width = weight.shape
    return pl.pallas_call(
        load_rows_kernel,
        out_shape=jax.ShapeDtypeStruct((2, deep // 4, width), weight.dtype),
        in_specs=[pl.BlockSpec(memory_space=pltpu.SMEM), pl.BlockSpec(memory_space=pl.ANY)],
        out_specs=pl.BlockSpec(memory_space=pltpu.VMEM),
        scratch_shapes=[pltpu.SemaphoreType.DMA((2, 4))],
        compiler_params=pltpu.CompilerParams(vmem_limit_bytes=VMEM),
        cost_estimate=pl.CostEstimate(flops=COST, bytes_accessed=1, transcendentals=0),
    )(quarters, weight)


def products_kernel(has_total, one, two, weights, *rest):
    tile = 4 * TILE

    @pl.loop(0, weights.shape[2] // tile)
    def strip(j):
        here = pl.ds(pl.multiple_of(j * tile, tile), tile)
        value = dot(one[...], weights[0, :, here]) + dot(two[...], weights[1, :, here])
        rest[-1][:, here] = value + rest[0][:, here] if has_total else value


def products(pieces, weights, total=None):
    near = pl.BlockSpec(memory_space=pltpu.VMEM)
    return pl.pallas_call(
        functools.partial(products_kernel, total is not None),
        out_shape=jax.ShapeDtypeStruct((pieces[0].shape[0], weights.shape[2]), jnp.float32),
        in_specs=[near] * (3 + (total is not None)),
        out_specs=near,
        compiler_params=pltpu.CompilerParams(vmem_limit_bytes=VMEM),
        cost_estimate=pl.CostEstimate(flops=COST, bytes_accessed=1, transcendentals=0),
    )(*pieces, weights, *([] if total is None else [total]))


def begin_kernel(starts, values, turned_scales, *outs):
    scales = turned_scales[...].T
    for j in range(scales.shape[1]):
        here = pl.ds(j * 128, 128)
        scaled_values = narrow(wide(values[:, here]) * scales[:, j : j + 1])
        for i, out in enumerate(outs):
            out[:, here] = scaled_values[starts[i] : starts[i + 1]]


def begin(values, scales, starts):
    near = pl.BlockSpec(memory_space=pltpu.VMEM)
    count = len(starts) - 1
    return pl.pallas_call(
        functools.partial(begin_kernel, starts),
        out_shape=[jax.ShapeDtypeStruct((starts[i + 1] - starts[i], values.shape[1]), values.dtype) for i in range(count)],
        in_specs=[near] * 2,
        out_specs=[near] * count,
        compiler_params=pltpu.CompilerParams(vmem_limit_bytes=VMEM),
        cost_estimate=pl.CostEstimate(flops=LOAD_COST, bytes_accessed=1, transcendentals=0),
    )(values, scales.T)


def hide_kernel(held, *rest):
    got, out = rest[:-1], rest[-1]
    got_gate, got_up = got if len(got) == 2 else (got[0].at[0], got[0].at[1])
    rows = 32

    @pl.loop(0, out.shape[0] // rows)
    def strip(i):
        here = pl.ds(pl.multiple_of(i * rows, rows), rows)
        gate = held[0, here] + wide(got_gate[here])
        up = held[1, here] + wide(got_up[here])
        out[here] = narrow(jax.nn.silu(gate) * up)


def hide(held, *got):
    near = pl.BlockSpec(memory_space=pltpu.VMEM)
    return pl.pallas_call(
        hide_kernel,
        out_shape=jax.ShapeDtypeStruct(held.shape[1:], got[0].dtype),
        in_specs=[near] * (1 + len(got)),
        out_specs=near,
        compiler_params=pltpu.CompilerParams(vmem_limit_bytes=VMEM),
        cost_estimate=pl.CostEstimate(flops=COST, bytes_accessed=1, transcendentals=0),
    )(held, *got)


def end_kernel(count, kept, got, *rest):
    before, (values, scales) = rest[: 2 * count], rest[2 * count :]
    first = sum(part.shape[0] for part in before[::2])
    rows = pl.ds(first, kept.shape[0])
    columns = []
    for j in range(kept.shape[1] // 128):
        here = pl.ds(j * 128, 128)
        total = kept[:, here] + wide(got[:, here])
        scale = jnp.max(jnp.abs(total), axis=1, keepdims=True) + 1e-06
        values[rows, here] = narrow(total / scale)
        columns.append(scale)
    ended = jnp.concatenate(columns, axis=1)
    if not count:
        scales[...] = ended
        return
    row = 0
    for part in before[::2]:
        values[pl.ds(row, part.shape[0])] = part[...]
        row += part.shape[0]
    scales[...] = jnp.concatenate([part[...] for part in before[1::2]] + [ended], axis=0).T


def end(kept, got, before=()):
    rows, width = kept.shape
    count = len(before)
    rows += sum(values.shape[0] for values, scales in before)
    near = pl.BlockSpec(memory_space=pltpu.VMEM)
    shape = (width // 128, rows) if count else (rows, width // 128)
    return pl.pallas_call(
        functools.partial(end_kernel, count),
        out_shape=(jax.ShapeDtypeStruct((rows, width), got.dtype), jax.ShapeDtypeStruct(shape, kept.dtype)),
        in_specs=[near] * (2 + 2 * count),
        out_specs=(near, near),
        compiler_params=pltpu.CompilerParams(vmem_limit_bytes=VMEM),
        cost_estimate=pl.CostEstimate(flops=COST, bytes_accessed=1, transcendentals=0),
    )(kept, got, *(array for pair in before for array in pair))


def small(kernel, outs, flags, *arrays):
    near = pl.BlockSpec(memory_space=pltpu.VMEM)
    return pl.pallas_call(
        kernel,
        out_shape=[jax.ShapeDtypeStruct(*out) for out in outs],
        in_specs=[pl.BlockSpec(memory_space=pltpu.SMEM)] + [near] * len(arrays),
        out_specs=[near] * len(outs),
        compiler_params=pltpu.CompilerParams(vmem_limit_bytes=VMEM),
        cost_estimate=pl.CostEstimate(flops=COST, bytes_accessed=1, transcendentals=0),
    )(flags, *arrays)


def strips(array):
    return pl.loop(0, array.shape[1] // TILE)


def out_kernel(flags, partial_sum, own, one, two):
    half = own.shape[0]
    low, top = pl.ds(0, half), pl.ds(half, half)

    @strips(own)
    def strip(j):
        here = pl.ds(pl.multiple_of(j * TILE, TILE), TILE)
        first, last = partial_sum[low, here], partial_sum[top, here]
        mine = jnp.where(flags[1] == 1, first, last)
        others = jnp.where(flags[1] == 1, last, first)
        own[:, here] = mine
        one[:, here] = narrow(jnp.where(flags[2] == 1, others, mine))
        two[:, here] = narrow(others)


def mix_kernel(flags, own, got_one, got_two, kept, sent):
    rows = kept.shape[0]

    @strips(own)
    def strip(j):
        here = pl.ds(pl.multiple_of(j * TILE, TILE), TILE)
        pair = wide(got_one[:, here]) + jnp.where(flags[2] == 1, own[:, here], wide(got_two[:, here]))
        kept[:, here] = jnp.where(flags[0] == 1, pair[:rows], pair[rows:])
        sent[:, here] = narrow(jnp.where(flags[0] == 1, pair[rows:], pair[:rows]))


def far_out_kernel(flags, kept, got, still, sent):
    @strips(kept)
    def strip(j):
        here = pl.ds(pl.multiple_of(j * TILE, TILE), TILE)
        mine, other = kept[:, here], wide(got[:, here])
        still[:, here] = jnp.where(flags[3] == 1, mine, other)
        sent[:, here] = narrow(jnp.where(flags[3] == 1, other, mine))


class Steps:

    def __init__(self, tokens_values, tokens_scales, gate_weight, up_weight, down_weight):
        tp, seq = lax.axis_index("tp"), lax.axis_index("seq")
        x, core, high = seq >> 1, seq & 1, tp >> 1
        facts = x == 0, core == 0, (tp ^ seq) & 1 == 0, high == x
        quarters = [(seq ^ bits).reshape(1) for bits in range(4)]
        pairs = [jnp.stack([seq ^ bits, seq ^ bits ^ 1]) for bits in (0, 2)]
        flags = jnp.stack(facts).astype(jnp.int32)
        facts, self.flags, self.quarters, self.pairs, gate_weight = lax.optimization_barrier(
            (facts, flags, quarters, pairs, gate_weight)
        )
        self.first_x, self.first_core, self.even, self.same_half = facts
        self.gate_weight = pltpu.with_memory_space_constraint(gate_weight, pltpu.HBM)
        self.up_weight = pltpu.with_memory_space_constraint(up_weight, pltpu.HBM)
        self.down_weight = pltpu.with_memory_space_constraint(down_weight, pltpu.HBM)
        unit = tokens_values.shape[0] // sum(ROWS)
        self.mine = begin(tokens_values, tokens_scales, [sum(ROWS[:i]) * unit for i in range(len(ROWS) + 1)])
        self.last = self.mine[0]
        self.held = {}

    def run(self, order):
        for step in order:
            with jax.named_scope(step):
                getattr(self, step[:-1])(int(step[-1]))
        values, scales = self.held["end", len(ROWS) - 1]
        return values, scales.T

    def now(self, array):
        return lax.optimization_barrier((array, self.last))[0]

    def far(self, i):
        part = self.now(self.mine[i])
        self.held["far", i] = part, over_tp(part, 2)

    def sel(self, i):
        part, other = self.held["far", i]
        other = self.now(other)
        sent = jnp.where(self.same_half, other, part)
        kept = jnp.where(self.same_half, part, other)
        self.held["sel", i] = kept, over_seq(sent, 2)
        self.last = sent

    def arr(self, i):
        kept, got = self.held["sel", i]
        pair = arrange(self.first_x, kept, self.now(got))
        self.held["arr", i] = pair, over_both(pair, FIRST_IN), over_both(pair, SECOND)
        self.last = pair

    def take(self, i):
        pair, first, second = self.held["arr", i]
        first = self.now(first)
        own = jnp.where(self.even, pair, first)
        others = jnp.where(self.even, first, second)
        self.held["take", i] = self.last = arrange(self.first_core, own, others)

    def load(self, bits):
        gate_weight = self.now(self.gate_weight)
        self.held["load", bits] = self.last = load(gate_weight, self.up_weight, self.quarters[bits])

    def part(self, i, bits, got=None, kind=jnp.bfloat16, split=False):
        some = self.now(self.held["take", i])
        result = sums(some, self.held["load", bits], got, kind, split)
        self.last = result[0] if split else result
        return result

    def a(self, i):
        self.held["a", i] = over_seq(self.part(i, 3), 1)

    def c(self, i):
        self.held["c", i] = over_seq(self.part(i, 1), 1)

    def b(self, i):
        sent = self.part(i, 2, self.held["a", i], split=i in SPLIT)
        self.held["b", i] = [over_seq(part, 2) for part in (sent if i in SPLIT else (sent,))]

    def d(self, i):
        self.held["d", i] = self.part(i, 0, self.held["c", i], jnp.float32)

    def hide(self, i):
        hidden = hide(self.held["d", i], *(self.now(got) for got in self.held["b", i]))
        far = over_seq(hidden, 2)
        self.held["hide", i] = hidden, far, over_seq(hidden, 1)
        self.last = hidden

    def down(self, bits):
        self.held["down", bits] = self.last = load_rows(self.now(self.down_weight), self.pairs[bits // 2])

    def own(self, i):
        hidden, far, near = self.held["hide", i]
        self.held["own", i] = self.last = products((self.now(hidden), near), self.held["down", 0])

    def forward(self, i):
        far = self.now(self.held["hide", i][1])
        self.held["pass", i] = far, over_seq(far, 1)

    def rest(self, i):
        far, last = self.held["pass", i]
        self.held["rest", i] = self.last = products((self.now(far), last), self.held["down", 2], self.held["own", i])

    def out(self, i):
        partial_sum = self.now(self.held["rest", i])
        half = partial_sum.shape[0] // 2, partial_sum.shape[1]
        outs = (half, jnp.float32), (half, jnp.bfloat16), (half, jnp.bfloat16)
        own, one, two = small(out_kernel, outs, self.flags, partial_sum)
        self.held["out", i] = own, over_both(one, FIRST_OUT), over_both(two, SECOND)
        self.last = one

    def mix(self, i):
        own, first, second = self.held["out", i]
        shape = own.shape[0] // 2, own.shape[1]
        outs = (shape, jnp.float32), (shape, jnp.bfloat16)
        kept, sent = small(mix_kernel, outs, self.flags, own, self.now(first), second)
        self.held["mix", i] = kept, over_seq(sent, 2)
        self.last = sent

    def far_out(self, i):
        kept, got = self.held["mix", i]
        outs = (kept.shape, jnp.float32), (kept.shape, jnp.bfloat16)
        kept, sent = small(far_out_kernel, outs, self.flags, kept, self.now(got))
        self.held["far_out", i] = kept, over_tp(sent, 2)
        self.last = sent

    def end(self, i):
        kept, got = self.held["far_out", i]
        before = [self.held["end", k] for k in range(i)] if i == len(ROWS) - 1 else ()
        self.held["end", i] = end(kept, self.now(got), before)
        self.last = self.held["end", i][0]


def four_shards(*arrays):
    return Steps(*arrays).run(ORDER)


def solution(mesh):
    placed = (
        P(("groups", "seq"), "tp"),
        P(("groups", "seq"), "tp"),
        P("seq", "tp"),
        P("seq", "tp"),
        P("tp", "seq"),
    )
    fours = mesh.shape["tp"] == 4 and mesh.shape["seq"] == 4
    return jax.shard_map(
        four_shards if fours else any_shards,
        mesh=mesh,
        in_specs=placed,
        out_specs=(P(("groups", "seq"), "tp"), P(("groups", "seq"), "tp")),
        check_vma=False,
    )
```
